32 devices in a mesh: groups: 2 (over y), epoch: 4 (over z), tile: 4 (over x, core).
Axes of the slice: x: 2, y: 2, z: 4, core: 2. Of those that a mesh axis runs over, the one named last changes fastest.
Arguments:
- frames: bfloat16 [8, 128, 16, 384], P('epoch', ('groups', 'tile')), parts along dimension 1, may hold values from -6 to 6
- valid: int32 [8, 128, 16], P('epoch', ('groups', 'tile')), parts along dimension 1, may hold values 0 or 1
- days: int32 [16], P('groups'), parts along dimension 0, may hold values from 0 to 239, as said below
- dw_kernel: float32 [7, 7, 384], replicated, may hold values from -0.875 to 0.875
- dw_bias: float32 [384], replicated, may hold values from -3 to 3
- norm_gain: float32 [384], replicated, may hold values from 0.5 to 1.5
- norm_shift: float32 [384], replicated, may hold values from -1.75 to 1.75
- w_expand: bfloat16 [384, 1536], replicated, may hold values from -0.3125 to 0.3125
- b_expand: float32 [1536], replicated, may hold values from -3 to 3
- w_reduce: bfloat16 [1536, 384], replicated, may hold values from -0.15625 to 0.15625
- layer_scale: float32 [384], replicated, may hold values from 0.3 to 1
- w_gates: bfloat16 [3, 3, 384, 1536], replicated, may hold values from -0.109375 to 0.109375
- b_gates: float32 [1536], replicated, may hold values from -3 to 3
- forget_rate: float32 [384], replicated, may hold values from 0.0625 to 1
- attn_gain: float32 [384], replicated, may hold values from 0.5 to 1.5
- w_query: bfloat16 [384, 384], replicated, as said below
- w_key: bfloat16 [384, 384], replicated, as said below
- w_value: bfloat16 [384, 384], replicated, may hold values from -0.3125 to 0.3125
- w_out: bfloat16 [384, 384], replicated, may hold values from -0.3125 to 0.3125
- head_slope: float32 [8], replicated, may hold values from 0.02 to 1
Outputs:
- memory: bfloat16 [8, 128, 16, 384], P('epoch', ('groups', 'tile')), parts along dimension 1
- change: bfloat16 [8, 8, 1, 384], P('epoch', ('groups', 'tile')), parts along dimension 1
The draws below stay inside these ranges and needn't reach their ends.
There are 2 independent parts, one for each index of `groups`. The reference program is written for one: setup_inputs(seed, part) draws one part's arguments, and reference() takes and returns one part's arrays. A program takes and returns all parts, laid end to end along the dimension named above; an argument that names none is the same for every part. Nothing has to cross between parts.
Inputs may be any that keep to these rules, and one draw needn't show every extreme that they name: days[t] lies between 30 t and 30 t + 29, so days rise strictly. `w_query`: a projection of the normalized patch features. `w_key`: a projection of the normalized patch features.
All inputs are finite; a program needn't handle non-finite values. No bound on the sum of `valid` on one device may be relied on, other than what follows from the above.
Results may differ from the reference program's by a relative error of at most 0.008.
Values may be sent and summed in bfloat16 or wider, within the bound.
No kernel may reach another device: no remote copies, remote signals or barrier semaphores. Data moves between devices by JAX's collectives and lax.ppermute only.
A program may use at most 192 MiB of HBM per device.

```python
import math
import jax
import jax.numpy as jnp
from jax import lax

C = 384
FFN = 1536
HEADS = 8
PATCH = 16
W = 16
EPOCHS = 8
H = 64


def query_key_pair(key):
    own_query = jax.random.normal(jax.random.fold_in(key, 7002), (C, C), jnp.float32)
    own_key = jax.random.normal(jax.random.fold_in(key, 7003), (C, C), jnp.float32)
    factor = 1.0 / math.sqrt(C)
    return (own_query * factor, own_key * factor)


def draw_w_query(key, part):
    return query_key_pair(key)[0].astype(jnp.bfloat16)


def draw_w_key(key, part):
    return query_key_pair(key)[1].astype(jnp.bfloat16)


def draw_days(key, part):
    base_day = jnp.arange(EPOCHS, dtype=jnp.int32) * 30
    jitter = jax.random.randint(jax.random.fold_in(key, 7100), (EPOCHS,), 0, 30, dtype=jnp.int32)
    return base_day + jitter


def draw_frames(key, part):
    key = jax.random.fold_in(key, 7200)
    coarse_shape = (EPOCHS, H // PATCH, W // PATCH, C)
    fine_shape = (EPOCHS, H, W, C)
    coarse = jax.random.normal(jax.random.fold_in(key, 1), coarse_shape, jnp.float32)
    fine = jax.random.normal(jax.random.fold_in(key, 2), fine_shape, jnp.float32)
    coarse_full = jnp.repeat(jnp.repeat(coarse, PATCH, axis=1), PATCH, axis=2)
    mixed = 0.8 * coarse_full + 0.7 * fine
    return jnp.clip(mixed, -6.0, 6.0).astype(jnp.bfloat16)


def set_ends(entries, stream_key, least, largest):
    index_at = [jax.random.randint(jax.random.fold_in(stream_key, axis), (), 0, length) for axis, length in enumerate(entries.shape)]
    main_axis = entries.shape.index(max(entries.shape))
    next_to = index_at[:main_axis] + [(index_at[main_axis] + 1) % entries.shape[main_axis]] + index_at[main_axis + 1:]
    return entries.at[tuple(index_at)].set(least).at[tuple(next_to)].set(largest)


def noise(key, extent, deviation, bound, held_as=jnp.bfloat16):
    array = deviation * jax.random.normal(key, extent, jnp.float32)
    return jnp.clip(array, min=-bound, max=bound).astype(held_as)


def setup_inputs(seed: int = 0, part: int = 0) -> dict:
    key_list = jax.random.split(jax.random.key(seed), 21)
    own_keys = jax.random.split(jax.random.fold_in(key_list[20], part), 21)
    frames = draw_frames(jax.random.fold_in(jax.random.fold_in(key_list[20], part), 71), part)
    valid = set_ends((jax.random.randint(own_keys[1], (EPOCHS, H, W), 0, 4) < 3).astype(jnp.int32), jax.random.fold_in(own_keys[1], 1), 0, 1)
    days = draw_days(jax.random.fold_in(jax.random.fold_in(key_list[20], part), 71), part)
    dw_kernel = noise(key_list[3], (7, 7, C), 49 ** -0.5, 0.875, jnp.float32)
    dw_bias = noise(key_list[4], (C,), 0.5, 3.0, jnp.float32)
    norm_gain = jnp.clip(1.0 + 0.1 * jax.random.normal(key_list[5], (C,), jnp.float32), 0.5, 1.5)
    norm_shift = noise(key_list[6], (C,), 0.3, 1.75, jnp.float32)
    w_expand = noise(key_list[7], (C, FFN), C ** -0.5, 0.3125)
    b_expand = noise(key_list[8], (FFN,), 0.5, 3.0, jnp.float32)
    w_reduce = noise(key_list[9], (FFN, C), FFN ** -0.5, 0.15625)
    layer_scale = jnp.clip(jax.random.uniform(key_list[10], (C,), jnp.float32, 0.3, 1.0), 0.3, 1.0)
    w_gates = noise(key_list[11], (3, 3, C, 4 * C), (9 * C) ** -0.5, 0.109375)
    b_gates = noise(key_list[12], (4 * C,), 0.5, 3.0, jnp.float32)
    forget_rate = jnp.clip(jnp.exp(jax.random.uniform(key_list[13], (C,), jnp.float32, math.log(0.0625), math.log(1.0))), 0.0625, 1.0)
    attn_gain = jnp.clip(1.0 + 0.1 * jax.random.normal(key_list[14], (C,), jnp.float32), 0.5, 1.5)
    w_query = draw_w_query(jax.random.fold_in(key_list[20], 71), part)
    w_key = draw_w_key(jax.random.fold_in(key_list[20], 71), part)
    w_value = noise(key_list[17], (C, C), C ** -0.5, 0.3125)
    w_out = noise(key_list[18], (C, C), C ** -0.5, 0.3125)
    head_slope = jnp.clip(jnp.exp(jax.random.uniform(key_list[19], (HEADS,), jnp.float32, math.log(0.02), math.log(1.0))), 0.02, 1.0)
    return {"frames": frames, "valid": valid, "days": days, "dw_kernel": dw_kernel, "dw_bias": dw_bias, "norm_gain": norm_gain, "norm_shift": norm_shift, "w_expand": w_expand, "b_expand": b_expand, "w_reduce": w_reduce, "layer_scale": layer_scale, "w_gates": w_gates, "b_gates": b_gates, "forget_rate": forget_rate, "attn_gain": attn_gain, "w_query": w_query, "w_key": w_key, "w_value": w_value, "w_out": w_out, "head_slope": head_slope}


def layer_norm(values):
    center = lax.optimization_barrier(jnp.mean(values, axis=-1, keepdims=True))
    centred = values - center
    spread = lax.optimization_barrier(jnp.mean(centred * centred, axis=-1, keepdims=True))
    return centred * lax.rsqrt(spread + 1e-06)

def depthwise(padded, kernel, height, width):
    total = jnp.zeros(padded.shape[:-3] + (height, width, padded.shape[-1]), jnp.float32)
    for offset_y in range(7):
        for offset_x in range(7):
            window = padded[..., offset_y:offset_y + height, offset_x:offset_x + width, :]
            total = total + window.astype(jnp.float32) * kernel[offset_y, offset_x]
    return total

def gate_conv(padded, weights, height, width):
    channels = padded.shape[-1]
    total = None
    for offset_y in range(3):
        for offset_x in range(3):
            window = padded[..., offset_y:offset_y + height, offset_x:offset_x + width, :].reshape(-1, channels)
            term = jnp.dot(window, weights[offset_y, offset_x], preferred_element_type=jnp.float32)
            total = term if total is None else total + term
    return total

def cell_inputs(preact, keep_mask, rates):
    count = preact.shape[-1] // 4
    split = preact.reshape(preact.shape[:-1] + (count, 4))
    gate_in = split[..., 0]
    gate_keep = split[..., 1]
    gate_new = split[..., 2]
    gate_out = split[..., 3]
    mask = keep_mask[..., None]
    decay = jnp.where(mask, jnp.exp(-rates * jax.nn.softplus(gate_keep)), 1.0)
    inflow = jnp.where(mask, jax.nn.sigmoid(gate_in) * jnp.tanh(gate_new), 0.0)
    return (decay, inflow, gate_out)

def reference(frames, valid, days, dw_kernel, dw_bias, norm_gain, norm_shift, w_expand, b_expand, w_reduce, layer_scale, w_gates, b_gates, forget_rate, attn_gain, w_query, w_key, w_value, w_out, head_slope):
    height = frames.shape[1]
    width = frames.shape[2]
    channels = frames.shape[3]

    def one_epoch(cell, inputs):
        frame, valid_now = inputs
        padded = jnp.pad(frame, ((3, 3), (3, 3), (0, 0)))
        spread = depthwise(padded, dw_kernel, height, width) + dw_bias
        normed = (layer_norm(spread) * norm_gain + norm_shift).astype(jnp.bfloat16)
        expanded = jax.nn.gelu(jnp.dot(normed.reshape(-1, channels), w_expand, preferred_element_type=jnp.float32) + b_expand, approximate=True).astype(jnp.bfloat16)
        reduced = jnp.dot(expanded, w_reduce, preferred_element_type=jnp.float32)
        features = (frame.astype(jnp.float32) + layer_scale * reduced.reshape(frame.shape)).astype(jnp.bfloat16)
        feature_pad = jnp.pad(features, ((1, 1), (1, 1), (0, 0)))
        preact = gate_conv(feature_pad, w_gates, height, width) + b_gates
        decay, inflow, gate_out = cell_inputs(preact.reshape(height, width, 4 * channels), valid_now > 0, forget_rate)
        cell = decay * cell + inflow
        result = (jax.nn.sigmoid(gate_out) * jnp.tanh(cell)).astype(jnp.bfloat16)
        return (cell, result)
    start_cell = jnp.zeros((height, width, channels), jnp.float32)
    final_cell, memory = lax.scan(one_epoch, start_cell, (frames, valid))
    epochs = frames.shape[0]
    rows_patch = height // PATCH
    cols_patch = width // PATCH
    patches = rows_patch * cols_patch
    pooled = memory.astype(jnp.float32).reshape(epochs, rows_patch, PATCH, cols_patch, PATCH, channels).mean(axis=(2, 4))
    tokens = (layer_norm(pooled.reshape(-1, channels)) * attn_gain).astype(jnp.bfloat16)
    heads = head_slope.shape[0]
    head_dim = channels // heads

    def project(weight):
        return jnp.dot(tokens, weight, preferred_element_type=jnp.float32).astype(jnp.bfloat16).reshape(epochs, patches, heads, head_dim)
    queries = project(w_query)
    keys = project(w_key)
    values = project(w_value)
    raw = jnp.einsum('tphd,sphd->hpts', queries.astype(jnp.float32), keys.astype(jnp.float32), precision=lax.Precision.HIGHEST) / math.sqrt(head_dim)
    months = days.astype(jnp.float32) / 30.0
    bias = -head_slope[:, None, None, None] * (months[:, None] - months[None, :])[None, None, :, :]
    index = jnp.arange(epochs, dtype=jnp.int32)
    allowed = index[:, None] >= index[None, :]
    scores = jnp.where(allowed[None, None], raw + bias, -1e+30)
    top = lax.optimization_barrier(jnp.max(scores, axis=-1, keepdims=True))
    expo = jnp.exp(scores - top)
    weights = expo / lax.optimization_barrier(jnp.sum(expo, axis=-1, keepdims=True))
    mixed = jnp.einsum('hpts,sphd->tphd', weights, values.astype(jnp.float32), precision=lax.Precision.HIGHEST)
    mixed = mixed.reshape(-1, channels).astype(jnp.bfloat16)
    change = jnp.dot(mixed, w_out, preferred_element_type=jnp.float32).astype(jnp.bfloat16)
    return (memory, change.reshape(epochs, rows_patch, cols_patch, channels))
```

```python
import functools
import math

import jax
import jax.numpy as jnp
from jax import lax
from jax.experimental import pallas as pl
from jax.experimental.pallas import tpu as pltpu
from jax.sharding import PartitionSpec as P

PATCH = 16
REACH = 4
LANES = 128
F32 = jnp.float32
BF16 = jnp.bfloat16


def sigmoid(x):
    return 0.5 * jnp.tanh(0.5 * x) + 0.5


def softplus(x):
    return jnp.maximum(x, 0.0) + jnp.log(1.0 + jnp.exp(-jnp.abs(x)))


def gelu(x):
    inner = x * (0.7978845608028654 + (0.7978845608028654 * 0.044715) * (x * x))
    half = 0.5 * x
    return half + half * jnp.tanh(inner)


def block_kernel(
    tiles,
    frames,
    recv_pair,
    recv_next,
    valid,
    dw_kernel,
    dw_bias,
    norm_gain,
    norm_shift,
    b_expand,
    layer_scale,
    b_gates,
    forget_rate,
    w_expand_hbm,
    w_reduce_hbm,
    w_gates_hbm,
    send,
    decay0,
    inflow0,
    keep,
    block,
    open0,
    open1,
    padded,
    spread,
    taps,
    w_expand,
    w_reduce,
    w_gates,
    sems,
):
    epochs, height, width, channels = frames.shape
    groups = channels // LANES
    hidden = w_expand.shape[1]
    rows = height + 2
    pixels = height * width
    wide = 4 * LANES

    copies = [
        pltpu.make_async_copy(w_expand_hbm, w_expand, sems.at[0]),
        pltpu.make_async_copy(w_reduce_hbm, w_reduce, sems.at[1]),
    ]
    gate_copies = [
        pltpu.make_async_copy(
            w_gates_hbm.at[:, pl.ds(j * wide, wide)],
            w_gates.at[:, pl.ds(j * wide, wide)],
            sems.at[2 + j],
        )
        for j in range(groups)
    ]
    for copy in copies + gate_copies:
        copy.start()

    me = lax.axis_index("tile")
    odd = lax.rem(me, 2)
    pair_row = (1 - odd) * (height + REACH)
    next_row = odd * (height + REACH)

    for c in range(groups):
        lanes = pl.ds(c * LANES, LANES)
        for e in range(epochs):
            total_rows = height + 2 * REACH
            padded[c, e, :, 0:8, :] = jnp.zeros((total_rows, 8, LANES), F32)
            padded[c, e, :, 8 + width : 16 + width, :] = jnp.zeros((total_rows, 8, LANES), F32)
            padded[c, e, REACH : REACH + height, 8 : 8 + width, :] = frames[e, :, :, lanes].astype(F32)
            padded[c, e, pl.ds(pair_row, REACH), 8 : 8 + width, :] = recv_pair[e, :, :, lanes].astype(F32)
            padded[c, e, pl.ds(next_row, REACH), 8 : 8 + width, :] = recv_next[e, :, :, lanes].astype(F32)

    step_rows = rows // 2

    def depthwise(index, carry):
        c = index // (2 * epochs)
        rest = index - c * (2 * epochs)
        e = rest // 2
        part = rest - e * 2
        lanes = pl.ds(pl.multiple_of(c * LANES, LANES), LANES)
        start = part * step_rows
        total = [None] * step_rows
        for ox in range(7):
            factors = [dw_kernel[oy, pl.ds(ox, 1), lanes] for oy in range(7)]
            for r in range(step_rows + 6):
                window = padded[c, e, start + r, pl.ds(5 + ox, width), :]
                for oy in range(7):
                    y = r - oy
                    if 0 <= y < step_rows:
                        term = window * factors[oy]
                        total[y] = term if total[y] is None else total[y] + term
        for y in range(step_rows):
            at = pl.multiple_of((e * rows + start + y) * width, width)
            spread[pl.ds(at, width), lanes] = total[y]
        return carry

    lax.fori_loop(0, groups * epochs * 2, depthwise, 0)

    for copy in copies:
        copy.wait()

    count = rows * width
    column = lax.broadcasted_iota(jnp.int32, (count, LANES), 0)
    across = lax.rem(column, width)
    line = column // width
    first = jnp.where(me == 0, 1, 0)
    last = jnp.where(me == tiles - 1, rows - 2, rows - 1)
    inside = jnp.where((line >= first) & (line <= last), 1.0, 0.0)
    for e in range(epochs):
        values = spread[e * count : (e + 1) * count, :] + dw_bias[...]
        center = jnp.mean(values, axis=-1, keepdims=True)
        centred = values - center
        variance = jnp.mean(centred * centred, axis=-1, keepdims=True)
        normed = (centred * lax.rsqrt(variance + 1e-06) * norm_gain[...] + norm_shift[...]).astype(BF16)
        reduced = None
        for k in range(hidden // 512):
            cols = slice(k * 512, (k + 1) * 512)
            grown = jnp.dot(normed, w_expand[:, cols], preferred_element_type=F32) + b_expand[:, cols]
            part = jnp.dot(gelu(grown).astype(BF16), w_reduce[cols, :], preferred_element_type=F32)
            reduced = part if reduced is None else reduced + part
        for c in range(groups):
            lanes = slice(c * LANES, (c + 1) * LANES)
            centre = padded[c, e, REACH - 1 : REACH + height + 1, 8 : 8 + width, :].reshape(count, LANES)
            feature = centre + layer_scale[:, lanes] * reduced[:, lanes]
            feature = (feature * inside).astype(BF16).astype(F32)
            before = jnp.where(across == 0, 0.0, pltpu.roll(feature, 1, 0))
            after = jnp.where(across == width - 1, 0.0, pltpu.roll(feature, count - 1, 0))
            for ox, shifted in enumerate((before, feature, after)):
                packed = shifted.astype(BF16)
                for oy in range(3):
                    at = (oy * 3 + ox) * channels + c * LANES
                    taps[e * pixels : (e + 1) * pixels, at : at + LANES] = packed[
                        oy * width : oy * width + pixels
                    ]

    source = lax.broadcasted_iota(jnp.int32, (wide, wide), 0)
    target = lax.broadcasted_iota(jnp.int32, (wide, wide), 1)
    order = jnp.where(
        source == 4 * lax.rem(target, LANES) + target // LANES, 1.0, 0.0
    ).astype(BF16)
    good = valid[...] > 0
    for j in range(groups):
        gate_copies[j].wait()
        cols = slice(j * wide, (j + 1) * wide)
        lanes = slice(j * LANES, (j + 1) * LANES)
        preact = jnp.dot(taps[...], w_gates[:, cols], preferred_element_type=F32) + b_gates[:, cols]
        high = preact.astype(BF16)
        low = (preact - high.astype(F32)).astype(BF16)
        gates = jnp.dot(high, order, preferred_element_type=F32) + jnp.dot(
            low, order, preferred_element_type=F32
        )
        gate_in = gates[:, :LANES]
        gate_keep = gates[:, LANES : 2 * LANES]
        gate_new = gates[:, 2 * LANES : 3 * LANES]
        gate_out = gates[:, 3 * LANES :]
        decay = jnp.where(good, jnp.exp(-forget_rate[:, lanes] * softplus(gate_keep)), 1.0)
        inflow = jnp.where(good, sigmoid(gate_in) * jnp.tanh(gate_new), 0.0)
        opened = sigmoid(gate_out)
        d0, d1 = decay[:pixels], decay[pixels:]
        i0, i1 = inflow[:pixels], inflow[pixels:]
        decay0[:, lanes] = d0
        inflow0[:, lanes] = i0
        keep[:, lanes] = d0 * d1
        total = d1 * i0 + i1
        block[:, lanes] = total
        send[:, lanes] = total.astype(BF16)
        open0[:, lanes] = opened[:pixels]
        open1[:, lanes] = opened[pixels:]


def run_block(tiles, frames, recv_pair, recv_next, valid, rows, weights):
    epochs, height, width, channels = frames.shape
    w_expand, w_reduce, w_gates = weights
    pixels = height * width
    count = height + 2
    plane = jax.ShapeDtypeStruct((pixels, channels), F32)
    vmem = pl.BlockSpec(memory_space=pltpu.VMEM)
    anywhere = pl.BlockSpec(memory_space=pl.ANY)
    flops = 2 * (epochs * count * width * 2 * w_expand.size + epochs * pixels * w_gates.size)
    return pl.pallas_call(
        functools.partial(block_kernel, tiles),
        name="block",
        out_shape=[jax.ShapeDtypeStruct((pixels, channels), BF16)] + [plane] * 6,
        in_specs=[vmem] * (4 + len(rows)) + [anywhere] * 3,
        out_specs=[vmem] * 7,
        scratch_shapes=[
            pltpu.VMEM((channels // LANES, epochs, height + 2 * REACH, width + 16, LANES), F32),
            pltpu.VMEM((epochs * count * width, channels), F32),
            pltpu.VMEM((epochs * pixels, 9 * channels), BF16),
            pltpu.VMEM(w_expand.shape, BF16),
            pltpu.VMEM(w_reduce.shape, BF16),
            pltpu.VMEM(w_gates.shape, BF16),
            pltpu.SemaphoreType.DMA((2 + channels // LANES,)),
        ],
        compiler_params=pltpu.CompilerParams(vmem_limit_bytes=48 * 2**20),
        cost_estimate=pl.CostEstimate(flops=flops, bytes_accessed=2 * w_gates.size, transcendentals=0),
    )(frames, recv_pair, recv_next, valid, *rows, w_expand, w_reduce, w_gates)


def patch_tokens(first, second, gain):
    pooled = jnp.concatenate(
        [jnp.mean(first, axis=0, keepdims=True), jnp.mean(second, axis=0, keepdims=True)], axis=0
    )
    center = jnp.mean(pooled, axis=-1, keepdims=True)
    centred = pooled - center
    variance = jnp.mean(centred * centred, axis=-1, keepdims=True)
    return (centred * lax.rsqrt(variance + 1e-06) * gain).astype(BF16).astype(F32)


def memory_of(incoming, decay0, inflow0, keep, block, open0, open1):
    cell0 = decay0[...] * incoming + inflow0[...]
    cell1 = keep[...] * incoming + block[...]
    first = (open0[...] * jnp.tanh(cell0)).astype(BF16)
    second = (open1[...] * jnp.tanh(cell1)).astype(BF16)
    return first, second


def put_tokens(known, own, at):
    line = lax.broadcasted_iota(jnp.int32, known.shape, 0)
    return jnp.where(line == at, own[0:1], jnp.where(line == at + 1, own[1:2], known))


def token_kernel(stage, received, incoming, decay0, inflow0, keep, block, open0, open1, gain, known, out):
    if received:
        state = incoming[...].astype(F32)
    else:
        state = jnp.zeros(incoming.shape, F32)
    first, second = memory_of(state, decay0, inflow0, keep, block, open0, open1)
    own = patch_tokens(first.astype(F32), second.astype(F32), gain[...])
    out[...] = put_tokens(known[...].astype(F32), own, 2 * stage).astype(BF16)


def final_kernel(
    incoming,
    decay0,
    inflow0,
    keep,
    block,
    open0,
    open1,
    gain,
    known,
    days,
    slope,
    w_query,
    w_key,
    w_value,
    w_out,
    memory,
    change,
):
    pixels, channels = incoming.shape
    first, second = memory_of(incoming[...].astype(F32), decay0, inflow0, keep, block, open0, open1)
    memory[0] = first
    memory[1] = second
    own = patch_tokens(first.astype(F32), second.astype(F32), gain[...])
    stage = lax.axis_index("epoch")
    tokens = put_tokens(known[...].astype(F32), own, 2 * stage).astype(BF16)
    total = tokens.shape[0]
    heads = slope.shape[1]
    depth = channels // heads

    def project(weight):
        out = jnp.dot(tokens, weight[...], preferred_element_type=F32)
        return out.astype(BF16).astype(F32)

    queries = project(w_query)
    keys = project(w_key)
    values = project(w_value)
    line = lax.broadcasted_iota(jnp.int32, (total, channels), 0)
    member = lax.broadcasted_iota(jnp.int32, (channels, heads), 0) // depth
    head_of = jnp.where(member == lax.broadcasted_iota(jnp.int32, (channels, heads), 1), 1.0, 0.0)
    member_t = lax.broadcasted_iota(jnp.int32, (heads, channels), 1) // depth
    channel_of = jnp.where(
        member_t == lax.broadcasted_iota(jnp.int32, (heads, channels), 0), 1.0, 0.0
    )
    key_index = lax.broadcasted_iota(jnp.int32, (total, heads), 0)
    months = days[...].astype(F32) / 30.0
    results = []
    for step in range(2):
        mine = 2 * stage + step
        query = jnp.sum(jnp.where(line == mine, queries, 0.0), axis=0, keepdims=True)
        raw = jnp.dot(query * keys, head_of, preferred_element_type=F32, precision=lax.Precision.HIGHEST)
        now = jnp.sum(jnp.where(key_index == mine, months, 0.0), axis=0, keepdims=True)
        scores = raw / math.sqrt(depth) - slope[...] * (now - months)
        scores = jnp.where(key_index <= mine, scores, -1e30)
        expo = jnp.exp(scores - jnp.max(scores, axis=0, keepdims=True))
        weights = expo / jnp.sum(expo, axis=0, keepdims=True)
        spread = jnp.dot(weights, channel_of, preferred_element_type=F32, precision=lax.Precision.HIGHEST)
        results.append(jnp.sum(spread * values, axis=0, keepdims=True))
    mixed = jnp.concatenate(results, axis=0).astype(BF16)
    change[...] = jnp.dot(mixed, w_out[...], preferred_element_type=F32).astype(BF16)


def pairs(count, start):
    links = []
    for i in range(start, count - 1, 2):
        links += [(i, i + 1), (i + 1, i)]
    return links


def body(
    frames,
    valid,
    days,
    dw_kernel,
    dw_bias,
    norm_gain,
    norm_shift,
    w_expand,
    b_expand,
    w_reduce,
    layer_scale,
    w_gates,
    b_gates,
    forget_rate,
    attn_gain,
    w_query,
    w_key,
    w_value,
    w_out,
    head_slope,
):
    epochs, height, width, channels = frames.shape
    pixels = height * width
    tiles = lax.axis_size("tile")
    stages = lax.axis_size("epoch")
    total = epochs * stages
    even = lax.rem(lax.axis_index("tile"), 2) == 0
    top = frames[:, :REACH]
    bottom = frames[:, height - REACH :]
    recv_pair = lax.ppermute(jnp.where(even, bottom, top), "tile", pairs(tiles, 0))
    recv_next = lax.ppermute(jnp.where(even, top, bottom), "tile", pairs(tiles, 1))

    def row(vector):
        return vector.reshape(1, -1)

    valid_wide = jnp.broadcast_to(valid.reshape(epochs * pixels, 1), (epochs * pixels, LANES))
    send, *state = run_block(
        tiles,
        frames,
        recv_pair,
        recv_next,
        valid_wide,
        [
            dw_kernel,
            row(dw_bias),
            row(norm_gain),
            row(norm_shift),
            row(b_expand),
            row(layer_scale),
            row(b_gates),
            row(forget_rate),
        ],
        (w_expand, w_reduce, w_gates.reshape(9 * channels, -1)),
    )
    keep, block = state[2], state[3]
    gain = row(attn_gain)
    vmem = pl.BlockSpec(memory_space=pltpu.VMEM)

    def tokens(stage, received, incoming, known):
        return pl.pallas_call(
            functools.partial(token_kernel, stage, received),
            name="tokens",
            out_shape=jax.ShapeDtypeStruct((total, channels), BF16),
            in_specs=[vmem] * 9,
            out_specs=vmem,
            compiler_params=pltpu.CompilerParams(vmem_limit_bytes=16 * 2**20),
        )(incoming, *state, gain, known)

    incoming = jnp.zeros((pixels, channels), BF16)
    known = jnp.zeros((total, channels), BF16)
    if stages <= 8:
        for stage in range(stages - 1):
            link = [(stage, stage + 1)]
            if stage > 0:
                send = (keep * incoming.astype(F32) + block).astype(BF16)
            arrived = lax.ppermute(send, "epoch", link)
            told = lax.ppermute(
                tokens(stage, stage > 0, incoming if stage > 0 else send, known), "epoch", link
            )
            incoming = incoming + arrived
            known = known + told
    else:
        chain = [(i, i + 1) for i in range(stages - 1)]

        def turn(_, arriving):
            out = (keep * arriving.astype(F32) + block).astype(BF16)
            return lax.ppermute(out, "epoch", chain)

        incoming = lax.fori_loop(0, stages - 1, turn, incoming)
        own = tokens(0, True, incoming, known)[:epochs]
        known = lax.all_gather(own, "epoch", axis=0, tiled=True)

    memory, change = pl.pallas_call(
        final_kernel,
        name="final",
        out_shape=[
            jax.ShapeDtypeStruct((epochs, pixels, channels), BF16),
            jax.ShapeDtypeStruct((epochs, channels), BF16),
        ],
        in_specs=[vmem] * 15,
        out_specs=[vmem] * 2,
        compiler_params=pltpu.CompilerParams(vmem_limit_bytes=24 * 2**20),
    )(
        incoming,
        *state,
        gain,
        known,
        days.reshape(-1, 1),
        row(head_slope),
        w_query,
        w_key,
        w_value,
        w_out,
    )
    return (
        memory.reshape(epochs, height, width, channels),
        change.reshape(epochs, 1, 1, channels),
    )


def solution(mesh):
    placed = (
        P("epoch", ("groups", "tile"), None, None),
        P("epoch", ("groups", "tile"), None),
        P("groups"),
    ) + (P(),) * 17
    return jax.shard_map(
        body,
        mesh=mesh,
        in_specs=placed,
        out_specs=(
            P("epoch", ("groups", "tile"), None, None),
            P("epoch", ("groups", "tile"), None, None),
        ),
        check_vma=False,
    )
```

```python
import functools
import math

import jax
import jax.numpy as jnp
from jax import lax
from jax.experimental import pallas as pl
from jax.experimental.pallas import tpu as pltpu
from jax.sharding import PartitionSpec as P

PATCH = 16
REACH = 4
LANES = 128
F32 = jnp.float32
BF16 = jnp.bfloat16


def sigmoid(x):
    return 0.5 * jnp.tanh(0.5 * x) + 0.5


def softplus(x):
    return jnp.maximum(x, 0.0) + jnp.log(1.0 + jnp.exp(-jnp.abs(x)))


def gelu(x):
    inner = x * (0.7978845608028654 + (0.7978845608028654 * 0.044715) * (x * x))
    half = 0.5 * x
    return half + half * jnp.tanh(inner)


def stage_kernel(
    frames_hbm,
    valid_hbm,
    days_hbm,
    dw_hbm,
    dw_bias_hbm,
    norm_gain_hbm,
    norm_shift_hbm,
    b_expand_hbm,
    layer_scale_hbm,
    b_gates_hbm,
    forget_rate_hbm,
    attn_gain_hbm,
    head_slope_hbm,
    w_expand_hbm,
    w_reduce_hbm,
    w_query_hbm,
    w_key_hbm,
    w_value_hbm,
    w_out_hbm,
    spread,
    mask,
    short_rows,
    long_rows,
    months,
    slope,
    frames,
    dw_kernel,
    w_expand,
    w_reduce,
    w_qkv,
    w_out,
    padded,
    valid,
    days,
    slope_line,
    short_lines,
    long_lines,
    sems,
):
    epochs, height, width, channels = frames.shape
    groups = channels // LANES
    rows = height + 2
    pixels = height * width
    moves = [
        (frames_hbm, frames),
        (dw_hbm, dw_kernel),
        (valid_hbm, valid),
        (days_hbm, days),
        (head_slope_hbm, slope_line),
        (b_expand_hbm, long_lines[0]),
        (b_gates_hbm, long_lines[1]),
        (dw_bias_hbm, short_lines[0]),
        (norm_gain_hbm, short_lines[1]),
        (norm_shift_hbm, short_lines[2]),
        (layer_scale_hbm, short_lines[3]),
        (forget_rate_hbm, short_lines[4]),
        (attn_gain_hbm, short_lines[5]),
        (w_expand_hbm, w_expand),
        (w_reduce_hbm, w_reduce),
        (w_query_hbm, w_qkv.at[:, pl.ds(0, channels)]),
        (w_key_hbm, w_qkv.at[:, pl.ds(channels, channels)]),
        (w_value_hbm, w_qkv.at[:, pl.ds(2 * channels, channels)]),
        (w_out_hbm, w_out),
    ]
    copies = [pltpu.make_async_copy(a, b, sems.at[i]) for i, (a, b) in enumerate(moves)]
    for copy in copies:
        copy.start()

    for c in range(groups):
        for e in range(epochs):
            padded[c, e, :, 0:8, :] = jnp.zeros((height, 8, LANES), F32)
            padded[c, e, :, 8 + width : 16 + width, :] = jnp.zeros((height, 8, LANES), F32)
    copies[0].wait()
    for c in range(groups):
        for e in range(epochs):
            lanes = slice(c * LANES, (c + 1) * LANES)
            padded[c, e, :, 8 : 8 + width, :] = frames[e, :, :, lanes].astype(F32)
    copies[1].wait()

    half = rows // 2

    def depthwise(index, carry):
        c = index // epochs
        e = index - c * epochs
        lanes = pl.ds(pl.multiple_of(c * LANES, LANES), LANES)
        for part in range(2):
            total = [None] * half
            for ox in range(7):
                factors = [dw_kernel[oy, pl.ds(ox, 1), lanes] for oy in range(7)]
                for r in range(height):
                    at = [(y, r + REACH - (part * half + y)) for y in range(half)]
                    at = [(y, oy) for y, oy in at if 0 <= oy < 7]
                    if not at:
                        continue
                    window = padded[c, e, r, pl.ds(5 + ox, width), :]
                    for y, oy in at:
                        term = window * factors[oy]
                        total[y] = term if total[y] is None else total[y] + term
            for y in range(half):
                line = (part * half + y) * width
                spread[e, pl.ds(line, width), lanes] = total[y]
        return carry

    lax.fori_loop(0, groups * epochs, depthwise, 0)

    for copy in copies[2:]:
        copy.wait()
    for k in range(6):
        short_rows[k : k + 1, :] = short_lines[k][...].reshape(1, -1)
    for k in range(2):
        long_rows[k : k + 1, :] = long_lines[k][...].reshape(1, -1)
    slope[...] = slope_line[...].reshape(1, -1)
    total = days.shape[0]
    eye = lax.broadcasted_iota(jnp.int32, (total, total), 0) == lax.broadcasted_iota(
        jnp.int32, (total, total), 1
    )
    month = days[...].astype(F32).reshape(1, -1) / 30.0
    months[...] = jnp.broadcast_to(
        jnp.sum(jnp.where(eye, month, 0.0), axis=1, keepdims=True), months.shape
    )
    down = lax.broadcasted_iota(jnp.int32, (pixels, height), 0) // width
    pick = jnp.where(down == lax.broadcasted_iota(jnp.int32, (pixels, height), 1), 1.0, 0.0).astype(BF16)
    side = lax.rem(lax.broadcasted_iota(jnp.int32, (pixels, width), 0), width)
    place = side == lax.broadcasted_iota(jnp.int32, (pixels, width), 1)
    ones = jnp.ones((width, LANES), BF16)
    for e in range(epochs):
        plane = jnp.where(valid[e] > 0, 1.0, 0.0).astype(BF16)
        lines = jnp.dot(pick, plane, preferred_element_type=F32)
        mask[e * pixels : (e + 1) * pixels, :] = jnp.dot(
            jnp.where(place, lines, 0.0).astype(BF16), ones, preferred_element_type=F32
        )


def run_stage(frames, valid, days, dw_kernel, short, long, slope, w_expand, w_reduce, w_qkvo):
    epochs, height, width, channels = frames.shape
    pixels = height * width
    total = days.shape[0]
    operands = [frames, valid, days, dw_kernel]
    operands += [short[0], short[1], short[2], long[0], short[3], long[1], short[4], short[5], slope]
    operands += [w_expand, w_reduce, *w_qkvo]
    hbm = pl.BlockSpec(memory_space=pltpu.HBM)
    vmem = pl.BlockSpec(memory_space=pltpu.VMEM)
    out_shape = [
        jax.ShapeDtypeStruct((epochs, (height + 2) * width, channels), F32),
        jax.ShapeDtypeStruct((epochs * pixels, LANES), F32),
        jax.ShapeDtypeStruct((8, channels), F32),
        jax.ShapeDtypeStruct((8, long[0].size), F32),
        jax.ShapeDtypeStruct((total, LANES), F32),
        jax.ShapeDtypeStruct((1, slope.size), F32),
        jax.ShapeDtypeStruct(frames.shape, BF16),
        jax.ShapeDtypeStruct(dw_kernel.shape, F32),
        jax.ShapeDtypeStruct(w_expand.shape, BF16),
        jax.ShapeDtypeStruct(w_reduce.shape, BF16),
        jax.ShapeDtypeStruct((channels, 3 * channels), BF16),
        jax.ShapeDtypeStruct((channels, channels), BF16),
    ]
    return pl.pallas_call(
        stage_kernel,
        name="stage",
        out_shape=out_shape,
        in_specs=[hbm] * len(operands),
        out_specs=[vmem] * len(out_shape),
        scratch_shapes=[
            pltpu.VMEM((channels // LANES, epochs, height, width + 16, LANES), F32),
            pltpu.VMEM(valid.shape, jnp.int32),
            pltpu.VMEM(days.shape, jnp.int32),
            pltpu.VMEM(slope.shape, F32),
            [pltpu.VMEM((channels,), F32)] * 6,
            [pltpu.VMEM((long[0].size,), F32)] * 2,
            pltpu.SemaphoreType.DMA((len(operands),)),
        ],
        compiler_params=pltpu.CompilerParams(vmem_limit_bytes=24 * 2**20),
        cost_estimate=pl.CostEstimate(
            flops=10**10, bytes_accessed=8 * w_expand.size, transcendentals=0
        ),
    )(*operands)


def block_kernel(
    tiles,
    spread,
    recv_pair,
    recv_next,
    frames,
    mask,
    short_rows,
    long_rows,
    dw_kernel,
    w_expand,
    w_reduce,
    w_gates_hbm,
    send,
    decay0,
    inflow0,
    keep,
    block,
    open0,
    open1,
    rim,
    edge,
    taps,
    w_gates,
    sems,
):
    epochs, height, width, channels = frames.shape
    groups = channels // LANES
    hidden = w_expand.shape[1]
    rows = height + 2
    pixels = height * width
    wide = 4 * LANES

    gate_copies = [
        pltpu.make_async_copy(
            w_gates_hbm.at[:, pl.ds(j * wide, wide)],
            w_gates.at[:, pl.ds(j * wide, wide)],
            sems.at[j],
        )
        for j in range(groups)
    ]
    for copy in gate_copies:
        copy.start()

    dw_bias = short_rows[0:1, :]
    norm_gain = short_rows[1:2, :]
    norm_shift = short_rows[2:3, :]
    layer_scale = short_rows[3:4, :]
    forget_rate = short_rows[4:5, :]
    attn_gain = short_rows[5:6, :]
    b_expand = long_rows[0:1, :]
    b_gates = long_rows[1:2, :]

    me = lax.axis_index("tile")
    odd = lax.rem(me, 2)
    pair_row = (1 - odd) * REACH
    next_row = odd * REACH

    for c in range(groups):
        lanes = slice(c * LANES, (c + 1) * LANES)
        for e in range(epochs):
            rim[c, e, :, 0:8, :] = jnp.zeros((2 * REACH, 8, LANES), F32)
            rim[c, e, :, 8 + width : 16 + width, :] = jnp.zeros((2 * REACH, 8, LANES), F32)
            rim[c, e, pl.ds(pair_row, REACH), 8 : 8 + width, :] = recv_pair[e, :, :, lanes].astype(F32)
            rim[c, e, pl.ds(next_row, REACH), 8 : 8 + width, :] = recv_next[e, :, :, lanes].astype(F32)

    def depthwise(index, carry):
        c = index // epochs
        e = index - c * epochs
        lanes = pl.ds(pl.multiple_of(c * LANES, LANES), LANES)
        total = [None] * (2 * REACH)
        for ox in range(7):
            factors = [dw_kernel[oy, pl.ds(ox, 1), lanes] for oy in range(7)]
            for k in range(REACH):
                above = rim[c, e, k, pl.ds(5 + ox, width), :]
                below = rim[c, e, REACH + k, pl.ds(5 + ox, width), :]
                for y in range(k + 1):
                    term = above * factors[k - y]
                    total[y] = term if total[y] is None else total[y] + term
                for y in range(k, REACH):
                    term = below * factors[6 + k - y]
                    at = REACH + y
                    total[at] = term if total[at] is None else total[at] + term
        for y in range(2 * REACH):
            edge[e, pl.ds(y * width, width), lanes] = total[y]
        return carry

    lax.fori_loop(0, groups * epochs, depthwise, 0)

    count = rows * width
    rimmed = REACH * width
    column = lax.broadcasted_iota(jnp.int32, (count, LANES), 0)
    across = lax.rem(column, width)
    line = column // width
    first = jnp.where(me == 0, 1, 0)
    last = jnp.where(me == tiles - 1, rows - 2, rows - 1)
    inside = jnp.where((line >= first) & (line <= last), 1.0, 0.0)
    for e in range(epochs):
        values = (
            jnp.concatenate(
                [
                    spread[e, :rimmed] + edge[e, :rimmed],
                    spread[e, rimmed : count - rimmed],
                    spread[e, count - rimmed :] + edge[e, rimmed:],
                ],
                axis=0,
            )
            + dw_bias
        )
        center = jnp.mean(values, axis=-1, keepdims=True)
        centred = values - center
        variance = jnp.mean(centred * centred, axis=-1, keepdims=True)
        normed = (centred * lax.rsqrt(variance + 1e-06) * norm_gain + norm_shift).astype(BF16)
        reduced = None
        for k in range(hidden // 512):
            cols = slice(k * 512, (k + 1) * 512)
            grown = jnp.dot(normed, w_expand[:, cols], preferred_element_type=F32) + b_expand[:, cols]
            part = jnp.dot(gelu(grown).astype(BF16), w_reduce[cols, :], preferred_element_type=F32)
            reduced = part if reduced is None else reduced + part
        for c in range(groups):
            lanes = slice(c * LANES, (c + 1) * LANES)
            centre = jnp.concatenate(
                [
                    rim[c, e, REACH - 1, 8 : 8 + width, :],
                    frames[e, :, :, lanes].astype(F32).reshape(pixels, LANES),
                    rim[c, e, REACH, 8 : 8 + width, :],
                ],
                axis=0,
            )
            feature = centre + layer_scale[:, lanes] * reduced[:, lanes]
            feature = (feature * inside).astype(BF16).astype(F32)
            before = jnp.where(across == 0, 0.0, pltpu.roll(feature, 1, 0))
            after = jnp.where(across == width - 1, 0.0, pltpu.roll(feature, count - 1, 0))
            for ox, shifted in enumerate((before, feature, after)):
                packed = shifted.astype(BF16)
                for oy in range(3):
                    at = (oy * 3 + ox) * channels + c * LANES
                    taps[e * pixels : (e + 1) * pixels, at : at + LANES] = packed[
                        oy * width : oy * width + pixels
                    ]

    quarter = LANES // 4
    lane = lax.broadcasted_iota(jnp.int32, (epochs * pixels, LANES), 1)
    spot = lane // quarter
    within = lane - spot * quarter
    good = mask[...] > 0.5
    pooled = [[], []]
    for j in range(groups):
        gate_copies[j].wait()
        cols = slice(j * wide, (j + 1) * wide)
        lanes = slice(j * LANES, (j + 1) * LANES)
        preact = jnp.dot(taps[...], w_gates[:, cols], preferred_element_type=F32) + b_gates[:, cols]
        sorted_ = []
        for i in range(4):
            gate = lax.rem(spot - i + 4, 4)
            sorted_.append(
                jnp.take_along_axis(preact[:, i * LANES : (i + 1) * LANES], 4 * within + gate, axis=1)
            )
        gates = []
        for g in range(4):
            out = sorted_[0]
            for i in range(1, 4):
                out = jnp.where(spot == (g + i) % 4, sorted_[i], out)
            gates.append(out if g == 0 else pltpu.roll(out, LANES - g * quarter, 1))
        gate_in, gate_keep, gate_new, gate_out = gates
        decay = jnp.where(good, jnp.exp(-forget_rate[:, lanes] * softplus(gate_keep)), 1.0)
        inflow = jnp.where(good, sigmoid(gate_in) * jnp.tanh(gate_new), 0.0)
        opened = sigmoid(gate_out)
        d0, d1 = decay[:pixels], decay[pixels:]
        i0, i1 = inflow[:pixels], inflow[pixels:]
        decay0[:, lanes] = d0
        inflow0[:, lanes] = i0
        keep[:, lanes] = d0 * d1
        total = d1 * i0 + i1
        block[:, lanes] = total
        send[:pixels, lanes] = total.astype(BF16)
        open0[:, lanes] = opened[:pixels]
        open1[:, lanes] = opened[pixels:]
        pooled[0].append(pool(opened[:pixels] * jnp.tanh(i0)))
        pooled[1].append(pool(opened[pixels:] * jnp.tanh(total)))
    own = tokens_of([jnp.concatenate(parts, axis=1) for parts in pooled], attn_gain)
    known = jnp.zeros((send.shape[0] - pixels, channels), F32)
    send[pixels:, :] = put_tokens(known, own, 0).astype(BF16)


def run_block(tiles, staged, recv_pair, recv_next, w_gates, tail):
    spread, mask, short_rows, long_rows, frames, dw_kernel, w_expand, w_reduce = staged
    epochs, height, width, channels = frames.shape
    pixels = height * width
    plane = jax.ShapeDtypeStruct((pixels, channels), F32)
    vmem = pl.BlockSpec(memory_space=pltpu.VMEM)
    hbm = pl.BlockSpec(memory_space=pltpu.HBM)
    flops = 2 * epochs * pixels * (2 * w_expand.size + w_gates.size)
    return pl.pallas_call(
        functools.partial(block_kernel, tiles),
        name="block",
        out_shape=[jax.ShapeDtypeStruct((pixels + tail, channels), BF16)] + [plane] * 6,
        in_specs=[vmem] * 10 + [hbm],
        out_specs=[vmem] * 7,
        scratch_shapes=[
            pltpu.VMEM((channels // LANES, epochs, 2 * REACH, width + 16, LANES), F32),
            pltpu.VMEM((epochs, 2 * REACH * width, channels), F32),
            pltpu.VMEM((epochs * pixels, 9 * channels), BF16),
            pltpu.VMEM(w_gates.shape, BF16),
            pltpu.SemaphoreType.DMA((channels // LANES,)),
        ],
        compiler_params=pltpu.CompilerParams(vmem_limit_bytes=40 * 2**20),
        cost_estimate=pl.CostEstimate(flops=flops, bytes_accessed=2 * w_gates.size, transcendentals=0),
    )(spread, recv_pair, recv_next, frames, mask, short_rows, long_rows, dw_kernel, w_expand, w_reduce, w_gates)


def pool(memory):
    return jnp.mean(memory.astype(BF16).astype(F32), axis=0, keepdims=True)


def tokens_of(pooled, gain):
    both = jnp.concatenate(pooled, axis=0)
    center = jnp.mean(both, axis=-1, keepdims=True)
    centred = both - center
    variance = jnp.mean(centred * centred, axis=-1, keepdims=True)
    return (centred * lax.rsqrt(variance + 1e-06) * gain).astype(BF16).astype(F32)


def put_tokens(known, own, at):
    line = lax.broadcasted_iota(jnp.int32, known.shape, 0)
    return jnp.where(line == at, own[0:1], jnp.where(line == at + 1, own[1:2], known))


def relay_kernel(stage, arrived, decay0, inflow0, keep, block, open0, open1, short_rows, send):
    pixels = keep.shape[0]
    state = arrived[:pixels].astype(F32)
    cell = keep[...] * state + block[...]
    send[:pixels] = cell.astype(BF16)
    pooled = [
        pool(open0[...] * jnp.tanh(decay0[...] * state + inflow0[...])),
        pool(open1[...] * jnp.tanh(cell)),
    ]
    own = tokens_of(pooled, short_rows[5:6, :])
    send[pixels:] = put_tokens(arrived[pixels:].astype(F32), own, 2 * stage).astype(BF16)


def final_kernel(
    count,
    *refs,
):
    arrived = refs[:count]
    decay0, inflow0, keep, block, open0, open1, short_rows, months, slope, w_qkv, w_out = refs[count : count + 11]
    memory_hbm, change, memory, sems = refs[count + 11 :]
    pixels, channels = keep.shape
    total = months.shape[0]
    tail = arrived[0].shape[0] - pixels
    state = arrived[0][:pixels].astype(F32)
    known = arrived[0][pixels:].astype(F32)
    for more in arrived[1:]:
        state = state + more[:pixels].astype(F32)
        known = known + more[pixels:].astype(F32)
    cell0 = decay0[...] * state + inflow0[...]
    cell1 = keep[...] * state + block[...]
    outs = []
    copies = []
    for e, (gate, cell) in enumerate(((open0, cell0), (open1, cell1))):
        out = (gate[...] * jnp.tanh(cell)).astype(BF16)
        memory[e] = out
        copies.append(pltpu.make_async_copy(memory.at[e], memory_hbm.at[e], sems.at[e]))
        copies[-1].start()
        outs.append(out)
    own = tokens_of([pool(out) for out in outs], short_rows[5:6, :])
    stage = lax.axis_index("epoch")
    tokens = put_tokens(known, own, 2 * stage).astype(BF16)
    heads = slope.shape[1]
    depth = channels // heads
    qkv = jnp.dot(tokens, w_qkv[...], preferred_element_type=F32).astype(BF16).astype(F32)[:total]
    queries = qkv[:, :channels]
    keys = qkv[:, channels : 2 * channels]
    values = qkv[:, 2 * channels :]
    line = lax.broadcasted_iota(jnp.int32, (total, channels), 0)
    member = lax.broadcasted_iota(jnp.int32, (channels, heads), 0) // depth
    head_of = jnp.where(member == lax.broadcasted_iota(jnp.int32, (channels, heads), 1), 1.0, 0.0)
    member_t = lax.broadcasted_iota(jnp.int32, (heads, channels), 1) // depth
    channel_of = jnp.where(
        member_t == lax.broadcasted_iota(jnp.int32, (heads, channels), 0), 1.0, 0.0
    )
    key_index = lax.broadcasted_iota(jnp.int32, (total, heads), 0)
    month = months[:, :heads]
    results = []
    for step in range(2):
        mine = 2 * stage + step
        query = jnp.sum(jnp.where(line == mine, queries, 0.0), axis=0, keepdims=True)
        raw = jnp.dot(query * keys, head_of, preferred_element_type=F32, precision=lax.Precision.HIGHEST)
        now = jnp.sum(jnp.where(key_index == mine, month, 0.0), axis=0, keepdims=True)
        scores = raw / math.sqrt(depth) - slope[...] * (now - month)
        scores = jnp.where(key_index <= mine, scores, -1e30)
        expo = jnp.exp(scores - jnp.max(scores, axis=0, keepdims=True))
        weights = expo / jnp.sum(expo, axis=0, keepdims=True)
        spread = jnp.dot(weights, channel_of, preferred_element_type=F32, precision=lax.Precision.HIGHEST)
        results.append(jnp.sum(spread * values, axis=0, keepdims=True))
    mixed = jnp.concatenate(results, axis=0).astype(BF16)
    change[...] = jnp.dot(mixed, w_out[...], preferred_element_type=F32).astype(BF16)
    for copy in copies:
        copy.wait()


def pairs(count, start):
    links = []
    for i in range(start, count - 1, 2):
        links += [(i, i + 1), (i + 1, i)]
    return links


def body(
    frames,
    valid,
    days,
    dw_kernel,
    dw_bias,
    norm_gain,
    norm_shift,
    w_expand,
    b_expand,
    w_reduce,
    layer_scale,
    w_gates,
    b_gates,
    forget_rate,
    attn_gain,
    w_query,
    w_key,
    w_value,
    w_out,
    head_slope,
):

    epochs, height, width, channels = frames.shape
    pixels = height * width
    tiles = lax.axis_size("tile")
    stages = lax.axis_size("epoch")
    total = epochs * stages
    tail = -(-total // 16) * 16
    even = lax.rem(lax.axis_index("tile"), 2) == 0
    top = frames[:, :REACH]
    bottom = frames[:, height - REACH :]
    recv_pair = lax.ppermute(jnp.where(even, bottom, top), "tile", pairs(tiles, 0))
    recv_next = lax.ppermute(jnp.where(even, top, bottom), "tile", pairs(tiles, 1))
    (
        spread,
        mask,
        short_rows,
        long_rows,
        months,
        slope,
        frames_near,
        dw_near,
        expand_near,
        reduce_near,
        qkv_near,
        out_near,
    ) = run_stage(
        frames,
        valid,
        days,
        dw_kernel,
        [dw_bias, norm_gain, norm_shift, layer_scale, forget_rate, attn_gain],
        [b_expand, b_gates],
        head_slope,
        w_expand,
        w_reduce,
        [w_query, w_key, w_value, w_out],
    )
    send, *state = run_block(
        tiles,
        (spread, mask, short_rows, long_rows, frames_near, dw_near, expand_near, reduce_near),
        recv_pair,
        recv_next,
        w_gates.reshape(9 * channels, -1),
        tail,
    )
    vmem = pl.BlockSpec(memory_space=pltpu.VMEM)

    def relay(stage, arrived):
        return pl.pallas_call(
            functools.partial(relay_kernel, stage),
            name="relay",
            out_shape=jax.ShapeDtypeStruct((pixels + tail, channels), BF16),
            in_specs=[vmem] * 8,
            out_specs=vmem,
            compiler_params=pltpu.CompilerParams(vmem_limit_bytes=16 * 2**20),
        )(arrived, *state, short_rows)

    arrived = []
    if stages <= 8:
        for stage in range(stages - 1):
            if stage > 0:
                send = relay(stage, arrived[-1])
            arrived.append(lax.ppermute(send, "epoch", [(stage, stage + 1)]))
    else:
        chain = [(i, i + 1) for i in range(stages - 1)]
        keep, block = state[2], state[3]

        def turn(_, arriving):
            out = (keep * arriving.astype(F32) + block).astype(BF16)
            return lax.ppermute(out, "epoch", chain)

        incoming = lax.fori_loop(0, stages - 1, turn, jnp.zeros((pixels, channels), BF16))
        blank = jnp.zeros((tail, channels), BF16)
        own = relay(0, jnp.concatenate([incoming, blank]))[pixels : pixels + epochs]
        known = lax.all_gather(own, "epoch", axis=0, tiled=True)
        known = jnp.concatenate([known, jnp.zeros((tail - total, channels), BF16)])
        arrived.append(jnp.concatenate([incoming, known]))

    memory, change = pl.pallas_call(
        functools.partial(final_kernel, len(arrived)),
        name="final",
        out_shape=[
            jax.ShapeDtypeStruct((epochs, pixels, channels), BF16),
            jax.ShapeDtypeStruct((epochs, channels), BF16),
        ],
        in_specs=[vmem] * (len(arrived) + 11),
        out_specs=[pl.BlockSpec(memory_space=pltpu.HBM), vmem],
        scratch_shapes=[
            pltpu.VMEM((epochs, pixels, channels), BF16),
            pltpu.SemaphoreType.DMA((epochs,)),
        ],
        compiler_params=pltpu.CompilerParams(vmem_limit_bytes=24 * 2**20),
    )(*arrived, *state, short_rows, months, slope, qkv_near, out_near)
    return (
        memory.reshape(epochs, height, width, channels),
        change.reshape(epochs, 1, 1, channels),
    )


def solution(mesh):
    placed = (
        P("epoch", ("groups", "tile"), None, None),
        P("epoch", ("groups", "tile"), None),
        P("groups"),
    ) + (P(),) * 17
    return jax.shard_map(
        body,
        mesh=mesh,
        in_specs=placed,
        out_specs=(
            P("epoch", ("groups", "tile"), None, None),
            P("epoch", ("groups", "tile"), None, None),
        ),
        check_vma=False,
    )
```

```python
import functools
import math

import jax
import jax.numpy as jnp
from jax import lax
from jax.experimental import pallas as pl
from jax.experimental.pallas import tpu as pltpu
from jax.sharding import PartitionSpec as P

PATCH = 16
REACH = 4
LANES = 128
F32 = jnp.float32
BF16 = jnp.bfloat16


def sigmoid(x):
    return 0.5 * jnp.tanh(0.5 * x) + 0.5


def softplus(x):
    return jnp.maximum(x, 0.0) + jnp.log(1.0 + jnp.exp(-jnp.abs(x)))


def gelu(x):
    inner = x * (0.7978845608028654 + (0.7978845608028654 * 0.044715) * (x * x))
    half = 0.5 * x
    return half + half * jnp.tanh(inner)


def stage_kernel(
    frames_hbm,
    valid_hbm,
    days_hbm,
    dw_hbm,
    dw_bias_hbm,
    norm_gain_hbm,
    norm_shift_hbm,
    b_expand_hbm,
    layer_scale_hbm,
    b_gates_hbm,
    forget_rate_hbm,
    attn_gain_hbm,
    head_slope_hbm,
    w_expand_hbm,
    w_reduce_hbm,
    w_query_hbm,
    w_key_hbm,
    w_value_hbm,
    w_out_hbm,
    spread,
    mask,
    short_rows,
    long_rows,
    months,
    slope,
    frames,
    dw_kernel,
    w_expand,
    w_reduce,
    w_qkv,
    w_out,
    padded,
    valid,
    days,
    slope_line,
    short_lines,
    long_lines,
    sems,
):
    epochs, height, width, channels = frames.shape
    groups = channels // LANES
    rows = height + 2
    pixels = height * width
    moves = [
        (frames_hbm, frames),
        (dw_hbm, dw_kernel),
        (valid_hbm, valid),
        (days_hbm, days),
        (head_slope_hbm, slope_line),
        (b_expand_hbm, long_lines[0]),
        (b_gates_hbm, long_lines[1]),
        (dw_bias_hbm, short_lines[0]),
        (norm_gain_hbm, short_lines[1]),
        (norm_shift_hbm, short_lines[2]),
        (layer_scale_hbm, short_lines[3]),
        (forget_rate_hbm, short_lines[4]),
        (attn_gain_hbm, short_lines[5]),
        (w_expand_hbm, w_expand),
        (w_reduce_hbm, w_reduce),
        (w_query_hbm, w_qkv.at[:, pl.ds(0, channels)]),
        (w_key_hbm, w_qkv.at[:, pl.ds(channels, channels)]),
        (w_value_hbm, w_qkv.at[:, pl.ds(2 * channels, channels)]),
        (w_out_hbm, w_out),
    ]
    copies = [pltpu.make_async_copy(a, b, sems.at[i]) for i, (a, b) in enumerate(moves)]
    for copy in copies:
        copy.start()

    for c in range(groups):
        for e in range(epochs):
            padded[c, e, :, 0:8, :] = jnp.zeros((height, 8, LANES), F32)
            padded[c, e, :, 8 + width : 16 + width, :] = jnp.zeros((height, 8, LANES), F32)
    copies[0].wait()
    for c in range(groups):
        for e in range(epochs):
            lanes = slice(c * LANES, (c + 1) * LANES)
            padded[c, e, :, 8 : 8 + width, :] = frames[e, :, :, lanes].astype(F32)
    copies[1].wait()

    half = rows // 2

    def depthwise(index, carry):
        c = index // epochs
        e = index - c * epochs
        lanes = pl.ds(pl.multiple_of(c * LANES, LANES), LANES)
        for part in range(2):
            total = [None] * half
            for ox in range(7):
                factors = [dw_kernel[oy, pl.ds(ox, 1), lanes] for oy in range(7)]
                for r in range(height):
                    at = [(y, r + REACH - (part * half + y)) for y in range(half)]
                    at = [(y, oy) for y, oy in at if 0 <= oy < 7]
                    if not at:
                        continue
                    window = padded[c, e, r, pl.ds(5 + ox, width), :]
                    for y, oy in at:
                        term = window * factors[oy]
                        total[y] = term if total[y] is None else total[y] + term
            for y in range(half):
                line = (part * half + y) * width
                spread[e, pl.ds(line, width), lanes] = total[y]
        return carry

    lax.fori_loop(0, groups * epochs, depthwise, 0)

    for copy in copies[2:]:
        copy.wait()
    for k in range(6):
        short_rows[k : k + 1, :] = short_lines[k][...].reshape(1, -1)
    for k in range(2):
        long_rows[k : k + 1, :] = long_lines[k][...].reshape(1, -1)
    slope[...] = slope_line[...].reshape(1, -1)
    total = days.shape[0]
    eye = lax.broadcasted_iota(jnp.int32, (total, total), 0) == lax.broadcasted_iota(
        jnp.int32, (total, total), 1
    )
    month = days[...].astype(F32).reshape(1, -1) / 30.0
    months[...] = jnp.broadcast_to(
        jnp.sum(jnp.where(eye, month, 0.0), axis=1, keepdims=True), months.shape
    )
    down = lax.broadcasted_iota(jnp.int32, (pixels, height), 0) // width
    pick = jnp.where(down == lax.broadcasted_iota(jnp.int32, (pixels, height), 1), 1.0, 0.0).astype(BF16)
    side = lax.rem(lax.broadcasted_iota(jnp.int32, (pixels, width), 0), width)
    place = side == lax.broadcasted_iota(jnp.int32, (pixels, width), 1)
    ones = jnp.ones((width, LANES), BF16)
    for e in range(epochs):
        plane = jnp.where(valid[e] > 0, 1.0, 0.0).astype(BF16)
        lines = jnp.dot(pick, plane, preferred_element_type=F32)
        mask[e * pixels : (e + 1) * pixels, :] = jnp.dot(
            jnp.where(place, lines, 0.0).astype(BF16), ones, preferred_element_type=F32
        )


def run_stage(frames, valid, days, dw_kernel, short, long, slope, w_expand, w_reduce, w_qkvo):
    epochs, height, width, channels = frames.shape
    pixels = height * width
    total = days.shape[0]
    operands = [frames, valid, days, dw_kernel]
    operands += [short[0], short[1], short[2], long[0], short[3], long[1], short[4], short[5], slope]
    operands += [w_expand, w_reduce, *w_qkvo]
    operands = [pltpu.with_memory_space_constraint(x, pltpu.HBM) for x in operands]
    hbm = pl.BlockSpec(memory_space=pltpu.HBM)
    vmem = pl.BlockSpec(memory_space=pltpu.VMEM)
    out_shape = [
        jax.ShapeDtypeStruct((epochs, (height + 2) * width, channels), F32),
        jax.ShapeDtypeStruct((epochs * pixels, LANES), F32),
        jax.ShapeDtypeStruct((8, channels), F32),
        jax.ShapeDtypeStruct((8, long[0].size), F32),
        jax.ShapeDtypeStruct((total, LANES), F32),
        jax.ShapeDtypeStruct((1, slope.size), F32),
        jax.ShapeDtypeStruct(frames.shape, BF16),
        jax.ShapeDtypeStruct(dw_kernel.shape, F32),
        jax.ShapeDtypeStruct(w_expand.shape, BF16),
        jax.ShapeDtypeStruct(w_reduce.shape, BF16),
        jax.ShapeDtypeStruct((channels, 3 * channels), BF16),
        jax.ShapeDtypeStruct((channels, channels), BF16),
    ]
    return pl.pallas_call(
        stage_kernel,
        name="stage",
        out_shape=out_shape,
        in_specs=[hbm] * len(operands),
        out_specs=[vmem] * len(out_shape),
        scratch_shapes=[
            pltpu.VMEM((channels // LANES, epochs, height, width + 16, LANES), F32),
            pltpu.VMEM(valid.shape, jnp.int32),
            pltpu.VMEM(days.shape, jnp.int32),
            pltpu.VMEM(slope.shape, F32),
            [pltpu.VMEM((channels,), F32)] * 6,
            [pltpu.VMEM((long[0].size,), F32)] * 2,
            pltpu.SemaphoreType.DMA((len(operands),)),
        ],
        compiler_params=pltpu.CompilerParams(vmem_limit_bytes=24 * 2**20),
        cost_estimate=pl.CostEstimate(
            flops=10**10, bytes_accessed=8 * w_expand.size, transcendentals=0
        ),
    )(*operands)


def block_kernel(
    tiles,
    spread,
    recv_pair,
    recv_next,
    frames,
    mask,
    short_rows,
    long_rows,
    dw_kernel,
    w_expand,
    w_reduce,
    w_gates_hbm,
    send,
    decay0,
    inflow0,
    keep,
    block,
    open0,
    open1,
    rim,
    edge,
    taps,
    w_gates,
    sems,
):
    epochs, height, width, channels = frames.shape
    groups = channels // LANES
    hidden = w_expand.shape[1]
    rows = height + 2
    pixels = height * width
    wide = 4 * LANES

    gate_copies = [
        pltpu.make_async_copy(
            w_gates_hbm.at[:, pl.ds(j * wide, wide)],
            w_gates.at[:, pl.ds(j * wide, wide)],
            sems.at[j],
        )
        for j in range(groups)
    ]
    for copy in gate_copies:
        copy.start()

    dw_bias = short_rows[0:1, :]
    norm_gain = short_rows[1:2, :]
    norm_shift = short_rows[2:3, :]
    layer_scale = short_rows[3:4, :]
    forget_rate = short_rows[4:5, :]
    attn_gain = short_rows[5:6, :]
    b_expand = long_rows[0:1, :]
    b_gates = long_rows[1:2, :]

    me = lax.axis_index("tile")
    odd = lax.rem(me, 2)
    pair_row = (1 - odd) * REACH
    next_row = odd * REACH

    for c in range(groups):
        lanes = slice(c * LANES, (c + 1) * LANES)
        for e in range(epochs):
            rim[c, e, :, 0:8, :] = jnp.zeros((2 * REACH, 8, LANES), F32)
            rim[c, e, :, 8 + width : 16 + width, :] = jnp.zeros((2 * REACH, 8, LANES), F32)
            rim[c, e, pl.ds(pair_row, REACH), 8 : 8 + width, :] = recv_pair[e, :, :, lanes].astype(F32)
            rim[c, e, pl.ds(next_row, REACH), 8 : 8 + width, :] = recv_next[e, :, :, lanes].astype(F32)

    def depthwise(index, carry):
        c = index // epochs
        e = index - c * epochs
        lanes = pl.ds(pl.multiple_of(c * LANES, LANES), LANES)
        total = [None] * (2 * REACH)
        for ox in range(7):
            factors = [dw_kernel[oy, pl.ds(ox, 1), lanes] for oy in range(7)]
            for k in range(REACH):
                above = rim[c, e, k, pl.ds(5 + ox, width), :]
                below = rim[c, e, REACH + k, pl.ds(5 + ox, width), :]
                for y in range(k + 1):
                    term = above * factors[k - y]
                    total[y] = term if total[y] is None else total[y] + term
                for y in range(k, REACH):
                    term = below * factors[6 + k - y]
                    at = REACH + y
                    total[at] = term if total[at] is None else total[at] + term
        for y in range(2 * REACH):
            edge[e, pl.ds(y * width, width), lanes] = total[y]
        return carry

    lax.fori_loop(0, groups * epochs, depthwise, 0)

    count = rows * width
    rimmed = REACH * width
    column = lax.broadcasted_iota(jnp.int32, (count, LANES), 0)
    across = lax.rem(column, width)
    line = column // width
    first = jnp.where(me == 0, 1, 0)
    last = jnp.where(me == tiles - 1, rows - 2, rows - 1)
    inside = jnp.where((line >= first) & (line <= last), 1.0, 0.0)
    for e in range(epochs):
        values = (
            jnp.concatenate(
                [
                    spread[e, :rimmed] + edge[e, :rimmed],
                    spread[e, rimmed : count - rimmed],
                    spread[e, count - rimmed :] + edge[e, rimmed:],
                ],
                axis=0,
            )
            + dw_bias
        )
        center = jnp.mean(values, axis=-1, keepdims=True)
        centred = values - center
        variance = jnp.mean(centred * centred, axis=-1, keepdims=True)
        normed = (centred * lax.rsqrt(variance + 1e-06) * norm_gain + norm_shift).astype(BF16)
        reduced = None
        for k in range(hidden // 512):
            cols = slice(k * 512, (k + 1) * 512)
            grown = jnp.dot(normed, w_expand[:, cols], preferred_element_type=F32) + b_expand[:, cols]
            part = jnp.dot(gelu(grown).astype(BF16), w_reduce[cols, :], preferred_element_type=F32)
            reduced = part if reduced is None else reduced + part
        for c in range(groups):
            lanes = slice(c * LANES, (c + 1) * LANES)
            centre = jnp.concatenate(
                [
                    rim[c, e, REACH - 1, 8 : 8 + width, :],
                    frames[e, :, :, lanes].astype(F32).reshape(pixels, LANES),
                    rim[c, e, REACH, 8 : 8 + width, :],
                ],
                axis=0,
            )
            feature = centre + layer_scale[:, lanes] * reduced[:, lanes]
            feature = (feature * inside).astype(BF16).astype(F32)
            before = jnp.where(across == 0, 0.0, pltpu.roll(feature, 1, 0))
            after = jnp.where(across == width - 1, 0.0, pltpu.roll(feature, count - 1, 0))
            for ox, shifted in enumerate((before, feature, after)):
                packed = shifted.astype(BF16)
                for oy in range(3):
                    at = (oy * 3 + ox) * channels + c * LANES
                    taps[e * pixels : (e + 1) * pixels, at : at + LANES] = packed[
                        oy * width : oy * width + pixels
                    ]

    quarter = LANES // 4
    lane = lax.broadcasted_iota(jnp.int32, (epochs * pixels, LANES), 1)
    spot = lane // quarter
    within = lane - spot * quarter
    good = mask[...] > 0.5
    pooled = [[], []]
    for j in range(groups):
        gate_copies[j].wait()
        cols = slice(j * wide, (j + 1) * wide)
        lanes = slice(j * LANES, (j + 1) * LANES)
        preact = jnp.dot(taps[...], w_gates[:, cols], preferred_element_type=F32) + b_gates[:, cols]
        sorted_ = []
        for i in range(4):
            gate = lax.rem(spot - i + 4, 4)
            sorted_.append(
                jnp.take_along_axis(preact[:, i * LANES : (i + 1) * LANES], 4 * within + gate, axis=1)
            )
        gates = []
        for g in range(4):
            out = sorted_[0]
            for i in range(1, 4):
                out = jnp.where(spot == (g + i) % 4, sorted_[i], out)
            gates.append(out if g == 0 else pltpu.roll(out, LANES - g * quarter, 1))
        gate_in, gate_keep, gate_new, gate_out = gates
        decay = jnp.where(good, jnp.exp(-forget_rate[:, lanes] * softplus(gate_keep)), 1.0)
        inflow = jnp.where(good, sigmoid(gate_in) * jnp.tanh(gate_new), 0.0)
        opened = sigmoid(gate_out)
        d0, d1 = decay[:pixels], decay[pixels:]
        i0, i1 = inflow[:pixels], inflow[pixels:]
        decay0[:, lanes] = d0
        inflow0[:, lanes] = i0
        keep[:, lanes] = d0 * d1
        total = d1 * i0 + i1
        block[:, lanes] = total
        send[:pixels, lanes] = total.astype(BF16)
        open0[:, lanes] = opened[:pixels]
        open1[:, lanes] = opened[pixels:]
        pooled[0].append(pool(opened[:pixels] * jnp.tanh(i0)))
        pooled[1].append(pool(opened[pixels:] * jnp.tanh(total)))
    own = tokens_of([jnp.concatenate(parts, axis=1) for parts in pooled], attn_gain)
    known = jnp.zeros((send.shape[0] - pixels, channels), F32)
    send[pixels:, :] = put_tokens(known, own, 0).astype(BF16)


def run_block(tiles, staged, recv_pair, recv_next, w_gates, tail):
    spread, mask, short_rows, long_rows, frames, dw_kernel, w_expand, w_reduce = staged
    epochs, height, width, channels = frames.shape
    pixels = height * width
    plane = jax.ShapeDtypeStruct((pixels, channels), F32)
    vmem = pl.BlockSpec(memory_space=pltpu.VMEM)
    hbm = pl.BlockSpec(memory_space=pltpu.HBM)
    flops = 2 * epochs * pixels * (2 * w_expand.size + w_gates.size)
    return pl.pallas_call(
        functools.partial(block_kernel, tiles),
        name="block",
        out_shape=[jax.ShapeDtypeStruct((pixels + tail, channels), BF16)] + [plane] * 6,
        in_specs=[vmem] * 10 + [hbm],
        out_specs=[vmem] * 7,
        scratch_shapes=[
            pltpu.VMEM((channels // LANES, epochs, 2 * REACH, width + 16, LANES), F32),
            pltpu.VMEM((epochs, 2 * REACH * width, channels), F32),
            pltpu.VMEM((epochs * pixels, 9 * channels), BF16),
            pltpu.VMEM(w_gates.shape, BF16),
            pltpu.SemaphoreType.DMA((channels // LANES,)),
        ],
        compiler_params=pltpu.CompilerParams(vmem_limit_bytes=40 * 2**20),
        cost_estimate=pl.CostEstimate(flops=flops, bytes_accessed=2 * w_gates.size, transcendentals=0),
    )(spread, recv_pair, recv_next, frames, mask, short_rows, long_rows, dw_kernel, w_expand, w_reduce, w_gates)


def pool(memory):
    return jnp.mean(memory.astype(BF16).astype(F32), axis=0, keepdims=True)


def tokens_of(pooled, gain):
    both = jnp.concatenate(pooled, axis=0)
    center = jnp.mean(both, axis=-1, keepdims=True)
    centred = both - center
    variance = jnp.mean(centred * centred, axis=-1, keepdims=True)
    return (centred * lax.rsqrt(variance + 1e-06) * gain).astype(BF16).astype(F32)


def put_tokens(known, own, at):
    line = lax.broadcasted_iota(jnp.int32, known.shape, 0)
    return jnp.where(line == at, own[0:1], jnp.where(line == at + 1, own[1:2], known))


def relay_kernel(stage, arrived, decay0, inflow0, keep, block, open0, open1, short_rows, send):
    pixels = keep.shape[0]
    state = arrived[:pixels].astype(F32)
    cell = keep[...] * state + block[...]
    send[:pixels] = cell.astype(BF16)
    pooled = [
        pool(open0[...] * jnp.tanh(decay0[...] * state + inflow0[...])),
        pool(open1[...] * jnp.tanh(cell)),
    ]
    own = tokens_of(pooled, short_rows[5:6, :])
    send[pixels:] = put_tokens(arrived[pixels:].astype(F32), own, 2 * stage).astype(BF16)


def final_kernel(
    count,
    *refs,
):
    arrived = refs[:count]
    decay0, inflow0, keep, block, open0, open1, short_rows, months, slope, w_qkv, w_out = refs[count : count + 11]
    memory_hbm, change, memory, sems = refs[count + 11 :]
    pixels, channels = keep.shape
    total = months.shape[0]
    tail = arrived[0].shape[0] - pixels
    state = arrived[0][:pixels].astype(F32)
    known = arrived[0][pixels:].astype(F32)
    for more in arrived[1:]:
        state = state + more[:pixels].astype(F32)
        known = known + more[pixels:].astype(F32)
    cell0 = decay0[...] * state + inflow0[...]
    cell1 = keep[...] * state + block[...]
    outs = []
    copies = []
    for e, (gate, cell) in enumerate(((open0, cell0), (open1, cell1))):
        out = (gate[...] * jnp.tanh(cell)).astype(BF16)
        memory[e] = out
        copies.append(pltpu.make_async_copy(memory.at[e], memory_hbm.at[e], sems.at[e]))
        copies[-1].start()
        outs.append(out)
    own = tokens_of([pool(out) for out in outs], short_rows[5:6, :])
    stage = lax.axis_index("epoch")
    tokens = put_tokens(known, own, 2 * stage).astype(BF16)
    heads = slope.shape[1]
    depth = channels // heads
    qkv = jnp.dot(tokens, w_qkv[...], preferred_element_type=F32).astype(BF16).astype(F32)[:total]
    queries = qkv[:, :channels]
    keys = qkv[:, channels : 2 * channels]
    values = qkv[:, 2 * channels :]
    line = lax.broadcasted_iota(jnp.int32, (total, channels), 0)
    member = lax.broadcasted_iota(jnp.int32, (channels, heads), 0) // depth
    head_of = jnp.where(member == lax.broadcasted_iota(jnp.int32, (channels, heads), 1), 1.0, 0.0)
    member_t = lax.broadcasted_iota(jnp.int32, (heads, channels), 1) // depth
    channel_of = jnp.where(
        member_t == lax.broadcasted_iota(jnp.int32, (heads, channels), 0), 1.0, 0.0
    )
    key_index = lax.broadcasted_iota(jnp.int32, (total, heads), 0)
    month = months[:, :heads]
    results = []
    for step in range(2):
        mine = 2 * stage + step
        query = jnp.sum(jnp.where(line == mine, queries, 0.0), axis=0, keepdims=True)
        raw = jnp.dot(query * keys, head_of, preferred_element_type=F32, precision=lax.Precision.HIGHEST)
        now = jnp.sum(jnp.where(key_index == mine, month, 0.0), axis=0, keepdims=True)
        scores = raw / math.sqrt(depth) - slope[...] * (now - month)
        scores = jnp.where(key_index <= mine, scores, -1e30)
        expo = jnp.exp(scores - jnp.max(scores, axis=0, keepdims=True))
        weights = expo / jnp.sum(expo, axis=0, keepdims=True)
        spread = jnp.dot(weights, channel_of, preferred_element_type=F32, precision=lax.Precision.HIGHEST)
        results.append(jnp.sum(spread * values, axis=0, keepdims=True))
    mixed = jnp.concatenate(results, axis=0).astype(BF16)
    change[...] = jnp.dot(mixed, w_out[...], preferred_element_type=F32).astype(BF16)
    for copy in copies:
        copy.wait()


def pairs(count, start):
    links = []
    for i in range(start, count - 1, 2):
        links += [(i, i + 1), (i + 1, i)]
    return links


def body(
    frames,
    valid,
    days,
    dw_kernel,
    dw_bias,
    norm_gain,
    norm_shift,
    w_expand,
    b_expand,
    w_reduce,
    layer_scale,
    w_gates,
    b_gates,
    forget_rate,
    attn_gain,
    w_query,
    w_key,
    w_value,
    w_out,
    head_slope,
):

    epochs, height, width, channels = frames.shape
    pixels = height * width
    tiles = lax.axis_size("tile")
    stages = lax.axis_size("epoch")
    total = epochs * stages
    tail = -(-total // 16) * 16
    even = lax.rem(lax.axis_index("tile"), 2) == 0
    top = frames[:, :REACH]
    bottom = frames[:, height - REACH :]
    recv_pair = lax.ppermute(jnp.where(even, bottom, top), "tile", pairs(tiles, 0))
    recv_next = lax.ppermute(jnp.where(even, top, bottom), "tile", pairs(tiles, 1))
    (
        spread,
        mask,
        short_rows,
        long_rows,
        months,
        slope,
        frames_near,
        dw_near,
        expand_near,
        reduce_near,
        qkv_near,
        out_near,
    ) = run_stage(
        frames,
        valid,
        days,
        dw_kernel,
        [dw_bias, norm_gain, norm_shift, layer_scale, forget_rate, attn_gain],
        [b_expand, b_gates],
        head_slope,
        w_expand,
        w_reduce,
        [w_query, w_key, w_value, w_out],
    )
    send, *state = run_block(
        tiles,
        (spread, mask, short_rows, long_rows, frames_near, dw_near, expand_near, reduce_near),
        recv_pair,
        recv_next,
        w_gates.reshape(9 * channels, -1),
        tail,
    )
    vmem = pl.BlockSpec(memory_space=pltpu.VMEM)

    def relay(stage, arrived):
        return pl.pallas_call(
            functools.partial(relay_kernel, stage),
            name="relay",
            out_shape=jax.ShapeDtypeStruct((pixels + tail, channels), BF16),
            in_specs=[vmem] * 8,
            out_specs=vmem,
            compiler_params=pltpu.CompilerParams(vmem_limit_bytes=16 * 2**20),
        )(arrived, *state, short_rows)

    arrived = []
    if stages <= 8:
        for stage in range(stages - 1):
            if stage > 0:
                send = relay(stage, arrived[-1])
            arrived.append(lax.ppermute(send, "epoch", [(stage, stage + 1)]))
    else:
        chain = [(i, i + 1) for i in range(stages - 1)]
        keep, block = state[2], state[3]

        def turn(_, arriving):
            out = (keep * arriving.astype(F32) + block).astype(BF16)
            return lax.ppermute(out, "epoch", chain)

        incoming = lax.fori_loop(0, stages - 1, turn, jnp.zeros((pixels, channels), BF16))
        blank = jnp.zeros((tail, channels), BF16)
        own = relay(0, jnp.concatenate([incoming, blank]))[pixels : pixels + epochs]
        known = lax.all_gather(own, "epoch", axis=0, tiled=True)
        known = jnp.concatenate([known, jnp.zeros((tail - total, channels), BF16)])
        arrived.append(jnp.concatenate([incoming, known]))

    memory, change = pl.pallas_call(
        functools.partial(final_kernel, len(arrived)),
        name="final",
        out_shape=[
            jax.ShapeDtypeStruct((epochs, pixels, channels), BF16),
            jax.ShapeDtypeStruct((epochs, channels), BF16),
        ],
        in_specs=[vmem] * (len(arrived) + 11),
        out_specs=[pl.BlockSpec(memory_space=pltpu.HBM), vmem],
        scratch_shapes=[
            pltpu.VMEM((epochs, pixels, channels), BF16),
            pltpu.SemaphoreType.DMA((epochs,)),
        ],
        compiler_params=pltpu.CompilerParams(vmem_limit_bytes=24 * 2**20),
    )(*arrived, *state, short_rows, months, slope, qkv_near, out_near)
    return (
        memory.reshape(epochs, height, width, channels),
        change.reshape(epochs, 1, 1, channels),
    )


def solution(mesh):
    placed = (
        P("epoch", ("groups", "tile"), None, None),
        P("epoch", ("groups", "tile"), None),
        P("groups"),
    ) + (P(),) * 17
    return jax.shard_map(
        body,
        mesh=mesh,
        in_specs=placed,
        out_specs=(
            P("epoch", ("groups", "tile"), None, None),
            P("epoch", ("groups", "tile"), None, None),
        ),
        check_vma=False,
    )
```

```python
import functools
import math

import jax
import jax.numpy as jnp
from jax import lax
from jax.experimental import pallas as pl
from jax.experimental.pallas import tpu as pltpu
from jax.sharding import PartitionSpec as P

PATCH = 16
REACH = 4
LANES = 128
F32 = jnp.float32
BF16 = jnp.bfloat16


def sigmoid(x):
    return 0.5 * jnp.tanh(0.5 * x) + 0.5


def softplus(x):
    return jnp.maximum(x, 0.0) + jnp.log(1.0 + jnp.exp(-jnp.abs(x)))


def gelu(x):
    inner = x * (0.7978845608028654 + (0.7978845608028654 * 0.044715) * (x * x))
    half = 0.5 * x
    return half + half * jnp.tanh(inner)


def stage_kernel(
    frames_hbm,
    valid_hbm,
    days_hbm,
    dw_hbm,
    dw_bias_hbm,
    norm_gain_hbm,
    norm_shift_hbm,
    b_expand_hbm,
    layer_scale_hbm,
    b_gates_hbm,
    forget_rate_hbm,
    attn_gain_hbm,
    head_slope_hbm,
    w_expand_hbm,
    w_reduce_hbm,
    w_query_hbm,
    w_key_hbm,
    w_value_hbm,
    w_out_hbm,
    spread,
    mask,
    short_rows,
    long_rows,
    months,
    slope,
    frames,
    dw_kernel,
    w_expand,
    w_reduce,
    w_qkv,
    w_out,
    padded,
    valid,
    days,
    slope_line,
    short_lines,
    long_lines,
    sems,
):
    epochs, height, width, channels = frames.shape
    groups = channels // LANES
    rows = height + 2
    pixels = height * width
    moves = [
        (frames_hbm, frames),
        (dw_hbm, dw_kernel),
        (valid_hbm, valid),
        (days_hbm, days),
        (head_slope_hbm, slope_line),
        (b_expand_hbm, long_lines[0]),
        (b_gates_hbm, long_lines[1]),
        (dw_bias_hbm, short_lines[0]),
        (norm_gain_hbm, short_lines[1]),
        (norm_shift_hbm, short_lines[2]),
        (layer_scale_hbm, short_lines[3]),
        (forget_rate_hbm, short_lines[4]),
        (attn_gain_hbm, short_lines[5]),
        (w_expand_hbm, w_expand),
        (w_reduce_hbm, w_reduce),
        (w_query_hbm, w_qkv.at[:, pl.ds(0, channels)]),
        (w_key_hbm, w_qkv.at[:, pl.ds(channels, channels)]),
        (w_value_hbm, w_qkv.at[:, pl.ds(2 * channels, channels)]),
        (w_out_hbm, w_out),
    ]
    copies = [pltpu.make_async_copy(a, b, sems.at[i]) for i, (a, b) in enumerate(moves)]
    for copy in copies:
        copy.start()

    for c in range(groups):
        for e in range(epochs):
            padded[c, e, :, 0:8, :] = jnp.zeros((height, 8, LANES), F32)
            padded[c, e, :, 8 + width : 16 + width, :] = jnp.zeros((height, 8, LANES), F32)
    copies[0].wait()
    for c in range(groups):
        for e in range(epochs):
            lanes = slice(c * LANES, (c + 1) * LANES)
            padded[c, e, :, 8 : 8 + width, :] = frames[e, :, :, lanes].astype(F32)
    copies[1].wait()

    half = rows // 2

    def depthwise(index, carry):
        c = index // epochs
        e = index - c * epochs
        lanes = pl.ds(pl.multiple_of(c * LANES, LANES), LANES)
        for part in range(2):
            total = [None] * half
            for ox in range(7):
                factors = [dw_kernel[oy, pl.ds(ox, 1), lanes] for oy in range(7)]
                for r in range(height):
                    at = [(y, r + REACH - (part * half + y)) for y in range(half)]
                    at = [(y, oy) for y, oy in at if 0 <= oy < 7]
                    if not at:
                        continue
                    window = padded[c, e, r, pl.ds(5 + ox, width), :]
                    for y, oy in at:
                        term = window * factors[oy]
                        total[y] = term if total[y] is None else total[y] + term
            for y in range(half):
                line = (part * half + y) * width
                spread[e, pl.ds(line, width), lanes] = total[y]
        return carry

    lax.fori_loop(0, groups * epochs, depthwise, 0)

    for copy in copies[2:]:
        copy.wait()
    for k in range(6):
        short_rows[k : k + 1, :] = short_lines[k][...].reshape(1, -1)
    for k in range(2):
        long_rows[k : k + 1, :] = long_lines[k][...].reshape(1, -1)
    slope[...] = slope_line[...].reshape(1, -1)
    total = days.shape[0]
    eye = lax.broadcasted_iota(jnp.int32, (total, total), 0) == lax.broadcasted_iota(
        jnp.int32, (total, total), 1
    )
    month = days[...].astype(F32).reshape(1, -1) / 30.0
    months[...] = jnp.broadcast_to(
        jnp.sum(jnp.where(eye, month, 0.0), axis=1, keepdims=True), months.shape
    )
    down = lax.broadcasted_iota(jnp.int32, (pixels, height), 0) // width
    pick = jnp.where(down == lax.broadcasted_iota(jnp.int32, (pixels, height), 1), 1.0, 0.0).astype(BF16)
    side = lax.rem(lax.broadcasted_iota(jnp.int32, (pixels, width), 0), width)
    place = side == lax.broadcasted_iota(jnp.int32, (pixels, width), 1)
    ones = jnp.ones((width, LANES), BF16)
    for e in range(epochs):
        plane = jnp.where(valid[e] > 0, 1.0, 0.0).astype(BF16)
        lines = jnp.dot(pick, plane, preferred_element_type=F32)
        mask[e * pixels : (e + 1) * pixels, :] = jnp.dot(
            jnp.where(place, lines, 0.0).astype(BF16), ones, preferred_element_type=F32
        )


def run_stage(frames, valid, days, dw_kernel, short, long, slope, w_expand, w_reduce, w_qkvo):
    epochs, height, width, channels = frames.shape
    pixels = height * width
    total = days.shape[0]
    operands = [frames, valid, days, dw_kernel]
    operands += [short[0], short[1], short[2], long[0], short[3], long[1], short[4], short[5], slope]
    operands += [w_expand, w_reduce, *w_qkvo]
    operands = [pltpu.with_memory_space_constraint(x, pltpu.HBM) for x in operands]
    hbm = pl.BlockSpec(memory_space=pltpu.HBM)
    vmem = pl.BlockSpec(memory_space=pltpu.VMEM)
    out_shape = [
        jax.ShapeDtypeStruct((epochs, (height + 2) * width, channels), F32),
        jax.ShapeDtypeStruct((epochs * pixels, LANES), F32),
        jax.ShapeDtypeStruct((8, channels), F32),
        jax.ShapeDtypeStruct((8, long[0].size), F32),
        jax.ShapeDtypeStruct((total, LANES), F32),
        jax.ShapeDtypeStruct((1, slope.size), F32),
        jax.ShapeDtypeStruct(frames.shape, BF16),
        jax.ShapeDtypeStruct(dw_kernel.shape, F32),
        jax.ShapeDtypeStruct(w_expand.shape, BF16),
        jax.ShapeDtypeStruct(w_reduce.shape, BF16),
        jax.ShapeDtypeStruct((channels, 3 * channels), BF16),
        jax.ShapeDtypeStruct((channels, channels), BF16),
    ]
    return pl.pallas_call(
        stage_kernel,
        name="stage",
        out_shape=out_shape,
        in_specs=[hbm] * len(operands),
        out_specs=[vmem] * len(out_shape),
        scratch_shapes=[
            pltpu.VMEM((channels // LANES, epochs, height, width + 16, LANES), F32),
            pltpu.VMEM(valid.shape, jnp.int32),
            pltpu.VMEM(days.shape, jnp.int32),
            pltpu.VMEM(slope.shape, F32),
            [pltpu.VMEM((channels,), F32)] * 6,
            [pltpu.VMEM((long[0].size,), F32)] * 2,
            pltpu.SemaphoreType.DMA((len(operands),)),
        ],
        compiler_params=pltpu.CompilerParams(vmem_limit_bytes=24 * 2**20),
        cost_estimate=pl.CostEstimate(
            flops=10**10, bytes_accessed=8 * w_expand.size, transcendentals=0
        ),
    )(*operands)


def block_kernel(
    tiles,
    spread,
    recv_pair,
    recv_next,
    frames,
    mask,
    short_rows,
    long_rows,
    dw_kernel,
    w_expand,
    w_reduce,
    w_gates_hbm,
    send,
    pooled,
    decay0,
    inflow0,
    keep,
    block,
    open0,
    open1,
    taps,
    w_later,
    rim,
    edge,
    w_gates,
    sems,
):
    epochs, height, width, channels = frames.shape
    groups = channels // LANES
    hidden = w_expand.shape[1]
    rows = height + 2
    pixels = height * width
    wide = 4 * LANES

    early = w_gates.shape[1] // wide
    gate_copies = [
        pltpu.make_async_copy(
            w_gates_hbm.at[:, pl.ds(j * wide, wide)],
            w_gates.at[:, pl.ds(j * wide, wide)] if j < early else w_later.at[:, pl.ds((j - early) * wide, wide)],
            sems.at[j],
        )
        for j in range(groups)
    ]
    for copy in gate_copies:
        copy.start()

    dw_bias = short_rows[0:1, :]
    norm_gain = short_rows[1:2, :]
    norm_shift = short_rows[2:3, :]
    layer_scale = short_rows[3:4, :]
    b_expand = long_rows[0:1, :]

    me = lax.axis_index("tile")
    odd = lax.rem(me, 2)
    pair_row = (1 - odd) * REACH
    next_row = odd * REACH

    for c in range(groups):
        lanes = slice(c * LANES, (c + 1) * LANES)
        for e in range(epochs):
            rim[c, e, :, 0:8, :] = jnp.zeros((2 * REACH, 8, LANES), F32)
            rim[c, e, :, 8 + width : 16 + width, :] = jnp.zeros((2 * REACH, 8, LANES), F32)
            rim[c, e, pl.ds(pair_row, REACH), 8 : 8 + width, :] = recv_pair[e, :, :, lanes].astype(F32)
            rim[c, e, pl.ds(next_row, REACH), 8 : 8 + width, :] = recv_next[e, :, :, lanes].astype(F32)

    def depthwise(index, carry):
        c = index // epochs
        e = index - c * epochs
        lanes = pl.ds(pl.multiple_of(c * LANES, LANES), LANES)
        total = [None] * (2 * REACH)
        for ox in range(7):
            factors = [dw_kernel[oy, pl.ds(ox, 1), lanes] for oy in range(7)]
            for k in range(REACH):
                above = rim[c, e, k, pl.ds(5 + ox, width), :]
                below = rim[c, e, REACH + k, pl.ds(5 + ox, width), :]
                for y in range(k + 1):
                    term = above * factors[k - y]
                    total[y] = term if total[y] is None else total[y] + term
                for y in range(k, REACH):
                    term = below * factors[6 + k - y]
                    at = REACH + y
                    total[at] = term if total[at] is None else total[at] + term
        for y in range(2 * REACH):
            edge[e, pl.ds(y * width, width), lanes] = total[y]
        return carry

    lax.fori_loop(0, groups * epochs, depthwise, 0)

    count = rows * width
    rimmed = REACH * width
    column = lax.broadcasted_iota(jnp.int32, (count, LANES), 0)
    across = lax.rem(column, width)
    line = column // width
    first = jnp.where(me == 0, 1, 0)
    last = jnp.where(me == tiles - 1, rows - 2, rows - 1)
    inside = jnp.where((line >= first) & (line <= last), 1.0, 0.0)
    for e in range(epochs):
        values = (
            jnp.concatenate(
                [
                    spread[e, :rimmed] + edge[e, :rimmed],
                    spread[e, rimmed : count - rimmed],
                    spread[e, count - rimmed :] + edge[e, rimmed:],
                ],
                axis=0,
            )
            + dw_bias
        )
        center = jnp.mean(values, axis=-1, keepdims=True)
        centred = values - center
        variance = jnp.mean(centred * centred, axis=-1, keepdims=True)
        normed = (centred * lax.rsqrt(variance + 1e-06) * norm_gain + norm_shift).astype(BF16)
        reduced = None
        for k in range(hidden // 512):
            cols = slice(k * 512, (k + 1) * 512)
            grown = jnp.dot(normed, w_expand[:, cols], preferred_element_type=F32) + b_expand[:, cols]
            part = jnp.dot(gelu(grown).astype(BF16), w_reduce[cols, :], preferred_element_type=F32)
            reduced = part if reduced is None else reduced + part
        for c in range(groups):
            lanes = slice(c * LANES, (c + 1) * LANES)
            centre = jnp.concatenate(
                [
                    rim[c, e, REACH - 1, 8 : 8 + width, :],
                    frames[e, :, :, lanes].astype(F32).reshape(pixels, LANES),
                    rim[c, e, REACH, 8 : 8 + width, :],
                ],
                axis=0,
            )
            feature = centre + layer_scale[:, lanes] * reduced[:, lanes]
            feature = (feature * inside).astype(BF16).astype(F32)
            before = jnp.where(across == 0, 0.0, pltpu.roll(feature, 1, 0))
            after = jnp.where(across == width - 1, 0.0, pltpu.roll(feature, count - 1, 0))
            for ox, shifted in enumerate((before, feature, after)):
                packed = shifted.astype(BF16)
                for oy in range(3):
                    at = (oy * 3 + ox) * channels + c * LANES
                    taps[e * pixels : (e + 1) * pixels, at : at + LANES] = packed[
                        oy * width : oy * width + pixels
                    ]

    for j in range(early):
        gate_copies[j].wait()
    cells_of(
        range(early), 0, taps, w_gates, mask, short_rows, long_rows,
        send, pooled, (decay0, inflow0, keep, block, open0, open1),
    )
    for copy in gate_copies[early:]:
        copy.wait()


def cells_of(parts, first, taps, w_gates, mask, short_rows, long_rows, send, pooled, state):
    decay0, inflow0, keep, block, open0, open1 = state
    pixels = keep.shape[0]
    wide = 4 * LANES
    quarter = LANES // 4
    lane = lax.broadcasted_iota(jnp.int32, mask.shape, 1)
    spot = lane // quarter
    within = lane - spot * quarter
    good = mask[...] > 0.5
    for j in parts:
        cols = slice((j - first) * wide, (j - first + 1) * wide)
        lanes = slice((j - first) * LANES, (j - first + 1) * LANES)
        bias = long_rows[1:2, j * wide : (j + 1) * wide]
        rate = short_rows[4:5, j * LANES : (j + 1) * LANES]
        preact = jnp.dot(taps[...], w_gates[:, cols], preferred_element_type=F32) + bias
        sorted_ = []
        for i in range(4):
            gate = lax.rem(spot - i + 4, 4)
            sorted_.append(
                jnp.take_along_axis(preact[:, i * LANES : (i + 1) * LANES], 4 * within + gate, axis=1)
            )
        gates = []
        for g in range(4):
            out = sorted_[0]
            for i in range(1, 4):
                out = jnp.where(spot == (g + i) % 4, sorted_[i], out)
            gates.append(out if g == 0 else pltpu.roll(out, LANES - g * quarter, 1))
        gate_in, gate_keep, gate_new, gate_out = gates
        decay = jnp.where(good, jnp.exp(-rate * softplus(gate_keep)), 1.0)
        inflow = jnp.where(good, sigmoid(gate_in) * jnp.tanh(gate_new), 0.0)
        opened = sigmoid(gate_out)
        d0, d1 = decay[:pixels], decay[pixels:]
        i0, i1 = inflow[:pixels], inflow[pixels:]
        decay0[:, lanes] = d0
        inflow0[:, lanes] = i0
        keep[:, lanes] = d0 * d1
        total = d1 * i0 + i1
        block[:, lanes] = total
        send[:pixels, lanes] = total.astype(BF16)
        open0[:, lanes] = opened[:pixels]
        open1[:, lanes] = opened[pixels:]
        pooled[0:1, lanes] = pool(opened[:pixels] * jnp.tanh(i0))
        pooled[1:2, lanes] = pool(opened[pixels:] * jnp.tanh(total))


def later_kernel(
    first,
    taps,
    w_gates,
    mask,
    short_rows,
    long_rows,
    pooled_early,
    send_early,
    send,
    decay0,
    inflow0,
    keep,
    block,
    open0,
    open1,
    pooled,
):
    channels = short_rows.shape[1]
    cells_of(
        range(first, channels // LANES), first, taps, w_gates, mask, short_rows, long_rows,
        send, pooled, (decay0, inflow0, keep, block, open0, open1),
    )
    pixels = keep.shape[0]
    both = jnp.concatenate([pooled_early[0:2, :], pooled[0:2, :]], axis=1)
    own = tokens_of(both, short_rows[5:6, :])
    tail = (send.shape[0] - pixels) * LANES // channels
    known = jnp.zeros((tail, channels), F32)
    write_tail(send, pixels, put_tokens(known, own, 0))


def write_tail(send, pixels, tokens):
    tail, channels = tokens.shape
    for c in range(channels // LANES):
        at = pixels + c * tail
        send[at : at + tail, :] = tokens[:, c * LANES : (c + 1) * LANES].astype(BF16)


def read_tail(arrived, pixels, channels):
    tail = (arrived.shape[0] - pixels) * LANES // channels
    parts = [
        arrived[pixels + c * tail : pixels + (c + 1) * tail, :].astype(F32)
        for c in range(channels // LANES)
    ]
    return jnp.concatenate(parts, axis=1)


def run_block(tiles, early, staged, recv_pair, recv_next, w_gates, tail):
    spread, mask, short_rows, long_rows, frames, dw_kernel, w_expand, w_reduce = staged
    epochs, height, width, channels = frames.shape
    pixels = height * width
    depth = w_gates.shape[0]
    vmem = pl.BlockSpec(memory_space=pltpu.VMEM)
    hbm = pl.BlockSpec(memory_space=pltpu.HBM)
    near = early * LANES
    far = channels - near

    def state(lanes):
        return [jax.ShapeDtypeStruct((pixels, lanes), F32)] * 6

    flops = 2 * epochs * pixels * (2 * w_expand.size + w_gates.size)
    send, pooled, *rest = pl.pallas_call(
        functools.partial(block_kernel, tiles),
        name="block",
        out_shape=[
            jax.ShapeDtypeStruct((pixels, near), BF16),
            jax.ShapeDtypeStruct((8, near), F32),
            *state(near),
            jax.ShapeDtypeStruct((epochs * pixels, depth), BF16),
            jax.ShapeDtypeStruct((depth, 4 * far), BF16),
        ],
        in_specs=[vmem] * 10 + [hbm],
        out_specs=[vmem] * 10,
        scratch_shapes=[
            pltpu.VMEM((channels // LANES, epochs, 2 * REACH, width + 16, LANES), F32),
            pltpu.VMEM((epochs, 2 * REACH * width, channels), F32),
            pltpu.VMEM((depth, 4 * near), BF16),
            pltpu.SemaphoreType.DMA((channels // LANES,)),
        ],
        compiler_params=pltpu.CompilerParams(vmem_limit_bytes=32 * 2**20),
        cost_estimate=pl.CostEstimate(flops=flops, bytes_accessed=2 * w_gates.size, transcendentals=0),
    )(
        spread,
        recv_pair,
        recv_next,
        frames,
        mask,
        short_rows,
        long_rows,
        dw_kernel,
        w_expand,
        w_reduce,
        pltpu.with_memory_space_constraint(w_gates, pltpu.HBM),
    )
    *state_near, taps, w_later = rest
    send_far, *state_far = pl.pallas_call(
        functools.partial(later_kernel, early),
        name="later",
        out_shape=[
            jax.ShapeDtypeStruct((pixels + tail * channels // LANES, far), BF16),
            *state(far),
        ],
        in_specs=[vmem] * 6 + [pl.BlockSpec(memory_space=pl.ANY)],
        out_specs=[vmem] * 7,
        scratch_shapes=[pltpu.VMEM((8, far), F32)],
        compiler_params=pltpu.CompilerParams(vmem_limit_bytes=24 * 2**20),
        cost_estimate=pl.CostEstimate(flops=10**10, bytes_accessed=0, transcendentals=0),
    )(taps, w_later, mask, short_rows, long_rows, pooled, send)
    return (send, state_near), (send_far, state_far)


def pool(memory):
    return jnp.mean(memory.astype(BF16).astype(F32), axis=0, keepdims=True)


def tokens_of(both, gain):
    center = jnp.mean(both, axis=-1, keepdims=True)
    centred = both - center
    variance = jnp.mean(centred * centred, axis=-1, keepdims=True)
    return (centred * lax.rsqrt(variance + 1e-06) * gain).astype(BF16).astype(F32)


def put_tokens(known, own, at):
    line = lax.broadcasted_iota(jnp.int32, known.shape, 0)
    return jnp.where(line == at, own[0:1], jnp.where(line == at + 1, own[1:2], known))


def step_cells(arrived, decay0, inflow0, keep, block):
    state = arrived[: keep.shape[0]].astype(F32)
    return decay0[...] * state + inflow0[...], keep[...] * state + block[...]


def relay_kernel(arrived, decay0, inflow0, keep, block, open0, open1, before, send, pooled):
    cell0, cell1 = step_cells(arrived, decay0, inflow0, keep, block)
    send[...] = cell1.astype(BF16)
    pooled[0:1, :] = pool(open0[...] * jnp.tanh(cell0))
    pooled[1:2, :] = pool(open1[...] * jnp.tanh(cell1))


def relay_later_kernel(
    stage, arrived, decay0, inflow0, keep, block, open0, open1, pooled_early, short_rows, send
):
    pixels = keep.shape[0]
    cell0, cell1 = step_cells(arrived, decay0, inflow0, keep, block)
    send[:pixels] = cell1.astype(BF16)
    pooled = jnp.concatenate(
        [pool(open0[...] * jnp.tanh(cell0)), pool(open1[...] * jnp.tanh(cell1))], axis=0
    )
    both = jnp.concatenate([pooled_early[0:2, :], pooled], axis=1)
    own = tokens_of(both, short_rows[5:6, :])
    known = read_tail(arrived, pixels, short_rows.shape[1])
    write_tail(send, pixels, put_tokens(known, own, 2 * stage))


def final_kernel(
    count,
    *refs,
):
    halves = [
        (refs[:count], refs[2 * count : 2 * count + 6]),
        (refs[count : 2 * count], refs[2 * count + 6 : 2 * count + 12]),
    ]
    short_rows, months, slope, w_qkv, w_out = refs[2 * count + 12 : 2 * count + 17]
    memory_hbm, change, memory, sems = refs[2 * count + 17 :]
    epochs, pixels, channels = memory.shape
    total = months.shape[0]
    pooled = [[], []]
    at = 0
    for arrived, (decay0, inflow0, keep, block, open0, open1) in halves:
        lanes = slice(at, at + keep.shape[1])
        at += keep.shape[1]
        state = arrived[0][:pixels].astype(F32)
        for more in arrived[1:]:
            state = state + more[:pixels].astype(F32)
        cell0 = decay0[...] * state + inflow0[...]
        cell1 = keep[...] * state + block[...]
        for e, (gate, cell) in enumerate(((open0, cell0), (open1, cell1))):
            out = (gate[...] * jnp.tanh(cell)).astype(BF16)
            memory[e, :, lanes] = out
            pooled[e].append(pool(out))
    copies = [pltpu.make_async_copy(memory.at[e], memory_hbm.at[e], sems.at[e]) for e in range(epochs)]
    for copy in copies:
        copy.start()
    known = read_tail(halves[1][0][0], pixels, channels)
    for more in halves[1][0][1:]:
        known = known + read_tail(more, pixels, channels)
    both = jnp.concatenate([jnp.concatenate(parts, axis=1) for parts in pooled], axis=0)
    own = tokens_of(both, short_rows[5:6, :])
    stage = lax.axis_index("epoch")
    tokens = put_tokens(known, own, 2 * stage).astype(BF16)
    heads = slope.shape[1]
    depth = channels // heads
    qkv = jnp.dot(tokens, w_qkv[...], preferred_element_type=F32).astype(BF16).astype(F32)[:total]
    queries = qkv[:, :channels]
    keys = qkv[:, channels : 2 * channels]
    values = qkv[:, 2 * channels :]
    line = lax.broadcasted_iota(jnp.int32, (total, channels), 0)
    member = lax.broadcasted_iota(jnp.int32, (channels, heads), 0) // depth
    head_of = jnp.where(member == lax.broadcasted_iota(jnp.int32, (channels, heads), 1), 1.0, 0.0)
    member_t = lax.broadcasted_iota(jnp.int32, (heads, channels), 1) // depth
    channel_of = jnp.where(
        member_t == lax.broadcasted_iota(jnp.int32, (heads, channels), 0), 1.0, 0.0
    )
    key_index = lax.broadcasted_iota(jnp.int32, (total, heads), 0)
    month = months[:, :heads]
    results = []
    for step in range(2):
        mine = 2 * stage + step
        query = jnp.sum(jnp.where(line == mine, queries, 0.0), axis=0, keepdims=True)
        raw = jnp.dot(query * keys, head_of, preferred_element_type=F32, precision=lax.Precision.HIGHEST)
        now = jnp.sum(jnp.where(key_index == mine, month, 0.0), axis=0, keepdims=True)
        scores = raw / math.sqrt(depth) - slope[...] * (now - month)
        scores = jnp.where(key_index <= mine, scores, -1e30)
        expo = jnp.exp(scores - jnp.max(scores, axis=0, keepdims=True))
        weights = expo / jnp.sum(expo, axis=0, keepdims=True)
        spread = jnp.dot(weights, channel_of, preferred_element_type=F32, precision=lax.Precision.HIGHEST)
        results.append(jnp.sum(spread * values, axis=0, keepdims=True))
    mixed = jnp.concatenate(results, axis=0).astype(BF16)
    change[...] = jnp.dot(mixed, w_out[...], preferred_element_type=F32).astype(BF16)
    for copy in copies:
        copy.wait()


def pairs(count, start):
    links = []
    for i in range(start, count - 1, 2):
        links += [(i, i + 1), (i + 1, i)]
    return links


def body(
    frames,
    valid,
    days,
    dw_kernel,
    dw_bias,
    norm_gain,
    norm_shift,
    w_expand,
    b_expand,
    w_reduce,
    layer_scale,
    w_gates,
    b_gates,
    forget_rate,
    attn_gain,
    w_query,
    w_key,
    w_value,
    w_out,
    head_slope,
):

    epochs, height, width, channels = frames.shape
    pixels = height * width
    tiles = lax.axis_size("tile")
    stages = lax.axis_size("epoch")
    total = epochs * stages
    tail = -(-total // 16) * 16
    even = lax.rem(lax.axis_index("tile"), 2) == 0
    top = frames[:, :REACH]
    bottom = frames[:, height - REACH :]
    recv_pair = lax.ppermute(jnp.where(even, bottom, top), "tile", pairs(tiles, 0))
    recv_next = lax.ppermute(jnp.where(even, top, bottom), "tile", pairs(tiles, 1))
    (
        spread,
        mask,
        short_rows,
        long_rows,
        months,
        slope,
        frames_near,
        dw_near,
        expand_near,
        reduce_near,
        qkv_near,
        out_near,
    ) = run_stage(
        frames,
        valid,
        days,
        dw_kernel,
        [dw_bias, norm_gain, norm_shift, layer_scale, forget_rate, attn_gain],
        [b_expand, b_gates],
        head_slope,
        w_expand,
        w_reduce,
        [w_query, w_key, w_value, w_out],
    )
    early = max(1, channels // LANES - 1)
    (send, near), (send_far, far) = run_block(
        tiles,
        early,
        (spread, mask, short_rows, long_rows, frames_near, dw_near, expand_near, reduce_near),
        recv_pair,
        recv_next,
        w_gates.reshape(9 * channels, -1),
        tail,
    )
    vmem = pl.BlockSpec(memory_space=pltpu.VMEM)
    params = pltpu.CompilerParams(vmem_limit_bytes=16 * 2**20)
    cost = pl.CostEstimate(flops=10**10, bytes_accessed=0, transcendentals=0)

    def relay(arrived, before):
        return pl.pallas_call(
            relay_kernel,
            name="relay",
            out_shape=[
                jax.ShapeDtypeStruct((pixels, early * LANES), BF16),
                jax.ShapeDtypeStruct((8, early * LANES), F32),
            ],
            in_specs=[vmem] * 7 + [pl.BlockSpec(memory_space=pl.ANY)],
            out_specs=[vmem] * 2,
            compiler_params=params,
            cost_estimate=cost,
        )(arrived, *near, before)

    def relay_later(stage, arrived, pooled):
        return pl.pallas_call(
            functools.partial(relay_later_kernel, stage),
            name="relay_later",
            out_shape=jax.ShapeDtypeStruct(send_far.shape, BF16),
            in_specs=[vmem] * 9,
            out_specs=vmem,
            compiler_params=params,
            cost_estimate=cost,
        )(arrived, *far, pooled, short_rows)

    arrived = []
    arrived_far = []
    if stages <= 8:
        for stage in range(stages - 1):
            link = [(stage, stage + 1)]
            if stage > 0:
                send, pooled = relay(arrived[-1], send_far)
                send_far = relay_later(stage, arrived_far[-1], pooled)
            arrived.append(lax.ppermute(send, "epoch", link))
            arrived_far.append(lax.ppermute(send_far, "epoch", link))
    else:
        chain = [(i, i + 1) for i in range(stages - 1)]

        def along(state, width):
            keep, block = state[2], state[3]

            def turn(_, arriving):
                out = (keep * arriving.astype(F32) + block).astype(BF16)
                return lax.ppermute(out, "epoch", chain)

            return lax.fori_loop(0, stages - 1, turn, jnp.zeros((pixels, width), BF16))

        def unfold(tokens):
            parts = jnp.split(tokens, channels // LANES, axis=1)
            return jnp.concatenate(parts, axis=0)

        incoming = along(near, early * LANES)
        incoming_far = along(far, channels - early * LANES)
        _, pooled = relay(incoming, send_far)
        blank = jnp.zeros((tail * channels // LANES, LANES), BF16)
        told = relay_later(0, jnp.concatenate([incoming_far, blank]), pooled)[pixels:]
        told = jnp.concatenate(jnp.split(told, channels // LANES, axis=0), axis=1)
        known = lax.all_gather(told[:epochs], "epoch", axis=0, tiled=True)
        known = jnp.concatenate([known, jnp.zeros((tail - total, channels), BF16)])
        arrived.append(incoming)
        arrived_far.append(jnp.concatenate([incoming_far, unfold(known)]))

    memory, change = pl.pallas_call(
        functools.partial(final_kernel, len(arrived)),
        name="final",
        out_shape=[
            jax.ShapeDtypeStruct((epochs, pixels, channels), BF16),
            jax.ShapeDtypeStruct((epochs, channels), BF16),
        ],
        in_specs=[vmem] * (2 * len(arrived) + 17),
        out_specs=[pl.BlockSpec(memory_space=pltpu.HBM), vmem],
        scratch_shapes=[
            pltpu.VMEM((epochs, pixels, channels), BF16),
            pltpu.SemaphoreType.DMA((epochs,)),
        ],
        compiler_params=pltpu.CompilerParams(vmem_limit_bytes=24 * 2**20),
    )(*arrived, *arrived_far, *near, *far, short_rows, months, slope, qkv_near, out_near)
    return (
        memory.reshape(epochs, height, width, channels),
        change.reshape(epochs, 1, 1, channels),
    )


def solution(mesh):
    placed = (
        P("epoch", ("groups", "tile"), None, None),
        P("epoch", ("groups", "tile"), None),
        P("groups"),
    ) + (P(),) * 17
    return jax.shard_map(
        body,
        mesh=mesh,
        in_specs=placed,
        out_specs=(
            P("epoch", ("groups", "tile"), None, None),
            P("epoch", ("groups", "tile"), None, None),
        ),
        check_vma=False,
    )
```

```python
import functools
import math

import jax
import jax.numpy as jnp
from jax import lax
from jax.experimental import pallas as pl
from jax.experimental.pallas import tpu as pltpu
from jax.sharding import PartitionSpec as P

PATCH = 16
REACH = 4
LANES = 128
F32 = jnp.float32
BF16 = jnp.bfloat16


def sigmoid(x):
    return 0.5 * jnp.tanh(0.5 * x) + 0.5


def softplus(x):
    return jnp.maximum(x, 0.0) + jnp.log(1.0 + jnp.exp(-jnp.abs(x)))


def gelu_twice(x):
    inner = x * (0.7978845608028654 + (0.7978845608028654 * 0.044715) * (x * x))
    return x + x * jnp.tanh(inner)


def near_kernel(*refs):
    count = len(refs) // 2 - 1
    sources, outs = refs[:count], refs[count : 2 * count]
    to_pair, to_next, sems = refs[2 * count :]
    copies = [pltpu.make_async_copy(a, b, sems.at[i]) for i, (a, b) in enumerate(zip(sources, outs))]
    for copy in copies:
        copy.start()
    copies[0].wait()
    frames = outs[0]
    bottom = frames.shape[1] - REACH
    odd = lax.rem(lax.axis_index("tile"), 2)
    to_pair[...] = frames[:, pl.ds((1 - odd) * bottom, REACH)]
    to_next[...] = frames[:, pl.ds(odd * bottom, REACH)]
    for copy in copies[1:]:
        copy.wait()


def run_near(arrays):
    frames = arrays[0]
    rim = jax.ShapeDtypeStruct((frames.shape[0], REACH) + frames.shape[2:], frames.dtype)
    hbm = pl.BlockSpec(memory_space=pltpu.HBM)
    vmem = pl.BlockSpec(memory_space=pltpu.VMEM)
    out = pl.pallas_call(
        near_kernel,
        name="near",
        out_shape=[jax.ShapeDtypeStruct(x.shape, x.dtype) for x in arrays] + [rim] * 2,
        in_specs=[hbm] * len(arrays),
        out_specs=[vmem] * (len(arrays) + 2),
        scratch_shapes=[pltpu.SemaphoreType.DMA((len(arrays),))],
        compiler_params=pltpu.CompilerParams(vmem_limit_bytes=16 * 2**20),
    )(*[pltpu.with_memory_space_constraint(x, pltpu.HBM) for x in arrays])
    return out[: len(arrays)], out[-2], out[-1]


def stage_kernel(
    frames,
    dw_kernel,
    valid,
    days,
    slope_line,
    b_expand,
    b_gates,
    dw_bias,
    norm_gain,
    norm_shift,
    layer_scale,
    forget_rate,
    attn_gain,
    w_expand_hbm,
    w_reduce_hbm,
    w_gates_hbm,
    w_query_hbm,
    w_key_hbm,
    w_value_hbm,
    w_out_hbm,
    spread,
    mask,
    short_rows,
    long_rows,
    months,
    slope,
    w_expand,
    w_reduce,
    w_first,
    w_qkv,
    w_out,
    padded,
    sems,
):
    epochs, height, width, channels = frames.shape
    groups = channels // LANES
    rows = height + 2
    pixels = height * width
    moves = [
        (w_expand_hbm, w_expand),
        (w_reduce_hbm, w_reduce),
        (w_gates_hbm.at[:, pl.ds(0, w_first.shape[1])], w_first),
        (w_query_hbm, w_qkv.at[:, pl.ds(0, channels)]),
        (w_key_hbm, w_qkv.at[:, pl.ds(channels, channels)]),
        (w_value_hbm, w_qkv.at[:, pl.ds(2 * channels, channels)]),
        (w_out_hbm, w_out),
    ]
    copies = [pltpu.make_async_copy(a, b, sems.at[i]) for i, (a, b) in enumerate(moves)]
    for copy in copies:
        copy.start()

    for c in range(groups):
        for e in range(epochs):
            lanes = slice(c * LANES, (c + 1) * LANES)
            padded[c, e, :, 0:8, :] = jnp.zeros((height, 8, LANES), F32)
            padded[c, e, :, 8 + width : 16 + width, :] = jnp.zeros((height, 8, LANES), F32)
            padded[c, e, :, 8 : 8 + width, :] = frames[e, :, :, lanes].astype(F32)

    half = rows // 2

    def depthwise(index, carry):
        c = index // epochs
        e = index - c * epochs
        lanes = pl.ds(pl.multiple_of(c * LANES, LANES), LANES)
        for part in range(2):
            total = [None] * half
            for ox in range(7):
                factors = [dw_kernel[oy, pl.ds(ox, 1), lanes] for oy in range(7)]
                for r in range(height):
                    at = [(y, r + REACH - (part * half + y)) for y in range(half)]
                    at = [(y, oy) for y, oy in at if 0 <= oy < 7]
                    if not at:
                        continue
                    window = padded[c, e, r, pl.ds(5 + ox, width), :]
                    for y, oy in at:
                        term = window * factors[oy]
                        total[y] = term if total[y] is None else total[y] + term
            for y in range(half):
                line = (part * half + y) * width
                spread[e, pl.ds(line, width), lanes] = total[y]
        return carry

    lax.fori_loop(0, groups * epochs, depthwise, 0)

    short = (dw_bias, norm_gain, norm_shift, layer_scale, forget_rate, attn_gain)
    for k, line in enumerate(short):
        short_rows[k : k + 1, :] = line[...].reshape(1, -1)
    for k, line in enumerate((b_expand, b_gates)):
        long_rows[k : k + 1, :] = line[...].reshape(1, -1)
    slope[...] = slope_line[...].reshape(1, -1)
    total = days.shape[0]
    eye = lax.broadcasted_iota(jnp.int32, (total, total), 0) == lax.broadcasted_iota(
        jnp.int32, (total, total), 1
    )
    month = days[...].astype(F32).reshape(1, -1) / 30.0
    months[...] = jnp.broadcast_to(
        jnp.sum(jnp.where(eye, month, 0.0), axis=1, keepdims=True), months.shape
    )
    down = lax.broadcasted_iota(jnp.int32, (pixels, height), 0) // width
    pick = jnp.where(down == lax.broadcasted_iota(jnp.int32, (pixels, height), 1), 1.0, 0.0).astype(BF16)
    side = lax.rem(lax.broadcasted_iota(jnp.int32, (pixels, width), 0), width)
    place = side == lax.broadcasted_iota(jnp.int32, (pixels, width), 1)
    ones = jnp.ones((width, LANES), BF16)
    for e in range(epochs):
        plane = jnp.where(valid[e] > 0, 1.0, 0.0).astype(BF16)
        lines = jnp.dot(pick, plane, preferred_element_type=F32)
        mask[e * pixels : (e + 1) * pixels, :] = jnp.dot(
            jnp.where(place, lines, 0.0).astype(BF16), ones, preferred_element_type=F32
        )
    for copy in copies:
        copy.wait()


def run_stage(near, w_expand, w_reduce, w_gates, w_qkvo):
    frames, dw_kernel, valid, days, slope = near[:5]
    epochs, height, width, channels = frames.shape
    pixels = height * width
    total = days.shape[0]
    far = [w_expand, w_reduce, w_gates, *w_qkvo]
    hbm = pl.BlockSpec(memory_space=pltpu.HBM)
    vmem = pl.BlockSpec(memory_space=pltpu.VMEM)
    out_shape = [
        jax.ShapeDtypeStruct((epochs, (height + 2) * width, channels), F32),
        jax.ShapeDtypeStruct((epochs * pixels, LANES), F32),
        jax.ShapeDtypeStruct((8, channels), F32),
        jax.ShapeDtypeStruct((8, w_gates.shape[1]), F32),
        jax.ShapeDtypeStruct((total, LANES), F32),
        jax.ShapeDtypeStruct((1, slope.size), F32),
        jax.ShapeDtypeStruct(w_expand.shape, BF16),
        jax.ShapeDtypeStruct(w_reduce.shape, BF16),
        jax.ShapeDtypeStruct((w_gates.shape[0], 4 * LANES), BF16),
        jax.ShapeDtypeStruct((channels, 3 * channels), BF16),
        jax.ShapeDtypeStruct((channels, channels), BF16),
    ]
    return pl.pallas_call(
        stage_kernel,
        name="stage",
        out_shape=out_shape,
        in_specs=[vmem] * len(near) + [hbm] * len(far),
        out_specs=[vmem] * len(out_shape),
        scratch_shapes=[
            pltpu.VMEM((channels // LANES, epochs, height, width + 16, LANES), F32),
            pltpu.SemaphoreType.DMA((len(far),)),
        ],
        compiler_params=pltpu.CompilerParams(vmem_limit_bytes=24 * 2**20),
        cost_estimate=pl.CostEstimate(
            flops=10**10, bytes_accessed=8 * w_expand.size, transcendentals=0
        ),
    )(*near, *[pltpu.with_memory_space_constraint(x, pltpu.HBM) for x in far])


def block_kernel(
    tiles,
    spread,
    recv_pair,
    recv_next,
    frames,
    mask,
    short_rows,
    long_rows,
    dw_kernel,
    w_expand,
    w_reduce,
    w_first,
    w_gates_hbm,
    send,
    pooled,
    decay0,
    inflow0,
    keep,
    block,
    open0,
    open1,
    taps,
    w_later,
    rim,
    edge,
    w_gates,
    sems,
):
    epochs, height, width, channels = frames.shape
    groups = channels // LANES
    rows = height + 2
    pixels = height * width
    wide = 4 * LANES

    early = send.shape[1] // LANES
    places = [w_gates.at[j] for j in range(early - 1)] + [w_later.at[j] for j in range(groups - early)]
    gate_copies = [
        pltpu.make_async_copy(w_gates_hbm.at[:, pl.ds((j + 1) * wide, wide)], place, sems.at[j])
        for j, place in enumerate(places)
    ]
    for copy in gate_copies:
        copy.start()

    dw_bias = short_rows[0:1, :]
    norm_gain = short_rows[1:2, :]
    norm_shift = short_rows[2:3, :]
    half_scale = 0.5 * short_rows[3:4, :]
    b_expand = long_rows[0:1, :]

    me = lax.axis_index("tile")
    odd = lax.rem(me, 2)
    pair_row = (1 - odd) * REACH
    next_row = odd * REACH

    for c in range(groups):
        lanes = slice(c * LANES, (c + 1) * LANES)
        for e in range(epochs):
            rim[c, e, :, 0:8, :] = jnp.zeros((2 * REACH, 8, LANES), F32)
            rim[c, e, :, 8 + width : 16 + width, :] = jnp.zeros((2 * REACH, 8, LANES), F32)
            rim[c, e, pl.ds(pair_row, REACH), 8 : 8 + width, :] = recv_pair[e, :, :, lanes].astype(F32)
            rim[c, e, pl.ds(next_row, REACH), 8 : 8 + width, :] = recv_next[e, :, :, lanes].astype(F32)

    def depthwise(index, carry):
        c = index // epochs
        e = index - c * epochs
        lanes = pl.ds(pl.multiple_of(c * LANES, LANES), LANES)
        total = [None] * (2 * REACH)
        for ox in range(7):
            factors = [dw_kernel[oy, pl.ds(ox, 1), lanes] for oy in range(7)]
            for k in range(REACH):
                above = rim[c, e, k, pl.ds(5 + ox, width), :]
                below = rim[c, e, REACH + k, pl.ds(5 + ox, width), :]
                for y in range(k + 1):
                    term = above * factors[k - y]
                    total[y] = term if total[y] is None else total[y] + term
                for y in range(k, REACH):
                    term = below * factors[6 + k - y]
                    at = REACH + y
                    total[at] = term if total[at] is None else total[at] + term
        for y in range(2 * REACH):
            edge[e, pl.ds(y * width, width), lanes] = total[y]
        return carry

    lax.fori_loop(0, groups * epochs, depthwise, 0)

    count = rows * width
    rimmed = REACH * width
    column = lax.broadcasted_iota(jnp.int32, (count, LANES), 0)
    across = lax.rem(column, width)
    line = column // width
    first = jnp.where(me == 0, 1, 0)
    last = jnp.where(me == tiles - 1, rows - 2, rows - 1)
    inside = jnp.where((line >= first) & (line <= last), 1.0, 0.0)
    for e in range(epochs):
        values = (
            jnp.concatenate(
                [
                    spread[e, :rimmed] + edge[e, :rimmed],
                    spread[e, rimmed : count - rimmed],
                    spread[e, count - rimmed :] + edge[e, rimmed:],
                ],
                axis=0,
            )
            + dw_bias
        )
        center = jnp.mean(values, axis=-1, keepdims=True)
        centred = values - center
        variance = jnp.mean(centred * centred, axis=-1, keepdims=True)
        normed = (centred * lax.rsqrt(variance + 1e-06) * norm_gain + norm_shift).astype(BF16)
        grown = jnp.dot(normed, w_expand[...], preferred_element_type=F32) + b_expand
        reduced = jnp.dot(gelu_twice(grown).astype(BF16), w_reduce[...], preferred_element_type=F32)
        for c in range(groups):
            lanes = slice(c * LANES, (c + 1) * LANES)
            centre = jnp.concatenate(
                [
                    rim[c, e, REACH - 1, 8 : 8 + width, :],
                    frames[e, :, :, lanes].astype(F32).reshape(pixels, LANES),
                    rim[c, e, REACH, 8 : 8 + width, :],
                ],
                axis=0,
            )
            feature = centre + half_scale[:, lanes] * reduced[:, lanes]
            feature = (feature * inside).astype(BF16).astype(F32)
            before = jnp.where(across == 0, 0.0, pltpu.roll(feature, 1, 0))
            after = jnp.where(across == width - 1, 0.0, pltpu.roll(feature, count - 1, 0))
            for ox, shifted in enumerate((before, feature, after)):
                packed = shifted.astype(BF16)
                for oy in range(3):
                    at = (oy * 3 + ox) * channels + c * LANES
                    taps[e * pixels : (e + 1) * pixels, at : at + LANES] = packed[
                        oy * width : oy * width + pixels
                    ]

    state = (decay0, inflow0, keep, block, open0, open1)
    cells_of(0, 0, taps, w_first, mask, short_rows, long_rows, send, pooled, state)
    for j in range(1, early):
        gate_copies[j - 1].wait()
        cells_of(j, j, taps, w_gates.at[j - 1], mask, short_rows, long_rows, send, pooled, state)
    for copy in gate_copies[early - 1 :]:
        copy.wait()


def gates_of(preact):
    quarter = LANES // 4
    lane = lax.broadcasted_iota(jnp.int32, (preact.shape[0], LANES), 1)
    spot = lane // quarter
    within = lane - spot * quarter
    sorted_ = []
    for i in range(4):
        gate = lax.rem(spot - i + 4, 4)
        sorted_.append(
            jnp.take_along_axis(preact[:, i * LANES : (i + 1) * LANES], 4 * within + gate, axis=1)
        )
    gates = []
    for g in range(4):
        out = sorted_[0]
        for i in range(1, 4):
            out = jnp.where(spot == (g + i) % 4, sorted_[i], out)
        gates.append(out if g == 0 else pltpu.roll(out, LANES - g * quarter, 1))
    return gates


def cells_of(j, at, taps, weights, mask, short_rows, long_rows, send, pooled, state):
    decay0, inflow0, keep, block, open0, open1 = state
    pixels = keep.shape[0]
    lanes = slice(at * LANES, (at + 1) * LANES)
    bias = long_rows[1:2, j * 4 * LANES : (j + 1) * 4 * LANES]
    rate = short_rows[4:5, j * LANES : (j + 1) * LANES]
    cell = None
    for e, opens in enumerate((open0, open1)):
        rows = slice(e * pixels, (e + 1) * pixels)
        preact = jnp.dot(taps[rows, :], weights[...], preferred_element_type=F32) + bias
        gate_in, gate_keep, gate_new, gate_out = gates_of(preact)
        good = mask[rows, :] > 0.5
        decay = jnp.where(good, jnp.exp(-rate * softplus(gate_keep)), 1.0)
        inflow = jnp.where(good, sigmoid(gate_in) * jnp.tanh(gate_new), 0.0)
        opened = sigmoid(gate_out)
        opens[:, lanes] = opened
        if e == 0:
            decay0[:, lanes] = decay
            inflow0[:, lanes] = inflow
            cell = inflow
        else:
            keep[:, lanes] = decay0[:, lanes] * decay
            cell = decay * inflow0[:, lanes] + inflow
            block[:, lanes] = cell
            send[:pixels, lanes] = cell.astype(BF16)
        pooled[e : e + 1, lanes] = pool(opened * jnp.tanh(cell))


def later_kernel(
    first,
    taps,
    w_gates,
    mask,
    short_rows,
    long_rows,
    pooled_early,
    send_early,
    send,
    decay0,
    inflow0,
    keep,
    block,
    open0,
    open1,
    pooled,
):
    channels = short_rows.shape[1]
    state = (decay0, inflow0, keep, block, open0, open1)
    for j in range(first, channels // LANES):
        at = j - first
        cells_of(j, at, taps, w_gates.at[at], mask, short_rows, long_rows, send, pooled, state)
    pixels = keep.shape[0]
    both = jnp.concatenate([pooled_early[0:2, :], pooled[0:2, :]], axis=1)
    own = tokens_of(both, short_rows[5:6, :])
    tail = (send.shape[0] - pixels) * LANES // channels
    known = jnp.zeros((tail, channels), F32)
    write_tail(send, pixels, put_tokens(known, own, 0))


def write_tail(send, pixels, tokens):
    tail, channels = tokens.shape
    for c in range(channels // LANES):
        at = pixels + c * tail
        send[at : at + tail, :] = tokens[:, c * LANES : (c + 1) * LANES].astype(BF16)


def read_tail(arrived, pixels, channels):
    tail = (arrived.shape[0] - pixels) * LANES // channels
    parts = [
        arrived[pixels + c * tail : pixels + (c + 1) * tail, :].astype(F32)
        for c in range(channels // LANES)
    ]
    return jnp.concatenate(parts, axis=1)


def run_block(tiles, early, staged, recv_pair, recv_next, w_gates, tail):
    spread, mask, short_rows, long_rows, frames, dw_kernel, w_expand, w_reduce, w_first = staged
    epochs, height, width, channels = frames.shape
    pixels = height * width
    depth = w_gates.shape[0]
    vmem = pl.BlockSpec(memory_space=pltpu.VMEM)
    hbm = pl.BlockSpec(memory_space=pltpu.HBM)
    near = early * LANES
    far = channels - near

    def state(lanes):
        return [jax.ShapeDtypeStruct((pixels, lanes), F32)] * 6

    flops = 2 * epochs * pixels * (2 * w_expand.size + w_gates.size)
    send, pooled, *rest = pl.pallas_call(
        functools.partial(block_kernel, tiles),
        name="block",
        out_shape=[
            jax.ShapeDtypeStruct((pixels, near), BF16),
            jax.ShapeDtypeStruct((8, near), F32),
            *state(near),
            jax.ShapeDtypeStruct((epochs * pixels, depth), BF16),
            jax.ShapeDtypeStruct((far // LANES, depth, 4 * LANES), BF16),
        ],
        in_specs=[vmem] * 11 + [hbm],
        out_specs=[vmem] * 10,
        scratch_shapes=[
            pltpu.VMEM((channels // LANES, epochs, 2 * REACH, width + 16, LANES), F32),
            pltpu.VMEM((epochs, 2 * REACH * width, channels), F32),
            pltpu.VMEM((max(1, early - 1), depth, 4 * LANES), BF16),
            pltpu.SemaphoreType.DMA((channels // LANES - 1,)),
        ],
        compiler_params=pltpu.CompilerParams(vmem_limit_bytes=32 * 2**20),
        cost_estimate=pl.CostEstimate(flops=flops, bytes_accessed=2 * w_gates.size, transcendentals=0),
    )(
        spread,
        recv_pair,
        recv_next,
        frames,
        mask,
        short_rows,
        long_rows,
        dw_kernel,
        w_expand,
        w_reduce,
        w_first,
        pltpu.with_memory_space_constraint(w_gates, pltpu.HBM),
    )
    *state_near, taps, w_later = rest
    send_far, *state_far = pl.pallas_call(
        functools.partial(later_kernel, early),
        name="later",
        out_shape=[
            jax.ShapeDtypeStruct((pixels + tail * channels // LANES, far), BF16),
            *state(far),
        ],
        in_specs=[vmem] * 6 + [pl.BlockSpec(memory_space=pl.ANY)],
        out_specs=[vmem] * 7,
        scratch_shapes=[pltpu.VMEM((8, far), F32)],
        compiler_params=pltpu.CompilerParams(vmem_limit_bytes=24 * 2**20),
        cost_estimate=pl.CostEstimate(flops=10**10, bytes_accessed=0, transcendentals=0),
    )(taps, w_later, mask, short_rows, long_rows, pooled, send)
    return (send, state_near), (send_far, state_far)


def pool(memory):
    return jnp.mean(memory.astype(BF16).astype(F32), axis=0, keepdims=True)


def tokens_of(both, gain):
    center = jnp.mean(both, axis=-1, keepdims=True)
    centred = both - center
    variance = jnp.mean(centred * centred, axis=-1, keepdims=True)
    return (centred * lax.rsqrt(variance + 1e-06) * gain).astype(BF16).astype(F32)


def put_tokens(known, own, at):
    line = lax.broadcasted_iota(jnp.int32, known.shape, 0)
    return jnp.where(line == at, own[0:1], jnp.where(line == at + 1, own[1:2], known))


def step_cells(arrived, decay0, inflow0, keep, block):
    state = arrived[: keep.shape[0]].astype(F32)
    return decay0[...] * state + inflow0[...], keep[...] * state + block[...]


def relay_kernel(arrived, decay0, inflow0, keep, block, open0, open1, before, send, pooled):
    cell0, cell1 = step_cells(arrived, decay0, inflow0, keep, block)
    send[...] = cell1.astype(BF16)
    pooled[0:1, :] = pool(open0[...] * jnp.tanh(cell0))
    pooled[1:2, :] = pool(open1[...] * jnp.tanh(cell1))


def relay_later_kernel(
    stage, arrived, decay0, inflow0, keep, block, open0, open1, pooled_early, short_rows, send
):
    pixels = keep.shape[0]
    cell0, cell1 = step_cells(arrived, decay0, inflow0, keep, block)
    send[:pixels] = cell1.astype(BF16)
    pooled = jnp.concatenate(
        [pool(open0[...] * jnp.tanh(cell0)), pool(open1[...] * jnp.tanh(cell1))], axis=0
    )
    both = jnp.concatenate([pooled_early[0:2, :], pooled], axis=1)
    own = tokens_of(both, short_rows[5:6, :])
    known = read_tail(arrived, pixels, short_rows.shape[1])
    write_tail(send, pixels, put_tokens(known, own, 2 * stage))


def final_kernel(
    count,
    *refs,
):
    halves = [
        (refs[:count], refs[2 * count : 2 * count + 6]),
        (refs[count : 2 * count], refs[2 * count + 6 : 2 * count + 12]),
    ]
    short_rows, months, slope, w_qkv, w_out = refs[2 * count + 12 : 2 * count + 17]
    memory_hbm, change, memory, sems = refs[2 * count + 17 :]
    epochs, pixels, channels = memory.shape
    total = months.shape[0]
    pooled = [[], []]
    at = 0
    for arrived, (decay0, inflow0, keep, block, open0, open1) in halves:
        lanes = slice(at, at + keep.shape[1])
        at += keep.shape[1]
        state = arrived[0][:pixels].astype(F32)
        for more in arrived[1:]:
            state = state + more[:pixels].astype(F32)
        cell0 = decay0[...] * state + inflow0[...]
        cell1 = keep[...] * state + block[...]
        for e, (gate, cell) in enumerate(((open0, cell0), (open1, cell1))):
            out = (gate[...] * jnp.tanh(cell)).astype(BF16)
            memory[e, :, lanes] = out
            pooled[e].append(pool(out))
    copies = [pltpu.make_async_copy(memory.at[e], memory_hbm.at[e], sems.at[e]) for e in range(epochs)]
    for copy in copies:
        copy.start()
    known = read_tail(halves[1][0][0], pixels, channels)
    for more in halves[1][0][1:]:
        known = known + read_tail(more, pixels, channels)
    both = jnp.concatenate([jnp.concatenate(parts, axis=1) for parts in pooled], axis=0)
    own = tokens_of(both, short_rows[5:6, :])
    stage = lax.axis_index("epoch")
    tokens = put_tokens(known, own, 2 * stage).astype(BF16)
    heads = slope.shape[1]
    depth = channels // heads
    qkv = jnp.dot(tokens, w_qkv[...], preferred_element_type=F32).astype(BF16).astype(F32)[:total]
    queries = qkv[:, :channels]
    keys = qkv[:, channels : 2 * channels]
    values = qkv[:, 2 * channels :]
    member = lax.broadcasted_iota(jnp.int32, (channels, heads), 0) // depth
    head_of = jnp.where(member == lax.broadcasted_iota(jnp.int32, (channels, heads), 1), 1.0, 0.0)
    member_t = lax.broadcasted_iota(jnp.int32, (heads, channels), 1) // depth
    channel_of = jnp.where(
        member_t == lax.broadcasted_iota(jnp.int32, (heads, channels), 0), 1.0, 0.0
    )

    def exact_dot(x, zero_one):
        high = x.astype(BF16)
        rest = x - high.astype(F32)
        low = rest.astype(BF16)
        least = (rest - low.astype(F32)).astype(BF16)
        out = jnp.dot(
            jnp.concatenate([high, low, least], axis=0), zero_one.astype(BF16), preferred_element_type=F32
        )
        count = x.shape[0]
        return out[:count] + out[count : 2 * count] + out[2 * count :]

    line = lax.broadcasted_iota(jnp.int32, (total, channels), 0)
    key_index = lax.broadcasted_iota(jnp.int32, (total, heads), 0)
    month = months[:, :heads]
    places = [epochs * stage + step for step in range(epochs)]
    products = []
    for mine in places:
        query = jnp.sum(jnp.where(line == mine, queries, 0.0), axis=0, keepdims=True)
        products.append(query * keys)
    raw = exact_dot(jnp.concatenate(products, axis=0), head_of)
    weights = []
    for step, mine in enumerate(places):
        now = jnp.sum(jnp.where(key_index == mine, month, 0.0), axis=0, keepdims=True)
        scores = raw[step * total : (step + 1) * total] / math.sqrt(depth) - slope[...] * (now - month)
        scores = jnp.where(key_index <= mine, scores, -1e30)
        expo = jnp.exp(scores - jnp.max(scores, axis=0, keepdims=True))
        weights.append(expo / jnp.sum(expo, axis=0, keepdims=True))
    wide = exact_dot(jnp.concatenate(weights, axis=0), channel_of)
    results = [
        jnp.sum(wide[step * total : (step + 1) * total] * values, axis=0, keepdims=True)
        for step in range(epochs)
    ]
    mixed = jnp.concatenate(results, axis=0).astype(BF16)
    change[...] = jnp.dot(mixed, w_out[...], preferred_element_type=F32).astype(BF16)
    for copy in copies:
        copy.wait()


def pairs(count, start):
    links = []
    for i in range(start, count - 1, 2):
        links += [(i, i + 1), (i + 1, i)]
    return links


def body(
    frames,
    valid,
    days,
    dw_kernel,
    dw_bias,
    norm_gain,
    norm_shift,
    w_expand,
    b_expand,
    w_reduce,
    layer_scale,
    w_gates,
    b_gates,
    forget_rate,
    attn_gain,
    w_query,
    w_key,
    w_value,
    w_out,
    head_slope,
):

    epochs, height, width, channels = frames.shape
    pixels = height * width
    tiles = lax.axis_size("tile")
    stages = lax.axis_size("epoch")
    total = epochs * stages
    tail = -(-total // 16) * 16
    gate_weights = w_gates.reshape(9 * channels, -1)
    near, to_pair, to_next = run_near(
        [
            frames,
            dw_kernel,
            valid,
            days,
            head_slope,
            b_expand,
            b_gates,
            dw_bias,
            norm_gain,
            norm_shift,
            layer_scale,
            forget_rate,
            attn_gain,
        ]
    )
    recv_pair = lax.ppermute(to_pair, "tile", pairs(tiles, 0))
    recv_next = lax.ppermute(to_next, "tile", pairs(tiles, 1))
    (
        spread,
        mask,
        short_rows,
        long_rows,
        months,
        slope,
        expand_near,
        reduce_near,
        w_first,
        qkv_near,
        out_near,
    ) = run_stage(near, w_expand, w_reduce, gate_weights, [w_query, w_key, w_value, w_out])
    early = max(1, channels // LANES - 1)
    (send, state_near), (send_far, state_far) = run_block(
        tiles,
        early,
        (
            spread,
            mask,
            short_rows,
            long_rows,
            near[0],
            near[1],
            expand_near,
            reduce_near,
            w_first,
        ),
        recv_pair,
        recv_next,
        gate_weights,
        tail,
    )
    vmem = pl.BlockSpec(memory_space=pltpu.VMEM)
    params = pltpu.CompilerParams(vmem_limit_bytes=16 * 2**20)
    cost = pl.CostEstimate(flops=10**10, bytes_accessed=0, transcendentals=0)

    def relay(arrived, before):
        return pl.pallas_call(
            relay_kernel,
            name="relay",
            out_shape=[
                jax.ShapeDtypeStruct((pixels, early * LANES), BF16),
                jax.ShapeDtypeStruct((8, early * LANES), F32),
            ],
            in_specs=[vmem] * 7 + [pl.BlockSpec(memory_space=pl.ANY)],
            out_specs=[vmem] * 2,
            compiler_params=params,
            cost_estimate=cost,
        )(arrived, *state_near, before)

    def relay_later(stage, arrived, pooled):
        return pl.pallas_call(
            functools.partial(relay_later_kernel, stage),
            name="relay_later",
            out_shape=jax.ShapeDtypeStruct(send_far.shape, BF16),
            in_specs=[vmem] * 9,
            out_specs=vmem,
            compiler_params=params,
            cost_estimate=cost,
        )(arrived, *state_far, pooled, short_rows)

    arrived = []
    arrived_far = []
    if stages <= 8:
        for stage in range(stages - 1):
            link = [(stage, stage + 1)]
            if stage > 0:
                send, pooled = relay(arrived[-1], send_far)
                send_far = relay_later(stage, arrived_far[-1], pooled)
            arrived.append(lax.ppermute(send, "epoch", link))
            arrived_far.append(lax.ppermute(send_far, "epoch", link))
    else:
        chain = [(i, i + 1) for i in range(stages - 1)]

        def along(state, width):
            keep, block = state[2], state[3]

            def turn(_, arriving):
                out = (keep * arriving.astype(F32) + block).astype(BF16)
                return lax.ppermute(out, "epoch", chain)

            return lax.fori_loop(0, stages - 1, turn, jnp.zeros((pixels, width), BF16))

        def unfold(tokens):
            parts = jnp.split(tokens, channels // LANES, axis=1)
            return jnp.concatenate(parts, axis=0)

        incoming = along(state_near, early * LANES)
        incoming_far = along(state_far, channels - early * LANES)
        _, pooled = relay(incoming, send_far)
        blank = jnp.zeros((tail * channels // LANES, LANES), BF16)
        told = relay_later(0, jnp.concatenate([incoming_far, blank]), pooled)[pixels:]
        told = jnp.concatenate(jnp.split(told, channels // LANES, axis=0), axis=1)
        known = lax.all_gather(told[:epochs], "epoch", axis=0, tiled=True)
        known = jnp.concatenate([known, jnp.zeros((tail - total, channels), BF16)])
        arrived.append(incoming)
        arrived_far.append(jnp.concatenate([incoming_far, unfold(known)]))

    memory, change = pl.pallas_call(
        functools.partial(final_kernel, len(arrived)),
        name="final",
        out_shape=[
            jax.ShapeDtypeStruct((epochs, pixels, channels), BF16),
            jax.ShapeDtypeStruct((epochs, channels), BF16),
        ],
        in_specs=[vmem] * (2 * len(arrived) + 17),
        out_specs=[pl.BlockSpec(memory_space=pltpu.HBM), vmem],
        scratch_shapes=[
            pltpu.VMEM((epochs, pixels, channels), BF16),
            pltpu.SemaphoreType.DMA((epochs,)),
        ],
        compiler_params=pltpu.CompilerParams(vmem_limit_bytes=24 * 2**20),
    )(*arrived, *arrived_far, *state_near, *state_far, short_rows, months, slope, qkv_near, out_near)
    return (
        memory.reshape(epochs, height, width, channels),
        change.reshape(epochs, 1, 1, channels),
    )


def solution(mesh):
    placed = (
        P("epoch", ("groups", "tile"), None, None),
        P("epoch", ("groups", "tile"), None),
        P("groups"),
    ) + (P(),) * 17
    return jax.shard_map(
        body,
        mesh=mesh,
        in_specs=placed,
        out_specs=(
            P("epoch", ("groups", "tile"), None, None),
            P("epoch", ("groups", "tile"), None, None),
        ),
        check_vma=False,
    )
```

```python
import functools
import math

import jax
import jax.numpy as jnp
from jax import lax
from jax.experimental import pallas as pl
from jax.experimental.pallas import tpu as pltpu
from jax.sharding import PartitionSpec as P

PATCH = 16
REACH = 4
LANES = 128
F32 = jnp.float32
BF16 = jnp.bfloat16


def sigmoid(x):
    return 0.5 * jnp.tanh(0.5 * x) + 0.5


def softplus(x):
    return jnp.maximum(x, 0.0) + jnp.log(1.0 + jnp.exp(-jnp.abs(x)))


def gelu_twice(x):
    inner = x * (0.7978845608028654 + (0.7978845608028654 * 0.044715) * (x * x))
    return x + x * jnp.tanh(inner)


def near_kernel(*refs):
    count = len(refs) // 2 - 1
    sources, outs = refs[:count], refs[count : 2 * count]
    to_pair, to_next, sems = refs[2 * count :]
    copies = [pltpu.make_async_copy(a, b, sems.at[i]) for i, (a, b) in enumerate(zip(sources, outs))]
    for copy in copies:
        copy.start()
    copies[0].wait()
    frames = outs[0]
    bottom = frames.shape[1] - REACH
    odd = lax.rem(lax.axis_index("tile"), 2)
    to_pair[...] = frames[:, pl.ds((1 - odd) * bottom, REACH)]
    to_next[...] = frames[:, pl.ds(odd * bottom, REACH)]
    for copy in copies[1:]:
        copy.wait()


def run_near(arrays):
    frames = arrays[0]
    rim = jax.ShapeDtypeStruct((frames.shape[0], REACH) + frames.shape[2:], frames.dtype)
    hbm = pl.BlockSpec(memory_space=pltpu.HBM)
    vmem = pl.BlockSpec(memory_space=pltpu.VMEM)
    out = pl.pallas_call(
        near_kernel,
        name="near",
        out_shape=[jax.ShapeDtypeStruct(x.shape, x.dtype) for x in arrays] + [rim] * 2,
        in_specs=[hbm] * len(arrays),
        out_specs=[vmem] * (len(arrays) + 2),
        scratch_shapes=[pltpu.SemaphoreType.DMA((len(arrays),))],
        compiler_params=pltpu.CompilerParams(vmem_limit_bytes=16 * 2**20),
    )(*[pltpu.with_memory_space_constraint(x, pltpu.HBM) for x in arrays])
    return out[: len(arrays)], out[-2], out[-1]


def stage_kernel(
    frames,
    dw_kernel,
    valid,
    days,
    slope_line,
    b_expand,
    b_gates,
    dw_bias,
    norm_gain,
    norm_shift,
    layer_scale,
    forget_rate,
    attn_gain,
    w_expand_hbm,
    w_reduce_hbm,
    w_gates_hbm,
    w_query_hbm,
    w_key_hbm,
    w_value_hbm,
    w_out_hbm,
    spread,
    mask,
    short_rows,
    long_rows,
    months,
    slope,
    w_expand,
    w_reduce,
    w_first,
    w_qkv,
    w_out,
    padded,
    sems,
):
    epochs, height, width, channels = frames.shape
    groups = channels // LANES
    rows = height + 2
    pixels = height * width
    moves = [
        (w_expand_hbm, w_expand),
        (w_reduce_hbm, w_reduce),
        (w_gates_hbm.at[:, pl.ds(0, w_first.shape[1])], w_first),
        (w_query_hbm, w_qkv.at[:, pl.ds(0, channels)]),
        (w_key_hbm, w_qkv.at[:, pl.ds(channels, channels)]),
        (w_value_hbm, w_qkv.at[:, pl.ds(2 * channels, channels)]),
        (w_out_hbm, w_out),
    ]
    copies = [pltpu.make_async_copy(a, b, sems.at[i]) for i, (a, b) in enumerate(moves)]
    for copy in copies:
        copy.start()

    for c in range(groups):
        for e in range(epochs):
            lanes = slice(c * LANES, (c + 1) * LANES)
            padded[c, e, :, 0:8, :] = jnp.zeros((height, 8, LANES), F32)
            padded[c, e, :, 8 + width : 16 + width, :] = jnp.zeros((height, 8, LANES), F32)
            padded[c, e, :, 8 : 8 + width, :] = frames[e, :, :, lanes].astype(F32)

    half = rows // 2

    def depthwise(index, carry):
        c = index // epochs
        e = index - c * epochs
        lanes = pl.ds(pl.multiple_of(c * LANES, LANES), LANES)
        for part in range(2):
            total = [None] * half
            for ox in range(7):
                factors = [dw_kernel[oy, pl.ds(ox, 1), lanes] for oy in range(7)]
                for r in range(height):
                    at = [(y, r + REACH - (part * half + y)) for y in range(half)]
                    at = [(y, oy) for y, oy in at if 0 <= oy < 7]
                    if not at:
                        continue
                    window = padded[c, e, r, pl.ds(5 + ox, width), :]
                    for y, oy in at:
                        term = window * factors[oy]
                        total[y] = term if total[y] is None else total[y] + term
            for y in range(half):
                line = (part * half + y) * width
                spread[e, pl.ds(line, width), lanes] = total[y]
        return carry

    lax.fori_loop(0, groups * epochs, depthwise, 0)

    short = (dw_bias, norm_gain, norm_shift, layer_scale, forget_rate, attn_gain)
    for k, line in enumerate(short):
        short_rows[k : k + 1, :] = line[...].reshape(1, -1)
    for k, line in enumerate((b_expand, b_gates)):
        long_rows[k : k + 1, :] = line[...].reshape(1, -1)
    slope[...] = slope_line[...].reshape(1, -1)
    total = days.shape[0]
    eye = lax.broadcasted_iota(jnp.int32, (total, total), 0) == lax.broadcasted_iota(
        jnp.int32, (total, total), 1
    )
    month = days[...].astype(F32).reshape(1, -1) / 30.0
    months[...] = jnp.broadcast_to(
        jnp.sum(jnp.where(eye, month, 0.0), axis=1, keepdims=True), months.shape
    )
    down = lax.broadcasted_iota(jnp.int32, (pixels, height), 0) // width
    pick = jnp.where(down == lax.broadcasted_iota(jnp.int32, (pixels, height), 1), 1.0, 0.0).astype(BF16)
    side = lax.rem(lax.broadcasted_iota(jnp.int32, (pixels, width), 0), width)
    place = side == lax.broadcasted_iota(jnp.int32, (pixels, width), 1)
    ones = jnp.ones((width, LANES), BF16)
    for e in range(epochs):
        plane = jnp.where(valid[e] > 0, 1.0, 0.0).astype(BF16)
        lines = jnp.dot(pick, plane, preferred_element_type=F32)
        mask[e * pixels : (e + 1) * pixels, :] = jnp.dot(
            jnp.where(place, lines, 0.0).astype(BF16), ones, preferred_element_type=F32
        )
    for copy in copies:
        copy.wait()


def run_stage(near, w_expand, w_reduce, w_gates, w_qkvo):
    frames, dw_kernel, valid, days, slope = near[:5]
    epochs, height, width, channels = frames.shape
    pixels = height * width
    total = days.shape[0]
    far = [w_expand, w_reduce, w_gates, *w_qkvo]
    hbm = pl.BlockSpec(memory_space=pltpu.HBM)
    vmem = pl.BlockSpec(memory_space=pltpu.VMEM)
    out_shape = [
        jax.ShapeDtypeStruct((epochs, (height + 2) * width, channels), F32),
        jax.ShapeDtypeStruct((epochs * pixels, LANES), F32),
        jax.ShapeDtypeStruct((8, channels), F32),
        jax.ShapeDtypeStruct((8, w_gates.shape[1]), F32),
        jax.ShapeDtypeStruct((total, LANES), F32),
        jax.ShapeDtypeStruct((1, slope.size), F32),
        jax.ShapeDtypeStruct(w_expand.shape, BF16),
        jax.ShapeDtypeStruct(w_reduce.shape, BF16),
        jax.ShapeDtypeStruct((w_gates.shape[0], 4 * LANES), BF16),
        jax.ShapeDtypeStruct((channels, 3 * channels), BF16),
        jax.ShapeDtypeStruct((channels, channels), BF16),
    ]
    return pl.pallas_call(
        stage_kernel,
        name="stage",
        out_shape=out_shape,
        in_specs=[vmem] * len(near) + [hbm] * len(far),
        out_specs=[vmem] * len(out_shape),
        scratch_shapes=[
            pltpu.VMEM((channels // LANES, epochs, height, width + 16, LANES), F32),
            pltpu.SemaphoreType.DMA((len(far),)),
        ],
        compiler_params=pltpu.CompilerParams(vmem_limit_bytes=24 * 2**20),
        cost_estimate=pl.CostEstimate(
            flops=10**10, bytes_accessed=8 * w_expand.size, transcendentals=0
        ),
    )(*near, *[pltpu.with_memory_space_constraint(x, pltpu.HBM) for x in far])


FIRST, REST, ALL = 0, 1, 2


def on_devices(turn, work):
    if turn == ALL:
        work()
    else:
        mine = (lax.axis_index("epoch") == 0) == (turn == FIRST)
        pl.when(mine)(work)


def block_kernel(tiles, turn, count, *refs):
    ins = refs[:12]
    outs = refs[count:]
    on_devices(turn, lambda: block_work(tiles, *ins, *outs))


def block_work(
    tiles,
    spread,
    recv_pair,
    recv_next,
    frames,
    mask,
    short_rows,
    long_rows,
    dw_kernel,
    w_expand,
    w_reduce,
    w_first,
    w_gates_hbm,
    send,
    pooled,
    decay0,
    inflow0,
    keep,
    block,
    open0,
    open1,
    taps,
    w_later,
    rim,
    edge,
    w_gates,
    sems,
):
    epochs, height, width, channels = frames.shape
    groups = channels // LANES
    rows = height + 2
    pixels = height * width
    wide = 4 * LANES

    early = send.shape[1] // LANES
    places = [w_gates.at[j] for j in range(early - 1)] + [w_later.at[j] for j in range(groups - early)]
    gate_copies = [
        pltpu.make_async_copy(w_gates_hbm.at[:, pl.ds((j + 1) * wide, wide)], place, sems.at[j])
        for j, place in enumerate(places)
    ]
    for copy in gate_copies:
        copy.start()

    dw_bias = short_rows[0:1, :]
    norm_gain = short_rows[1:2, :]
    norm_shift = short_rows[2:3, :]
    half_scale = 0.5 * short_rows[3:4, :]
    b_expand = long_rows[0:1, :]

    me = lax.axis_index("tile")
    odd = lax.rem(me, 2)
    pair_row = (1 - odd) * REACH
    next_row = odd * REACH

    for c in range(groups):
        lanes = slice(c * LANES, (c + 1) * LANES)
        for e in range(epochs):
            rim[c, e, :, 0:8, :] = jnp.zeros((2 * REACH, 8, LANES), F32)
            rim[c, e, :, 8 + width : 16 + width, :] = jnp.zeros((2 * REACH, 8, LANES), F32)
            rim[c, e, pl.ds(pair_row, REACH), 8 : 8 + width, :] = recv_pair[e, :, :, lanes].astype(F32)
            rim[c, e, pl.ds(next_row, REACH), 8 : 8 + width, :] = recv_next[e, :, :, lanes].astype(F32)

    def depthwise(index, carry):
        c = index // epochs
        e = index - c * epochs
        lanes = pl.ds(pl.multiple_of(c * LANES, LANES), LANES)
        total = [None] * (2 * REACH)
        for ox in range(7):
            factors = [dw_kernel[oy, pl.ds(ox, 1), lanes] for oy in range(7)]
            for k in range(REACH):
                above = rim[c, e, k, pl.ds(5 + ox, width), :]
                below = rim[c, e, REACH + k, pl.ds(5 + ox, width), :]
                for y in range(k + 1):
                    term = above * factors[k - y]
                    total[y] = term if total[y] is None else total[y] + term
                for y in range(k, REACH):
                    term = below * factors[6 + k - y]
                    at = REACH + y
                    total[at] = term if total[at] is None else total[at] + term
        for y in range(2 * REACH):
            edge[e, pl.ds(y * width, width), lanes] = total[y]
        return carry

    lax.fori_loop(0, groups * epochs, depthwise, 0)

    count = rows * width
    rimmed = REACH * width
    column = lax.broadcasted_iota(jnp.int32, (count, LANES), 0)
    across = lax.rem(column, width)
    line = column // width
    first = jnp.where(me == 0, 1, 0)
    last = jnp.where(me == tiles - 1, rows - 2, rows - 1)
    inside = jnp.where((line >= first) & (line <= last), 1.0, 0.0)
    for e in range(epochs):
        values = (
            jnp.concatenate(
                [
                    spread[e, :rimmed] + edge[e, :rimmed],
                    spread[e, rimmed : count - rimmed],
                    spread[e, count - rimmed :] + edge[e, rimmed:],
                ],
                axis=0,
            )
            + dw_bias
        )
        center = jnp.mean(values, axis=-1, keepdims=True)
        centred = values - center
        variance = jnp.mean(centred * centred, axis=-1, keepdims=True)
        normed = (centred * lax.rsqrt(variance + 1e-06) * norm_gain + norm_shift).astype(BF16)
        grown = jnp.dot(normed, w_expand[...], preferred_element_type=F32) + b_expand
        reduced = jnp.dot(gelu_twice(grown).astype(BF16), w_reduce[...], preferred_element_type=F32)
        for c in range(groups):
            lanes = slice(c * LANES, (c + 1) * LANES)
            centre = jnp.concatenate(
                [
                    rim[c, e, REACH - 1, 8 : 8 + width, :],
                    frames[e, :, :, lanes].astype(F32).reshape(pixels, LANES),
                    rim[c, e, REACH, 8 : 8 + width, :],
                ],
                axis=0,
            )
            feature = centre + half_scale[:, lanes] * reduced[:, lanes]
            feature = (feature * inside).astype(BF16).astype(F32)
            before = jnp.where(across == 0, 0.0, pltpu.roll(feature, 1, 0))
            after = jnp.where(across == width - 1, 0.0, pltpu.roll(feature, count - 1, 0))
            for ox, shifted in enumerate((before, feature, after)):
                packed = shifted.astype(BF16)
                for oy in range(3):
                    at = (oy * 3 + ox) * channels + c * LANES
                    taps[e * pixels : (e + 1) * pixels, at : at + LANES] = packed[
                        oy * width : oy * width + pixels
                    ]

    state = (decay0, inflow0, keep, block, open0, open1)
    cells_of(0, 0, taps, w_first, mask, short_rows, long_rows, send, pooled, state)
    for j in range(1, early):
        gate_copies[j - 1].wait()
        cells_of(j, j, taps, w_gates.at[j - 1], mask, short_rows, long_rows, send, pooled, state)
    for copy in gate_copies[early - 1 :]:
        copy.wait()


def gates_of(preact):
    quarter = LANES // 4
    lane = lax.broadcasted_iota(jnp.int32, (preact.shape[0], LANES), 1)
    spot = lane // quarter
    within = lane - spot * quarter
    sorted_ = []
    for i in range(4):
        gate = lax.rem(spot - i + 4, 4)
        sorted_.append(
            jnp.take_along_axis(preact[:, i * LANES : (i + 1) * LANES], 4 * within + gate, axis=1)
        )
    gates = []
    for g in range(4):
        out = sorted_[0]
        for i in range(1, 4):
            out = jnp.where(spot == (g + i) % 4, sorted_[i], out)
        gates.append(out if g == 0 else pltpu.roll(out, LANES - g * quarter, 1))
    return gates


def cells_of(j, at, taps, weights, mask, short_rows, long_rows, send, pooled, state):
    decay0, inflow0, keep, block, open0, open1 = state
    pixels = keep.shape[0]
    lanes = slice(at * LANES, (at + 1) * LANES)
    bias = long_rows[1:2, j * 4 * LANES : (j + 1) * 4 * LANES]
    rate = short_rows[4:5, j * LANES : (j + 1) * LANES]
    cell = None
    for e, opens in enumerate((open0, open1)):
        rows = slice(e * pixels, (e + 1) * pixels)
        preact = jnp.dot(taps[rows, :], weights[...], preferred_element_type=F32) + bias
        gate_in, gate_keep, gate_new, gate_out = gates_of(preact)
        good = mask[rows, :] > 0.5
        decay = jnp.where(good, jnp.exp(-rate * softplus(gate_keep)), 1.0)
        inflow = jnp.where(good, sigmoid(gate_in) * jnp.tanh(gate_new), 0.0)
        opened = sigmoid(gate_out)
        opens[:, lanes] = opened
        if e == 0:
            decay0[:, lanes] = decay
            inflow0[:, lanes] = inflow
            cell = inflow
        else:
            keep[:, lanes] = decay0[:, lanes] * decay
            cell = decay * inflow0[:, lanes] + inflow
            block[:, lanes] = cell
            send[:pixels, lanes] = cell.astype(BF16)
        pooled[e : e + 1, lanes] = pool(opened * jnp.tanh(cell))


def later_kernel(first, turn, count, *refs):
    on_devices(turn, lambda: later_work(first, *refs[:7], *refs[count:]))


def later_work(
    first,
    taps,
    w_gates,
    mask,
    short_rows,
    long_rows,
    pooled_early,
    send_early,
    send,
    decay0,
    inflow0,
    keep,
    block,
    open0,
    open1,
    pooled,
):
    channels = short_rows.shape[1]
    state = (decay0, inflow0, keep, block, open0, open1)
    for j in range(first, channels // LANES):
        at = j - first
        cells_of(j, at, taps, w_gates.at[at], mask, short_rows, long_rows, send, pooled, state)
    pixels = keep.shape[0]
    both = jnp.concatenate([pooled_early[0:2, :], pooled[0:2, :]], axis=1)
    own = tokens_of(both, short_rows[5:6, :])
    tail = (send.shape[0] - pixels) * LANES // channels
    known = jnp.zeros((tail, channels), F32)
    write_tail(send, pixels, put_tokens(known, own, 0))


def write_tail(send, pixels, tokens):
    tail, channels = tokens.shape
    for c in range(channels // LANES):
        at = pixels + c * tail
        send[at : at + tail, :] = tokens[:, c * LANES : (c + 1) * LANES].astype(BF16)


def read_tail(arrived, pixels, channels):
    tail = (arrived.shape[0] - pixels) * LANES // channels
    parts = [
        arrived[pixels + c * tail : pixels + (c + 1) * tail, :].astype(F32)
        for c in range(channels // LANES)
    ]
    return jnp.concatenate(parts, axis=1)


def run_block(tiles, early, turn, staged, recv_pair, recv_next, w_gates, tail, before):
    spread, mask, short_rows, long_rows, frames, dw_kernel, w_expand, w_reduce, w_first = staged
    epochs, height, width, channels = frames.shape
    pixels = height * width
    depth = w_gates.shape[0]
    vmem = pl.BlockSpec(memory_space=pltpu.VMEM)
    hbm = pl.BlockSpec(memory_space=pltpu.HBM)
    anywhere = pl.BlockSpec(memory_space=pl.ANY)
    near = early * LANES
    far = channels - near

    def state(lanes):
        return [jax.ShapeDtypeStruct((pixels, lanes), F32)] * 6

    kept = [] if before is None else [*before[0][1], before[1][0]]
    flops = 2 * epochs * pixels * (2 * w_expand.size + w_gates.size)
    send, pooled, *rest = pl.pallas_call(
        functools.partial(block_kernel, tiles, turn, 12 + len(kept)),
        name="block",
        out_shape=[
            jax.ShapeDtypeStruct((pixels, near), BF16),
            jax.ShapeDtypeStruct((8, near), F32),
            *state(near),
            jax.ShapeDtypeStruct((epochs * pixels, depth), BF16),
            jax.ShapeDtypeStruct((far // LANES, depth, 4 * LANES), BF16),
        ],
        in_specs=[vmem] * 11 + [hbm] + [vmem] * (len(kept) - 1) + [anywhere] * min(1, len(kept)),
        out_specs=[vmem] * 10,
        input_output_aliases={12 + k: 2 + k for k in range(len(kept) - 1)},
        scratch_shapes=[
            pltpu.VMEM((channels // LANES, epochs, 2 * REACH, width + 16, LANES), F32),
            pltpu.VMEM((epochs, 2 * REACH * width, channels), F32),
            pltpu.VMEM((max(1, early - 1), depth, 4 * LANES), BF16),
            pltpu.SemaphoreType.DMA((channels // LANES - 1,)),
        ],
        compiler_params=pltpu.CompilerParams(vmem_limit_bytes=20 * 2**20),
        cost_estimate=pl.CostEstimate(flops=flops, bytes_accessed=2 * w_gates.size, transcendentals=0),
    )(
        spread,
        recv_pair,
        recv_next,
        frames,
        mask,
        short_rows,
        long_rows,
        dw_kernel,
        w_expand,
        w_reduce,
        w_first,
        pltpu.with_memory_space_constraint(w_gates, pltpu.HBM),
        *kept,
    )
    *state_near, taps, w_later = rest
    kept = [] if before is None else before[1][1]
    send_far, *state_far = pl.pallas_call(
        functools.partial(later_kernel, early, turn, 7 + len(kept)),
        name="later",
        out_shape=[
            jax.ShapeDtypeStruct((pixels + tail * channels // LANES, far), BF16),
            *state(far),
        ],
        in_specs=[vmem] * 6 + [anywhere] + [vmem] * len(kept),
        out_specs=[vmem] * 7,
        input_output_aliases={7 + k: 1 + k for k in range(len(kept))},
        scratch_shapes=[pltpu.VMEM((8, far), F32)],
        compiler_params=pltpu.CompilerParams(vmem_limit_bytes=16 * 2**20),
        cost_estimate=pl.CostEstimate(flops=10**10, bytes_accessed=0, transcendentals=0),
    )(taps, w_later, mask, short_rows, long_rows, pooled, send, *kept)
    return (send, state_near), (send_far, state_far)


def pool(memory):
    return jnp.mean(memory.astype(BF16).astype(F32), axis=0, keepdims=True)


def tokens_of(both, gain):
    center = jnp.mean(both, axis=-1, keepdims=True)
    centred = both - center
    variance = jnp.mean(centred * centred, axis=-1, keepdims=True)
    return (centred * lax.rsqrt(variance + 1e-06) * gain).astype(BF16).astype(F32)


def put_tokens(known, own, at):
    line = lax.broadcasted_iota(jnp.int32, known.shape, 0)
    return jnp.where(line == at, own[0:1], jnp.where(line == at + 1, own[1:2], known))


def step_cells(arrived, decay0, inflow0, keep, block):
    state = arrived[: keep.shape[0]].astype(F32)
    return decay0[...] * state + inflow0[...], keep[...] * state + block[...]


def relay_kernel(arrived, decay0, inflow0, keep, block, open0, open1, before, send, pooled):
    cell0, cell1 = step_cells(arrived, decay0, inflow0, keep, block)
    send[...] = cell1.astype(BF16)
    pooled[0:1, :] = pool(open0[...] * jnp.tanh(cell0))
    pooled[1:2, :] = pool(open1[...] * jnp.tanh(cell1))


def relay_later_kernel(
    stage, arrived, decay0, inflow0, keep, block, open0, open1, pooled_early, short_rows, send
):
    pixels = keep.shape[0]
    cell0, cell1 = step_cells(arrived, decay0, inflow0, keep, block)
    send[:pixels] = cell1.astype(BF16)
    pooled = jnp.concatenate(
        [pool(open0[...] * jnp.tanh(cell0)), pool(open1[...] * jnp.tanh(cell1))], axis=0
    )
    both = jnp.concatenate([pooled_early[0:2, :], pooled], axis=1)
    own = tokens_of(both, short_rows[5:6, :])
    known = read_tail(arrived, pixels, short_rows.shape[1])
    write_tail(send, pixels, put_tokens(known, own, 2 * stage))


def final_kernel(
    count,
    *refs,
):
    halves = [
        (refs[:count], refs[2 * count : 2 * count + 6]),
        (refs[count : 2 * count], refs[2 * count + 6 : 2 * count + 12]),
    ]
    short_rows, months, slope, w_qkv, w_out = refs[2 * count + 12 : 2 * count + 17]
    memory_hbm, change, memory, sems = refs[2 * count + 17 :]
    epochs, pixels, channels = memory.shape
    total = months.shape[0]
    pooled = [[], []]
    at = 0
    for arrived, (decay0, inflow0, keep, block, open0, open1) in halves:
        lanes = slice(at, at + keep.shape[1])
        at += keep.shape[1]
        state = arrived[0][:pixels].astype(F32)
        for more in arrived[1:]:
            state = state + more[:pixels].astype(F32)
        cell0 = decay0[...] * state + inflow0[...]
        cell1 = keep[...] * state + block[...]
        for e, (gate, cell) in enumerate(((open0, cell0), (open1, cell1))):
            out = (gate[...] * jnp.tanh(cell)).astype(BF16)
            memory[e, :, lanes] = out
            pooled[e].append(pool(out))
    copies = [pltpu.make_async_copy(memory.at[e], memory_hbm.at[e], sems.at[e]) for e in range(epochs)]
    for copy in copies:
        copy.start()
    known = read_tail(halves[1][0][0], pixels, channels)
    for more in halves[1][0][1:]:
        known = known + read_tail(more, pixels, channels)
    both = jnp.concatenate([jnp.concatenate(parts, axis=1) for parts in pooled], axis=0)
    own = tokens_of(both, short_rows[5:6, :])
    stage = lax.axis_index("epoch")
    tokens = put_tokens(known, own, 2 * stage).astype(BF16)
    heads = slope.shape[1]
    depth = channels // heads
    qkv = jnp.dot(tokens, w_qkv[...], preferred_element_type=F32).astype(BF16).astype(F32)[:total]
    queries = qkv[:, :channels]
    keys = qkv[:, channels : 2 * channels]
    values = qkv[:, 2 * channels :]
    member = lax.broadcasted_iota(jnp.int32, (channels, heads), 0) // depth
    head_of = jnp.where(member == lax.broadcasted_iota(jnp.int32, (channels, heads), 1), 1.0, 0.0)
    member_t = lax.broadcasted_iota(jnp.int32, (heads, channels), 1) // depth
    channel_of = jnp.where(
        member_t == lax.broadcasted_iota(jnp.int32, (heads, channels), 0), 1.0, 0.0
    )

    def exact_dot(x, zero_one):
        high = x.astype(BF16)
        rest = x - high.astype(F32)
        low = rest.astype(BF16)
        least = (rest - low.astype(F32)).astype(BF16)
        out = jnp.dot(
            jnp.concatenate([high, low, least], axis=0), zero_one.astype(BF16), preferred_element_type=F32
        )
        count = x.shape[0]
        return out[:count] + out[count : 2 * count] + out[2 * count :]

    line = lax.broadcasted_iota(jnp.int32, (total, channels), 0)
    key_index = lax.broadcasted_iota(jnp.int32, (total, heads), 0)
    month = months[:, :heads]
    places = [epochs * stage + step for step in range(epochs)]
    products = []
    for mine in places:
        query = jnp.sum(jnp.where(line == mine, queries, 0.0), axis=0, keepdims=True)
        products.append(query * keys)
    raw = exact_dot(jnp.concatenate(products, axis=0), head_of)
    weights = []
    for step, mine in enumerate(places):
        now = jnp.sum(jnp.where(key_index == mine, month, 0.0), axis=0, keepdims=True)
        scores = raw[step * total : (step + 1) * total] / math.sqrt(depth) - slope[...] * (now - month)
        scores = jnp.where(key_index <= mine, scores, -1e30)
        expo = jnp.exp(scores - jnp.max(scores, axis=0, keepdims=True))
        weights.append(expo / jnp.sum(expo, axis=0, keepdims=True))
    wide = exact_dot(jnp.concatenate(weights, axis=0), channel_of)
    results = [
        jnp.sum(wide[step * total : (step + 1) * total] * values, axis=0, keepdims=True)
        for step in range(epochs)
    ]
    mixed = jnp.concatenate(results, axis=0).astype(BF16)
    change[...] = jnp.dot(mixed, w_out[...], preferred_element_type=F32).astype(BF16)
    for copy in copies:
        copy.wait()


def pairs(count, start):
    links = []
    for i in range(start, count - 1, 2):
        links += [(i, i + 1), (i + 1, i)]
    return links


def body(
    frames,
    valid,
    days,
    dw_kernel,
    dw_bias,
    norm_gain,
    norm_shift,
    w_expand,
    b_expand,
    w_reduce,
    layer_scale,
    w_gates,
    b_gates,
    forget_rate,
    attn_gain,
    w_query,
    w_key,
    w_value,
    w_out,
    head_slope,
):

    epochs, height, width, channels = frames.shape
    pixels = height * width
    tiles = lax.axis_size("tile")
    stages = lax.axis_size("epoch")
    total = epochs * stages
    tail = -(-total // 16) * 16
    gate_weights = w_gates.reshape(9 * channels, -1)
    near, to_pair, to_next = run_near(
        [
            frames,
            dw_kernel,
            valid,
            days,
            head_slope,
            b_expand,
            b_gates,
            dw_bias,
            norm_gain,
            norm_shift,
            layer_scale,
            forget_rate,
            attn_gain,
        ]
    )
    recv_pair = lax.ppermute(to_pair, "tile", pairs(tiles, 0))
    recv_next = lax.ppermute(to_next, "tile", pairs(tiles, 1))
    (
        spread,
        mask,
        short_rows,
        long_rows,
        months,
        slope,
        expand_near,
        reduce_near,
        w_first,
        qkv_near,
        out_near,
    ) = run_stage(near, w_expand, w_reduce, gate_weights, [w_query, w_key, w_value, w_out])
    early = max(1, channels // LANES - 1)
    staged = (spread, mask, short_rows, long_rows, near[0], near[1], expand_near, reduce_near, w_first)

    def blocks(turn, before):
        return run_block(
            tiles, early, turn, staged, recv_pair, recv_next, gate_weights, tail, before
        )

    short_chain = 1 < stages <= 8
    (send, state_near), (send_far, state_far) = first = blocks(FIRST if short_chain else ALL, None)
    if short_chain:
        (_, state_near), (_, state_far) = blocks(REST, first)
    vmem = pl.BlockSpec(memory_space=pltpu.VMEM)
    params = pltpu.CompilerParams(vmem_limit_bytes=16 * 2**20)
    cost = pl.CostEstimate(flops=10**10, bytes_accessed=0, transcendentals=0)

    def relay(arrived, before):
        return pl.pallas_call(
            relay_kernel,
            name="relay",
            out_shape=[
                jax.ShapeDtypeStruct((pixels, early * LANES), BF16),
                jax.ShapeDtypeStruct((8, early * LANES), F32),
            ],
            in_specs=[vmem] * 7 + [pl.BlockSpec(memory_space=pl.ANY)],
            out_specs=[vmem] * 2,
            compiler_params=params,
            cost_estimate=cost,
        )(arrived, *state_near, before)

    def relay_later(stage, arrived, pooled):
        return pl.pallas_call(
            functools.partial(relay_later_kernel, stage),
            name="relay_later",
            out_shape=jax.ShapeDtypeStruct(send_far.shape, BF16),
            in_specs=[vmem] * 9,
            out_specs=vmem,
            compiler_params=params,
            cost_estimate=cost,
        )(arrived, *state_far, pooled, short_rows)

    arrived = []
    arrived_far = []
    if stages <= 8:
        for stage in range(stages - 1):
            link = [(stage, stage + 1)]
            if stage > 0:
                send, pooled = relay(arrived[-1], send_far)
                send_far = relay_later(stage, arrived_far[-1], pooled)
            arrived.append(lax.ppermute(send, "epoch", link))
            arrived_far.append(lax.ppermute(send_far, "epoch", link))
    else:
        chain = [(i, i + 1) for i in range(stages - 1)]

        def along(state, width):
            keep, block = state[2], state[3]

            def turn(_, arriving):
                out = (keep * arriving.astype(F32) + block).astype(BF16)
                return lax.ppermute(out, "epoch", chain)

            return lax.fori_loop(0, stages - 1, turn, jnp.zeros((pixels, width), BF16))

        def unfold(tokens):
            parts = jnp.split(tokens, channels // LANES, axis=1)
            return jnp.concatenate(parts, axis=0)

        incoming = along(state_near, early * LANES)
        incoming_far = along(state_far, channels - early * LANES)
        _, pooled = relay(incoming, send_far)
        blank = jnp.zeros((tail * channels // LANES, LANES), BF16)
        told = relay_later(0, jnp.concatenate([incoming_far, blank]), pooled)[pixels:]
        told = jnp.concatenate(jnp.split(told, channels // LANES, axis=0), axis=1)
        known = lax.all_gather(told[:epochs], "epoch", axis=0, tiled=True)
        known = jnp.concatenate([known, jnp.zeros((tail - total, channels), BF16)])
        arrived.append(incoming)
        arrived_far.append(jnp.concatenate([incoming_far, unfold(known)]))

    memory, change = pl.pallas_call(
        functools.partial(final_kernel, len(arrived)),
        name="final",
        out_shape=[
            jax.ShapeDtypeStruct((epochs, pixels, channels), BF16),
            jax.ShapeDtypeStruct((epochs, channels), BF16),
        ],
        in_specs=[vmem] * (2 * len(arrived) + 17),
        out_specs=[pl.BlockSpec(memory_space=pltpu.HBM), vmem],
        scratch_shapes=[
            pltpu.VMEM((epochs, pixels, channels), BF16),
            pltpu.SemaphoreType.DMA((epochs,)),
        ],
        compiler_params=pltpu.CompilerParams(vmem_limit_bytes=24 * 2**20),
    )(*arrived, *arrived_far, *state_near, *state_far, short_rows, months, slope, qkv_near, out_near)
    return (
        memory.reshape(epochs, height, width, channels),
        change.reshape(epochs, 1, 1, channels),
    )


def solution(mesh):
    placed = (
        P("epoch", ("groups", "tile"), None, None),
        P("epoch", ("groups", "tile"), None),
        P("groups"),
    ) + (P(),) * 17
    return jax.shard_map(
        body,
        mesh=mesh,
        in_specs=placed,
        out_specs=(
            P("epoch", ("groups", "tile"), None, None),
            P("epoch", ("groups", "tile"), None, None),
        ),
        check_vma=False,
    )
```

```python
import functools
import math

import jax
import jax.numpy as jnp
from jax import lax
from jax.experimental import pallas as pl
from jax.experimental.pallas import tpu as pltpu
from jax.sharding import PartitionSpec as P

PATCH = 16
REACH = 4
LANES = 128
F32 = jnp.float32
BF16 = jnp.bfloat16


def sigmoid(x):
    return 0.5 * jnp.tanh(0.5 * x) + 0.5


def softplus(x):
    return jnp.maximum(x, 0.0) + jnp.log(1.0 + jnp.exp(-jnp.abs(x)))


def gelu_twice(x):
    inner = x * (0.7978845608028654 + (0.7978845608028654 * 0.044715) * (x * x))
    return x + x * jnp.tanh(inner)


def near_kernel(*refs):
    count = len(refs) // 2 - 1
    sources, outs = refs[:count], refs[count : 2 * count]
    to_pair, to_next, sems = refs[2 * count :]
    copies = [pltpu.make_async_copy(a, b, sems.at[i]) for i, (a, b) in enumerate(zip(sources, outs))]
    for copy in copies:
        copy.start()
    copies[0].wait()
    frames = outs[0]
    bottom = frames.shape[1] - REACH
    odd = lax.rem(lax.axis_index("tile"), 2)
    to_pair[...] = frames[:, pl.ds((1 - odd) * bottom, REACH)]
    to_next[...] = frames[:, pl.ds(odd * bottom, REACH)]
    for copy in copies[1:]:
        copy.wait()


def run_near(arrays):
    frames = arrays[0]
    rim = jax.ShapeDtypeStruct((frames.shape[0], REACH) + frames.shape[2:], frames.dtype)
    hbm = pl.BlockSpec(memory_space=pltpu.HBM)
    vmem = pl.BlockSpec(memory_space=pltpu.VMEM)
    out = pl.pallas_call(
        near_kernel,
        name="near",
        out_shape=[jax.ShapeDtypeStruct(x.shape, x.dtype) for x in arrays] + [rim] * 2,
        in_specs=[hbm] * len(arrays),
        out_specs=[vmem] * (len(arrays) + 2),
        scratch_shapes=[pltpu.SemaphoreType.DMA((len(arrays),))],
        compiler_params=pltpu.CompilerParams(vmem_limit_bytes=16 * 2**20),
    )(*[pltpu.with_memory_space_constraint(x, pltpu.HBM) for x in arrays])
    return out[: len(arrays)], out[-2], out[-1]


def stage_kernel(
    frames,
    dw_kernel,
    valid,
    days,
    slope_line,
    b_expand,
    b_gates,
    dw_bias,
    norm_gain,
    norm_shift,
    layer_scale,
    forget_rate,
    attn_gain,
    w_expand_hbm,
    w_reduce_hbm,
    w_gates_hbm,
    w_query_hbm,
    w_key_hbm,
    w_value_hbm,
    w_out_hbm,
    spread,
    mask,
    short_rows,
    long_rows,
    months,
    slope,
    w_expand,
    w_reduce,
    w_first,
    w_qkv,
    w_out,
    padded,
    sems,
):
    epochs, height, width, channels = frames.shape
    groups = channels // LANES
    rows = height + 2
    pixels = height * width
    moves = [
        (w_expand_hbm, w_expand),
        (w_reduce_hbm, w_reduce),
        (w_gates_hbm.at[:, pl.ds(0, w_first.shape[1])], w_first),
        (w_query_hbm, w_qkv.at[:, pl.ds(0, channels)]),
        (w_key_hbm, w_qkv.at[:, pl.ds(channels, channels)]),
        (w_value_hbm, w_qkv.at[:, pl.ds(2 * channels, channels)]),
        (w_out_hbm, w_out),
    ]
    copies = [pltpu.make_async_copy(a, b, sems.at[i]) for i, (a, b) in enumerate(moves)]
    for copy in copies:
        copy.start()

    for c in range(groups):
        for e in range(epochs):
            lanes = slice(c * LANES, (c + 1) * LANES)
            padded[c, e, :, 0:8, :] = jnp.zeros((height, 8, LANES), F32)
            padded[c, e, :, 8 + width : 16 + width, :] = jnp.zeros((height, 8, LANES), F32)
            padded[c, e, :, 8 : 8 + width, :] = frames[e, :, :, lanes].astype(F32)

    half = rows // 2

    def depthwise(index, carry):
        c = index // epochs
        e = index - c * epochs
        lanes = pl.ds(pl.multiple_of(c * LANES, LANES), LANES)
        for part in range(2):
            total = [None] * half
            for ox in range(7):
                factors = [dw_kernel[oy, pl.ds(ox, 1), lanes] for oy in range(7)]
                for r in range(height):
                    at = [(y, r + REACH - (part * half + y)) for y in range(half)]
                    at = [(y, oy) for y, oy in at if 0 <= oy < 7]
                    if not at:
                        continue
                    window = padded[c, e, r, pl.ds(5 + ox, width), :]
                    for y, oy in at:
                        term = window * factors[oy]
                        total[y] = term if total[y] is None else total[y] + term
            for y in range(half):
                line = (part * half + y) * width
                spread[e, pl.ds(line, width), lanes] = total[y]
        return carry

    lax.fori_loop(0, groups * epochs, depthwise, 0)

    short = (dw_bias, norm_gain, norm_shift, layer_scale, forget_rate, attn_gain)
    for k, line in enumerate(short):
        short_rows[k : k + 1, :] = line[...].reshape(1, -1)
    for k, line in enumerate((b_expand, b_gates)):
        long_rows[k : k + 1, :] = line[...].reshape(1, -1)
    slope[...] = slope_line[...].reshape(1, -1)
    total = days.shape[0]
    eye = lax.broadcasted_iota(jnp.int32, (total, total), 0) == lax.broadcasted_iota(
        jnp.int32, (total, total), 1
    )
    month = days[...].astype(F32).reshape(1, -1) / 30.0
    months[...] = jnp.broadcast_to(
        jnp.sum(jnp.where(eye, month, 0.0), axis=1, keepdims=True), months.shape
    )
    down = lax.broadcasted_iota(jnp.int32, (pixels, height), 0) // width
    pick = jnp.where(down == lax.broadcasted_iota(jnp.int32, (pixels, height), 1), 1.0, 0.0).astype(BF16)
    side = lax.rem(lax.broadcasted_iota(jnp.int32, (pixels, width), 0), width)
    place = side == lax.broadcasted_iota(jnp.int32, (pixels, width), 1)
    ones = jnp.ones((width, LANES), BF16)
    for e in range(epochs):
        plane = jnp.where(valid[e] > 0, 1.0, 0.0).astype(BF16)
        lines = jnp.dot(pick, plane, preferred_element_type=F32)
        mask[e * pixels : (e + 1) * pixels, :] = jnp.dot(
            jnp.where(place, lines, 0.0).astype(BF16), ones, preferred_element_type=F32
        )
    for copy in copies:
        copy.wait()


def run_stage(near, w_expand, w_reduce, w_gates, w_qkvo):
    frames, dw_kernel, valid, days, slope = near[:5]
    epochs, height, width, channels = frames.shape
    pixels = height * width
    total = days.shape[0]
    far = [w_expand, w_reduce, w_gates, *w_qkvo]
    hbm = pl.BlockSpec(memory_space=pltpu.HBM)
    vmem = pl.BlockSpec(memory_space=pltpu.VMEM)
    out_shape = [
        jax.ShapeDtypeStruct((epochs, (height + 2) * width, channels), F32),
        jax.ShapeDtypeStruct((epochs * pixels, LANES), F32),
        jax.ShapeDtypeStruct((8, channels), F32),
        jax.ShapeDtypeStruct((8, w_gates.shape[1]), F32),
        jax.ShapeDtypeStruct((total, LANES), F32),
        jax.ShapeDtypeStruct((1, slope.size), F32),
        jax.ShapeDtypeStruct(w_expand.shape, BF16),
        jax.ShapeDtypeStruct(w_reduce.shape, BF16),
        jax.ShapeDtypeStruct((w_gates.shape[0], 4 * LANES), BF16),
        jax.ShapeDtypeStruct((channels, 3 * channels), BF16),
        jax.ShapeDtypeStruct((channels, channels), BF16),
    ]
    return pl.pallas_call(
        stage_kernel,
        name="stage",
        out_shape=out_shape,
        in_specs=[vmem] * len(near) + [hbm] * len(far),
        out_specs=[vmem] * len(out_shape),
        scratch_shapes=[
            pltpu.VMEM((channels // LANES, epochs, height, width + 16, LANES), F32),
            pltpu.SemaphoreType.DMA((len(far),)),
        ],
        compiler_params=pltpu.CompilerParams(vmem_limit_bytes=24 * 2**20),
        cost_estimate=pl.CostEstimate(
            flops=10**10, bytes_accessed=8 * w_expand.size, transcendentals=0
        ),
    )(*near, *[pltpu.with_memory_space_constraint(x, pltpu.HBM) for x in far])


def on_devices(turn, work):
    if turn is None:
        work()
    else:
        stage = lax.axis_index("epoch")
        pl.when((stage >= turn[0]) & (stage < turn[1]))(work)


def block_kernel(tiles, turn, count, sends, *refs):
    outs = refs[count:]
    if not sends:
        outs = (None, None) + outs
    on_devices(turn, lambda: block_work(tiles, *refs[:12], *outs))


def block_work(
    tiles,
    spread,
    recv_pair,
    recv_next,
    frames,
    mask,
    short_rows,
    long_rows,
    dw_kernel,
    w_expand,
    w_reduce,
    w_first,
    w_gates_hbm,
    send,
    pooled,
    decay0,
    inflow0,
    keep,
    block,
    open0,
    open1,
    taps,
    w_later,
    rim,
    edge,
    w_gates,
    sems,
):
    epochs, height, width, channels = frames.shape
    groups = channels // LANES
    rows = height + 2
    pixels = height * width
    wide = 4 * LANES

    early = keep.shape[1] // LANES
    places = [w_gates.at[j] for j in range(early - 1)] + [w_later.at[j] for j in range(groups - early)]
    gate_copies = [
        pltpu.make_async_copy(w_gates_hbm.at[:, pl.ds((j + 1) * wide, wide)], place, sems.at[j])
        for j, place in enumerate(places)
    ]
    for copy in gate_copies:
        copy.start()

    dw_bias = short_rows[0:1, :]
    norm_gain = short_rows[1:2, :]
    norm_shift = short_rows[2:3, :]
    half_scale = 0.5 * short_rows[3:4, :]
    b_expand = long_rows[0:1, :]

    me = lax.axis_index("tile")
    odd = lax.rem(me, 2)
    pair_row = (1 - odd) * REACH
    next_row = odd * REACH

    for c in range(groups):
        lanes = slice(c * LANES, (c + 1) * LANES)
        for e in range(epochs):
            rim[c, e, :, 0:8, :] = jnp.zeros((2 * REACH, 8, LANES), F32)
            rim[c, e, :, 8 + width : 16 + width, :] = jnp.zeros((2 * REACH, 8, LANES), F32)
            rim[c, e, pl.ds(pair_row, REACH), 8 : 8 + width, :] = recv_pair[e, :, :, lanes].astype(F32)
            rim[c, e, pl.ds(next_row, REACH), 8 : 8 + width, :] = recv_next[e, :, :, lanes].astype(F32)

    def depthwise(index, carry):
        c = index // epochs
        e = index - c * epochs
        lanes = pl.ds(pl.multiple_of(c * LANES, LANES), LANES)
        total = [None] * (2 * REACH)
        for ox in range(7):
            factors = [dw_kernel[oy, pl.ds(ox, 1), lanes] for oy in range(7)]
            for k in range(REACH):
                above = rim[c, e, k, pl.ds(5 + ox, width), :]
                below = rim[c, e, REACH + k, pl.ds(5 + ox, width), :]
                for y in range(k + 1):
                    term = above * factors[k - y]
                    total[y] = term if total[y] is None else total[y] + term
                for y in range(k, REACH):
                    term = below * factors[6 + k - y]
                    at = REACH + y
                    total[at] = term if total[at] is None else total[at] + term
        for y in range(2 * REACH):
            edge[e, pl.ds(y * width, width), lanes] = total[y]
        return carry

    lax.fori_loop(0, groups * epochs, depthwise, 0)

    count = rows * width
    rimmed = REACH * width
    column = lax.broadcasted_iota(jnp.int32, (count, LANES), 0)
    across = lax.rem(column, width)
    line = column // width
    first = jnp.where(me == 0, 1, 0)
    last = jnp.where(me == tiles - 1, rows - 2, rows - 1)
    inside = jnp.where((line >= first) & (line <= last), 1.0, 0.0)
    for e in range(epochs):
        values = (
            jnp.concatenate(
                [
                    spread[e, :rimmed] + edge[e, :rimmed],
                    spread[e, rimmed : count - rimmed],
                    spread[e, count - rimmed :] + edge[e, rimmed:],
                ],
                axis=0,
            )
            + dw_bias
        )
        center = jnp.mean(values, axis=-1, keepdims=True)
        centred = values - center
        variance = jnp.mean(centred * centred, axis=-1, keepdims=True)
        normed = (centred * lax.rsqrt(variance + 1e-06) * norm_gain + norm_shift).astype(BF16)
        grown = jnp.dot(normed, w_expand[...], preferred_element_type=F32) + b_expand
        reduced = jnp.dot(gelu_twice(grown).astype(BF16), w_reduce[...], preferred_element_type=F32)
        for c in range(groups):
            lanes = slice(c * LANES, (c + 1) * LANES)
            centre = jnp.concatenate(
                [
                    rim[c, e, REACH - 1, 8 : 8 + width, :],
                    frames[e, :, :, lanes].astype(F32).reshape(pixels, LANES),
                    rim[c, e, REACH, 8 : 8 + width, :],
                ],
                axis=0,
            )
            feature = centre + half_scale[:, lanes] * reduced[:, lanes]
            feature = (feature * inside).astype(BF16).astype(F32)
            before = jnp.where(across == 0, 0.0, pltpu.roll(feature, 1, 0))
            after = jnp.where(across == width - 1, 0.0, pltpu.roll(feature, count - 1, 0))
            for ox, shifted in enumerate((before, feature, after)):
                packed = shifted.astype(BF16)
                for oy in range(3):
                    at = (oy * 3 + ox) * channels + c * LANES
                    taps[e * pixels : (e + 1) * pixels, at : at + LANES] = packed[
                        oy * width : oy * width + pixels
                    ]

    state = (decay0, inflow0, keep, block, open0, open1)
    cells_of(0, 0, taps, w_first, mask, short_rows, long_rows, send, pooled, state)
    for j in range(1, early):
        gate_copies[j - 1].wait()
        cells_of(j, j, taps, w_gates.at[j - 1], mask, short_rows, long_rows, send, pooled, state)
    for copy in gate_copies[early - 1 :]:
        copy.wait()


def gates_of(preact):
    quarter = LANES // 4
    lane = lax.broadcasted_iota(jnp.int32, (preact.shape[0], LANES), 1)
    spot = lane // quarter
    within = lane - spot * quarter
    sorted_ = []
    for i in range(4):
        gate = lax.rem(spot - i + 4, 4)
        sorted_.append(
            jnp.take_along_axis(preact[:, i * LANES : (i + 1) * LANES], 4 * within + gate, axis=1)
        )
    gates = []
    for g in range(4):
        out = sorted_[0]
        for i in range(1, 4):
            out = jnp.where(spot == (g + i) % 4, sorted_[i], out)
        gates.append(out if g == 0 else pltpu.roll(out, LANES - g * quarter, 1))
    return gates


def cells_of(j, at, taps, weights, mask, short_rows, long_rows, send, pooled, state):
    decay0, inflow0, keep, block, open0, open1 = state
    pixels = keep.shape[0]
    lanes = slice(at * LANES, (at + 1) * LANES)
    bias = long_rows[1:2, j * 4 * LANES : (j + 1) * 4 * LANES]
    rate = short_rows[4:5, j * LANES : (j + 1) * LANES]
    cell = None
    for e, opens in enumerate((open0, open1)):
        rows = slice(e * pixels, (e + 1) * pixels)
        preact = jnp.dot(taps[rows, :], weights[...], preferred_element_type=F32) + bias
        gate_in, gate_keep, gate_new, gate_out = gates_of(preact)
        good = mask[rows, :] > 0.5
        decay = jnp.where(good, jnp.exp(-rate * softplus(gate_keep)), 1.0)
        inflow = jnp.where(good, sigmoid(gate_in) * jnp.tanh(gate_new), 0.0)
        opened = sigmoid(gate_out)
        opens[:, lanes] = opened
        if e == 0:
            decay0[:, lanes] = decay
            inflow0[:, lanes] = inflow
            cell = inflow
        else:
            keep[:, lanes] = decay0[:, lanes] * decay
            cell = decay * inflow0[:, lanes] + inflow
            block[:, lanes] = cell
            if send is not None:
                send[:pixels, lanes] = cell.astype(BF16)
        if pooled is not None:
            pooled[e : e + 1, lanes] = pool(opened * jnp.tanh(cell))


def later_kernel(first, turn, count, sends, *refs):
    outs = refs[count:]
    if not sends:
        outs = (None,) + outs + (None,)
    on_devices(turn, lambda: later_work(first, *refs[:6], *outs))


def later_work(
    first,
    taps,
    w_gates,
    mask,
    short_rows,
    long_rows,
    pooled_early,
    send,
    decay0,
    inflow0,
    keep,
    block,
    open0,
    open1,
    pooled,
):
    channels = short_rows.shape[1]
    state = (decay0, inflow0, keep, block, open0, open1)
    for j in range(first, channels // LANES):
        at = j - first
        cells_of(j, at, taps, w_gates.at[at], mask, short_rows, long_rows, send, pooled, state)
    if send is None:
        return
    pixels = keep.shape[0]
    both = jnp.concatenate([pooled_early[0:2, :], pooled[0:2, :]], axis=1)
    own = tokens_of(both, short_rows[5:6, :])
    tail = (send.shape[0] - pixels) * LANES // channels
    known = jnp.zeros((tail, channels), F32)
    write_tail(send, pixels, put_tokens(known, own, 0))


def write_tail(send, pixels, tokens):
    tail, channels = tokens.shape
    for c in range(channels // LANES):
        at = pixels + c * tail
        send[at : at + tail, :] = tokens[:, c * LANES : (c + 1) * LANES].astype(BF16)


def read_tail(arrived, pixels, channels):
    tail = (arrived.shape[0] - pixels) * LANES // channels
    parts = [
        arrived[pixels + c * tail : pixels + (c + 1) * tail, :].astype(F32)
        for c in range(channels // LANES)
    ]
    return jnp.concatenate(parts, axis=1)


def run_block(tiles, early, turn, staged, recv_pair, recv_next, w_gates, kept, after):
    spread, mask, short_rows, long_rows, frames, dw_kernel, w_expand, w_reduce, w_first = staged
    epochs, height, width, channels = frames.shape
    pixels = height * width
    depth = w_gates.shape[0]
    vmem = pl.BlockSpec(memory_space=pltpu.VMEM)
    hbm = pl.BlockSpec(memory_space=pltpu.HBM)
    anywhere = pl.BlockSpec(memory_space=pl.ANY)
    near = early * LANES
    far = channels - near
    sends = not kept
    sent = [
        jax.ShapeDtypeStruct((pixels, near), BF16),
        jax.ShapeDtypeStruct((8, near), F32),
    ] * sends
    state = [jax.ShapeDtypeStruct((pixels, near), F32)] * 6
    flops = 2 * epochs * pixels * (2 * w_expand.size + w_gates.size)
    out = pl.pallas_call(
        functools.partial(block_kernel, tiles, turn, 12 + len(kept) + len(after), sends),
        name="block",
        out_shape=[
            *sent,
            *state,
            jax.ShapeDtypeStruct((epochs * pixels, depth), BF16),
            jax.ShapeDtypeStruct((far // LANES, depth, 4 * LANES), BF16),
        ],
        in_specs=[vmem] * 11 + [hbm] + [vmem] * len(kept) + [anywhere] * len(after),
        out_specs=[vmem] * (len(sent) + 8),
        input_output_aliases={12 + k: len(sent) + k for k in range(len(kept))},
        scratch_shapes=[
            pltpu.VMEM((channels // LANES, epochs, 2 * REACH, width + 16, LANES), F32),
            pltpu.VMEM((epochs, 2 * REACH * width, channels), F32),
            pltpu.VMEM((max(1, early - 1), depth, 4 * LANES), BF16),
            pltpu.SemaphoreType.DMA((channels // LANES - 1,)),
        ],
        compiler_params=pltpu.CompilerParams(vmem_limit_bytes=20 * 2**20),
        cost_estimate=pl.CostEstimate(flops=flops, bytes_accessed=2 * w_gates.size, transcendentals=0),
    )(
        spread,
        recv_pair,
        recv_next,
        frames,
        mask,
        short_rows,
        long_rows,
        dw_kernel,
        w_expand,
        w_reduce,
        w_first,
        pltpu.with_memory_space_constraint(w_gates, pltpu.HBM),
        *kept,
        *after,
    )
    return out[: len(sent)], out[len(sent) : -2], out[-2:]


def run_later(early, turn, staged, pooled, weighed, tail, kept, after):
    _, mask, short_rows, long_rows = staged[:4]
    taps, w_later = weighed
    pixels = taps.shape[0] // 2
    channels = short_rows.shape[1]
    far = channels - early * LANES
    vmem = pl.BlockSpec(memory_space=pltpu.VMEM)
    anywhere = pl.BlockSpec(memory_space=pl.ANY)
    sends = not kept
    sent = [jax.ShapeDtypeStruct((pixels + tail * channels // LANES, far), BF16)] * sends
    out = pl.pallas_call(
        functools.partial(later_kernel, early, turn, 6 + len(kept) + len(after), sends),
        name="later",
        out_shape=[*sent] + [jax.ShapeDtypeStruct((pixels, far), F32)] * 6,
        in_specs=[vmem] * 6 + [vmem] * len(kept) + [anywhere] * len(after),
        out_specs=[vmem] * (len(sent) + 6),
        input_output_aliases={6 + k: len(sent) + k for k in range(len(kept))},
        scratch_shapes=[pltpu.VMEM((8, far), F32)] * sends,
        compiler_params=pltpu.CompilerParams(vmem_limit_bytes=16 * 2**20),
        cost_estimate=pl.CostEstimate(flops=10**10, bytes_accessed=0, transcendentals=0),
    )(taps, w_later, mask, short_rows, long_rows, pooled, *kept, *after)
    return out[: len(sent)], out[len(sent) :]


def pool(memory):
    return jnp.mean(memory.astype(BF16).astype(F32), axis=0, keepdims=True)


def tokens_of(both, gain):
    center = jnp.mean(both, axis=-1, keepdims=True)
    centred = both - center
    variance = jnp.mean(centred * centred, axis=-1, keepdims=True)
    return (centred * lax.rsqrt(variance + 1e-06) * gain).astype(BF16).astype(F32)


def put_tokens(known, own, at):
    line = lax.broadcasted_iota(jnp.int32, known.shape, 0)
    return jnp.where(line == at, own[0:1], jnp.where(line == at + 1, own[1:2], known))


def step_cells(arrived, decay0, inflow0, keep, block):
    state = arrived[: keep.shape[0]].astype(F32)
    return decay0[...] * state + inflow0[...], keep[...] * state + block[...]


def relay_kernel(arrived, decay0, inflow0, keep, block, open0, open1, before, send, pooled):
    cell0, cell1 = step_cells(arrived, decay0, inflow0, keep, block)
    send[...] = cell1.astype(BF16)
    pooled[0:1, :] = pool(open0[...] * jnp.tanh(cell0))
    pooled[1:2, :] = pool(open1[...] * jnp.tanh(cell1))


def relay_later_kernel(
    stage, arrived, decay0, inflow0, keep, block, open0, open1, pooled_early, short_rows, send
):
    pixels = keep.shape[0]
    cell0, cell1 = step_cells(arrived, decay0, inflow0, keep, block)
    send[:pixels] = cell1.astype(BF16)
    pooled = jnp.concatenate(
        [pool(open0[...] * jnp.tanh(cell0)), pool(open1[...] * jnp.tanh(cell1))], axis=0
    )
    both = jnp.concatenate([pooled_early[0:2, :], pooled], axis=1)
    own = tokens_of(both, short_rows[5:6, :])
    known = read_tail(arrived, pixels, short_rows.shape[1])
    write_tail(send, pixels, put_tokens(known, own, 2 * stage))


def final_kernel(
    count,
    *refs,
):
    halves = [
        (refs[:count], refs[2 * count : 2 * count + 6]),
        (refs[count : 2 * count], refs[2 * count + 6 : 2 * count + 12]),
    ]
    short_rows, months, slope, w_qkv, w_out = refs[2 * count + 12 : 2 * count + 17]
    memory_hbm, change, memory, sems = refs[2 * count + 17 :]
    epochs, pixels, channels = memory.shape
    total = months.shape[0]
    pooled = [[], []]
    at = 0
    for arrived, (decay0, inflow0, keep, block, open0, open1) in halves:
        lanes = slice(at, at + keep.shape[1])
        at += keep.shape[1]
        state = arrived[0][:pixels].astype(F32)
        for more in arrived[1:]:
            state = state + more[:pixels].astype(F32)
        cell0 = decay0[...] * state + inflow0[...]
        cell1 = keep[...] * state + block[...]
        for e, (gate, cell) in enumerate(((open0, cell0), (open1, cell1))):
            out = (gate[...] * jnp.tanh(cell)).astype(BF16)
            memory[e, :, lanes] = out
            pooled[e].append(pool(out))
    copies = [pltpu.make_async_copy(memory.at[e], memory_hbm.at[e], sems.at[e]) for e in range(epochs)]
    for copy in copies:
        copy.start()
    known = read_tail(halves[1][0][0], pixels, channels)
    for more in halves[1][0][1:]:
        known = known + read_tail(more, pixels, channels)
    both = jnp.concatenate([jnp.concatenate(parts, axis=1) for parts in pooled], axis=0)
    own = tokens_of(both, short_rows[5:6, :])
    stage = lax.axis_index("epoch")
    tokens = put_tokens(known, own, 2 * stage).astype(BF16)
    heads = slope.shape[1]
    depth = channels // heads
    qkv = jnp.dot(tokens, w_qkv[...], preferred_element_type=F32).astype(BF16).astype(F32)[:total]
    queries = qkv[:, :channels]
    keys = qkv[:, channels : 2 * channels]
    values = qkv[:, 2 * channels :]
    member = lax.broadcasted_iota(jnp.int32, (channels, heads), 0) // depth
    head_of = jnp.where(member == lax.broadcasted_iota(jnp.int32, (channels, heads), 1), 1.0, 0.0)
    member_t = lax.broadcasted_iota(jnp.int32, (heads, channels), 1) // depth
    channel_of = jnp.where(
        member_t == lax.broadcasted_iota(jnp.int32, (heads, channels), 0), 1.0, 0.0
    )

    def exact_dot(x, zero_one):
        high = x.astype(BF16)
        rest = x - high.astype(F32)
        low = rest.astype(BF16)
        least = (rest - low.astype(F32)).astype(BF16)
        out = jnp.dot(
            jnp.concatenate([high, low, least], axis=0), zero_one.astype(BF16), preferred_element_type=F32
        )
        count = x.shape[0]
        return out[:count] + out[count : 2 * count] + out[2 * count :]

    line = lax.broadcasted_iota(jnp.int32, (total, channels), 0)
    key_index = lax.broadcasted_iota(jnp.int32, (total, heads), 0)
    month = months[:, :heads]
    places = [epochs * stage + step for step in range(epochs)]
    products = []
    for mine in places:
        query = jnp.sum(jnp.where(line == mine, queries, 0.0), axis=0, keepdims=True)
        products.append(query * keys)
    raw = exact_dot(jnp.concatenate(products, axis=0), head_of)
    weights = []
    for step, mine in enumerate(places):
        now = jnp.sum(jnp.where(key_index == mine, month, 0.0), axis=0, keepdims=True)
        scores = raw[step * total : (step + 1) * total] / math.sqrt(depth) - slope[...] * (now - month)
        scores = jnp.where(key_index <= mine, scores, -1e30)
        expo = jnp.exp(scores - jnp.max(scores, axis=0, keepdims=True))
        weights.append(expo / jnp.sum(expo, axis=0, keepdims=True))
    wide = exact_dot(jnp.concatenate(weights, axis=0), channel_of)
    results = [
        jnp.sum(wide[step * total : (step + 1) * total] * values, axis=0, keepdims=True)
        for step in range(epochs)
    ]
    mixed = jnp.concatenate(results, axis=0).astype(BF16)
    change[...] = jnp.dot(mixed, w_out[...], preferred_element_type=F32).astype(BF16)
    for copy in copies:
        copy.wait()


def pairs(count, start):
    links = []
    for i in range(start, count - 1, 2):
        links += [(i, i + 1), (i + 1, i)]
    return links


def body(
    frames,
    valid,
    days,
    dw_kernel,
    dw_bias,
    norm_gain,
    norm_shift,
    w_expand,
    b_expand,
    w_reduce,
    layer_scale,
    w_gates,
    b_gates,
    forget_rate,
    attn_gain,
    w_query,
    w_key,
    w_value,
    w_out,
    head_slope,
):

    epochs, height, width, channels = frames.shape
    pixels = height * width
    tiles = lax.axis_size("tile")
    stages = lax.axis_size("epoch")
    total = epochs * stages
    tail = -(-total // 16) * 16
    gate_weights = w_gates.reshape(9 * channels, -1)
    near, to_pair, to_next = run_near(
        [
            frames,
            dw_kernel,
            valid,
            days,
            head_slope,
            b_expand,
            b_gates,
            dw_bias,
            norm_gain,
            norm_shift,
            layer_scale,
            forget_rate,
            attn_gain,
        ]
    )
    recv_pair = lax.ppermute(to_pair, "tile", pairs(tiles, 0))
    recv_next = lax.ppermute(to_next, "tile", pairs(tiles, 1))
    (
        spread,
        mask,
        short_rows,
        long_rows,
        months,
        slope,
        expand_near,
        reduce_near,
        w_first,
        qkv_near,
        out_near,
    ) = run_stage(near, w_expand, w_reduce, gate_weights, [w_query, w_key, w_value, w_out])
    early = max(1, channels // LANES - 1)
    staged = (spread, mask, short_rows, long_rows, near[0], near[1], expand_near, reduce_near, w_first)

    def blocks(turn, kept, after):
        return run_block(
            tiles, early, turn, staged, recv_pair, recv_next, gate_weights, kept, after
        )

    short_chain = 1 < stages <= 8
    first = (0, 1) if short_chain else None
    (send, pooled), state_near, weighed = blocks(first, [], [])
    (send_far,), state_far = run_later(early, first, staged, pooled, weighed, tail, [], [send])
    if short_chain:
        _, state_near, weighed = blocks((1, stages), state_near, [send_far])
        _, state_far = run_later(early, (1, 2), staged, pooled, weighed, tail, state_far, [])
    vmem = pl.BlockSpec(memory_space=pltpu.VMEM)
    params = pltpu.CompilerParams(vmem_limit_bytes=16 * 2**20)
    cost = pl.CostEstimate(flops=10**10, bytes_accessed=0, transcendentals=0)

    def relay(arrived, before):
        return pl.pallas_call(
            relay_kernel,
            name="relay",
            out_shape=[
                jax.ShapeDtypeStruct((pixels, early * LANES), BF16),
                jax.ShapeDtypeStruct((8, early * LANES), F32),
            ],
            in_specs=[vmem] * 7 + [pl.BlockSpec(memory_space=pl.ANY)],
            out_specs=[vmem] * 2,
            compiler_params=params,
            cost_estimate=cost,
        )(arrived, *state_near, before)

    def relay_later(stage, arrived, pooled, state_far):
        return pl.pallas_call(
            functools.partial(relay_later_kernel, stage),
            name="relay_later",
            out_shape=jax.ShapeDtypeStruct(send_far.shape, BF16),
            in_specs=[vmem] * 9,
            out_specs=vmem,
            compiler_params=params,
            cost_estimate=cost,
        )(arrived, *state_far, pooled, short_rows)

    arrived = []
    arrived_far = []
    if stages <= 8:
        for stage in range(stages - 1):
            link = [(stage, stage + 1)]
            if stage > 0:
                send, pooled = relay(arrived[-1], send_far)
                if stage == 1 and stages > 2:
                    _, state_far = run_later(
                        early, (2, stages), staged, pooled, weighed, tail, state_far, [send]
                    )
                send_far = relay_later(stage, arrived_far[-1], pooled, state_far)
            arrived.append(lax.ppermute(send, "epoch", link))
            arrived_far.append(lax.ppermute(send_far, "epoch", link))
    else:
        chain = [(i, i + 1) for i in range(stages - 1)]

        def along(state, width):
            keep, block = state[2], state[3]

            def turn(_, arriving):
                out = (keep * arriving.astype(F32) + block).astype(BF16)
                return lax.ppermute(out, "epoch", chain)

            return lax.fori_loop(0, stages - 1, turn, jnp.zeros((pixels, width), BF16))

        def unfold(tokens):
            parts = jnp.split(tokens, channels // LANES, axis=1)
            return jnp.concatenate(parts, axis=0)

        incoming = along(state_near, early * LANES)
        incoming_far = along(state_far, channels - early * LANES)
        _, pooled = relay(incoming, send_far)
        blank = jnp.zeros((tail * channels // LANES, LANES), BF16)
        told = relay_later(0, jnp.concatenate([incoming_far, blank]), pooled, state_far)[pixels:]
        told = jnp.concatenate(jnp.split(told, channels // LANES, axis=0), axis=1)
        known = lax.all_gather(told[:epochs], "epoch", axis=0, tiled=True)
        known = jnp.concatenate([known, jnp.zeros((tail - total, channels), BF16)])
        arrived.append(incoming)
        arrived_far.append(jnp.concatenate([incoming_far, unfold(known)]))

    memory, change = pl.pallas_call(
        functools.partial(final_kernel, len(arrived)),
        name="final",
        out_shape=[
            jax.ShapeDtypeStruct((epochs, pixels, channels), BF16),
            jax.ShapeDtypeStruct((epochs, channels), BF16),
        ],
        in_specs=[vmem] * (2 * len(arrived) + 17),
        out_specs=[pl.BlockSpec(memory_space=pltpu.HBM), vmem],
        scratch_shapes=[
            pltpu.VMEM((epochs, pixels, channels), BF16),
            pltpu.SemaphoreType.DMA((epochs,)),
        ],
        compiler_params=pltpu.CompilerParams(vmem_limit_bytes=24 * 2**20),
    )(*arrived, *arrived_far, *state_near, *state_far, short_rows, months, slope, qkv_near, out_near)
    return (
        memory.reshape(epochs, height, width, channels),
        change.reshape(epochs, 1, 1, channels),
    )


def solution(mesh):
    placed = (
        P("epoch", ("groups", "tile"), None, None),
        P("epoch", ("groups", "tile"), None),
        P("groups"),
    ) + (P(),) * 17
    return jax.shard_map(
        body,
        mesh=mesh,
        in_specs=placed,
        out_specs=(
            P("epoch", ("groups", "tile"), None, None),
            P("epoch", ("groups", "tile"), None, None),
        ),
        check_vma=False,
    )
```

```python
import functools
import math

import jax
import jax.numpy as jnp
from jax import lax
from jax.experimental import pallas as pl
from jax.experimental.pallas import tpu as pltpu
from jax.sharding import PartitionSpec as P

PATCH = 16
REACH = 4
LANES = 128
F32 = jnp.float32
BF16 = jnp.bfloat16


def sigmoid(x):
    return 0.5 * jnp.tanh(0.5 * x) + 0.5


def softplus(x):
    return jnp.maximum(x, 0.0) + jnp.log(1.0 + jnp.exp(-jnp.abs(x)))


def gelu_twice(x):
    inner = x * (0.7978845608028654 + (0.7978845608028654 * 0.044715) * (x * x))
    return x + x * jnp.tanh(inner)


def near_kernel(*refs):
    count = len(refs) // 2 - 1
    sources, outs = refs[:count], refs[count : 2 * count]
    to_pair, to_next, sems = refs[2 * count :]
    copies = [pltpu.make_async_copy(a, b, sems.at[i]) for i, (a, b) in enumerate(zip(sources, outs))]
    for copy in copies:
        copy.start()
    copies[0].wait()
    frames = outs[0]
    bottom = frames.shape[1] - REACH
    odd = lax.rem(lax.axis_index("tile"), 2)
    to_pair[...] = frames[:, pl.ds((1 - odd) * bottom, REACH)]
    to_next[...] = frames[:, pl.ds(odd * bottom, REACH)]
    for copy in copies[1:]:
        copy.wait()


def run_near(arrays):
    frames = arrays[0]
    rim = jax.ShapeDtypeStruct((frames.shape[0], REACH) + frames.shape[2:], frames.dtype)
    hbm = pl.BlockSpec(memory_space=pltpu.HBM)
    vmem = pl.BlockSpec(memory_space=pltpu.VMEM)
    out = pl.pallas_call(
        near_kernel,
        name="near",
        out_shape=[jax.ShapeDtypeStruct(x.shape, x.dtype) for x in arrays] + [rim] * 2,
        in_specs=[hbm] * len(arrays),
        out_specs=[vmem] * (len(arrays) + 2),
        scratch_shapes=[pltpu.SemaphoreType.DMA((len(arrays),))],
        compiler_params=pltpu.CompilerParams(vmem_limit_bytes=16 * 2**20),
    )(*[pltpu.with_memory_space_constraint(x, pltpu.HBM) for x in arrays])
    return out[: len(arrays)], out[-2], out[-1]


def stage_kernel(
    frames,
    dw_kernel,
    valid,
    days,
    slope_line,
    b_expand,
    b_gates,
    dw_bias,
    norm_gain,
    norm_shift,
    layer_scale,
    forget_rate,
    attn_gain,
    w_expand_hbm,
    w_reduce_hbm,
    w_gates_hbm,
    w_query_hbm,
    w_key_hbm,
    w_value_hbm,
    w_out_hbm,
    spread,
    mask,
    short_rows,
    long_rows,
    months,
    slope,
    w_expand,
    w_reduce,
    w_first,
    w_qkv,
    w_out,
    padded,
    sems,
):
    epochs, height, width, channels = frames.shape
    groups = channels // LANES
    rows = height + 2
    pixels = height * width
    moves = [
        (w_expand_hbm, w_expand),
        (w_reduce_hbm, w_reduce),
        (w_gates_hbm.at[:, pl.ds(0, w_first.shape[1])], w_first),
        (w_query_hbm, w_qkv.at[:, pl.ds(0, channels)]),
        (w_key_hbm, w_qkv.at[:, pl.ds(channels, channels)]),
        (w_value_hbm, w_qkv.at[:, pl.ds(2 * channels, channels)]),
        (w_out_hbm, w_out),
    ]
    copies = [pltpu.make_async_copy(a, b, sems.at[i]) for i, (a, b) in enumerate(moves)]
    for copy in copies:
        copy.start()

    for c in range(groups):
        for e in range(epochs):
            lanes = slice(c * LANES, (c + 1) * LANES)
            padded[c, e, :, 0:8, :] = jnp.zeros((height, 8, LANES), F32)
            padded[c, e, :, 8 + width : 16 + width, :] = jnp.zeros((height, 8, LANES), F32)
            padded[c, e, :, 8 : 8 + width, :] = frames[e, :, :, lanes].astype(F32)

    half = rows // 2

    def depthwise(index, carry):
        c = index // epochs
        e = index - c * epochs
        lanes = pl.ds(pl.multiple_of(c * LANES, LANES), LANES)
        for part in range(2):
            total = [None] * half
            for ox in range(7):
                factors = [dw_kernel[oy, pl.ds(ox, 1), lanes] for oy in range(7)]
                for r in range(height):
                    at = [(y, r + REACH - (part * half + y)) for y in range(half)]
                    at = [(y, oy) for y, oy in at if 0 <= oy < 7]
                    if not at:
                        continue
                    window = padded[c, e, r, pl.ds(5 + ox, width), :]
                    for y, oy in at:
                        term = window * factors[oy]
                        total[y] = term if total[y] is None else total[y] + term
            for y in range(half):
                line = (part * half + y) * width
                spread[e, pl.ds(line, width), lanes] = total[y]
        return carry

    lax.fori_loop(0, groups * epochs, depthwise, 0)

    short = (dw_bias, norm_gain, norm_shift, layer_scale, forget_rate, attn_gain)
    for k, line in enumerate(short):
        short_rows[k : k + 1, :] = line[...].reshape(1, -1)
    for k, line in enumerate((b_expand, b_gates)):
        long_rows[k : k + 1, :] = line[...].reshape(1, -1)
    slope[...] = slope_line[...].reshape(1, -1)
    total = days.shape[0]
    eye = lax.broadcasted_iota(jnp.int32, (total, total), 0) == lax.broadcasted_iota(
        jnp.int32, (total, total), 1
    )
    month = days[...].astype(F32).reshape(1, -1) / 30.0
    months[...] = jnp.broadcast_to(
        jnp.sum(jnp.where(eye, month, 0.0), axis=1, keepdims=True), months.shape
    )
    down = lax.broadcasted_iota(jnp.int32, (pixels, height), 0) // width
    pick = jnp.where(down == lax.broadcasted_iota(jnp.int32, (pixels, height), 1), 1.0, 0.0).astype(BF16)
    side = lax.rem(lax.broadcasted_iota(jnp.int32, (pixels, width), 0), width)
    place = side == lax.broadcasted_iota(jnp.int32, (pixels, width), 1)
    ones = jnp.ones((width, LANES), BF16)
    for e in range(epochs):
        plane = jnp.where(valid[e] > 0, 1.0, 0.0).astype(BF16)
        lines = jnp.dot(pick, plane, preferred_element_type=F32)
        mask[e * pixels : (e + 1) * pixels, :] = jnp.dot(
            jnp.where(place, lines, 0.0).astype(BF16), ones, preferred_element_type=F32
        )
    for copy in copies:
        copy.wait()


def run_stage(near, w_expand, w_reduce, w_gates, w_qkvo):
    frames, dw_kernel, valid, days, slope = near[:5]
    epochs, height, width, channels = frames.shape
    pixels = height * width
    total = days.shape[0]
    far = [w_expand, w_reduce, w_gates, *w_qkvo]
    hbm = pl.BlockSpec(memory_space=pltpu.HBM)
    vmem = pl.BlockSpec(memory_space=pltpu.VMEM)
    out_shape = [
        jax.ShapeDtypeStruct((epochs, (height + 2) * width, channels), F32),
        jax.ShapeDtypeStruct((epochs * pixels, LANES), F32),
        jax.ShapeDtypeStruct((8, channels), F32),
        jax.ShapeDtypeStruct((8, w_gates.shape[1]), F32),
        jax.ShapeDtypeStruct((total, LANES), F32),
        jax.ShapeDtypeStruct((1, slope.size), F32),
        jax.ShapeDtypeStruct(w_expand.shape, BF16),
        jax.ShapeDtypeStruct(w_reduce.shape, BF16),
        jax.ShapeDtypeStruct((w_gates.shape[0], 4 * LANES), BF16),
        jax.ShapeDtypeStruct((channels, 3 * channels), BF16),
        jax.ShapeDtypeStruct((channels, channels), BF16),
    ]
    return pl.pallas_call(
        stage_kernel,
        name="stage",
        out_shape=out_shape,
        in_specs=[vmem] * len(near) + [hbm] * len(far),
        out_specs=[vmem] * len(out_shape),
        scratch_shapes=[
            pltpu.VMEM((channels // LANES, epochs, height, width + 16, LANES), F32),
            pltpu.SemaphoreType.DMA((len(far),)),
        ],
        compiler_params=pltpu.CompilerParams(vmem_limit_bytes=24 * 2**20),
        cost_estimate=pl.CostEstimate(
            flops=10**10, bytes_accessed=8 * w_expand.size, transcendentals=0
        ),
    )(*near, *[pltpu.with_memory_space_constraint(x, pltpu.HBM) for x in far])


def on_devices(turn, work):
    if turn is None:
        work()
    else:
        stage = lax.axis_index("epoch")
        pl.when((stage >= turn[0]) & (stage < turn[1]))(work)


def block_kernel(tiles, turn, count, sends, *refs):
    outs = refs[count:]
    if not sends:
        outs = (None, None) + outs
    on_devices(turn, lambda: block_work(tiles, *refs[:12], *outs))


def block_work(
    tiles,
    spread,
    recv_pair,
    recv_next,
    frames,
    mask,
    short_rows,
    long_rows,
    dw_kernel,
    w_expand,
    w_reduce,
    w_first,
    w_gates_hbm,
    send,
    pooled,
    decay0,
    inflow0,
    keep,
    block,
    open0,
    open1,
    taps,
    w_later,
    rim,
    edge,
    w_gates,
    sems,
):
    epochs, height, width, channels = frames.shape
    groups = channels // LANES
    rows = height + 2
    pixels = height * width
    wide = 4 * LANES

    early = keep.shape[1] // LANES
    places = [w_gates.at[j] for j in range(early - 1)] + [w_later.at[j] for j in range(groups - early)]
    gate_copies = [
        pltpu.make_async_copy(w_gates_hbm.at[:, pl.ds((j + 1) * wide, wide)], place, sems.at[j])
        for j, place in enumerate(places)
    ]
    for copy in gate_copies:
        copy.start()

    dw_bias = short_rows[0:1, :]
    norm_gain = short_rows[1:2, :]
    norm_shift = short_rows[2:3, :]
    half_scale = 0.5 * short_rows[3:4, :]
    b_expand = long_rows[0:1, :]

    me = lax.axis_index("tile")
    odd = lax.rem(me, 2)
    pair_row = (1 - odd) * REACH
    next_row = odd * REACH

    for c in range(groups):
        lanes = slice(c * LANES, (c + 1) * LANES)
        for e in range(epochs):
            rim[c, e, :, 0:8, :] = jnp.zeros((2 * REACH, 8, LANES), F32)
            rim[c, e, :, 8 + width : 16 + width, :] = jnp.zeros((2 * REACH, 8, LANES), F32)
            rim[c, e, pl.ds(pair_row, REACH), 8 : 8 + width, :] = recv_pair[e, :, :, lanes].astype(F32)
            rim[c, e, pl.ds(next_row, REACH), 8 : 8 + width, :] = recv_next[e, :, :, lanes].astype(F32)

    def depthwise(index, carry):
        c = index // epochs
        e = index - c * epochs
        lanes = pl.ds(pl.multiple_of(c * LANES, LANES), LANES)
        total = [None] * (2 * REACH)
        for ox in range(7):
            factors = [dw_kernel[oy, pl.ds(ox, 1), lanes] for oy in range(7)]
            for k in range(REACH):
                above = rim[c, e, k, pl.ds(5 + ox, width), :]
                below = rim[c, e, REACH + k, pl.ds(5 + ox, width), :]
                for y in range(k + 1):
                    term = above * factors[k - y]
                    total[y] = term if total[y] is None else total[y] + term
                for y in range(k, REACH):
                    term = below * factors[6 + k - y]
                    at = REACH + y
                    total[at] = term if total[at] is None else total[at] + term
        for y in range(2 * REACH):
            edge[e, pl.ds(y * width, width), lanes] = total[y]
        return carry

    lax.fori_loop(0, groups * epochs, depthwise, 0)

    count = rows * width
    rimmed = REACH * width
    column = lax.broadcasted_iota(jnp.int32, (count, LANES), 0)
    across = lax.rem(column, width)
    line = column // width
    first = jnp.where(me == 0, 1, 0)
    last = jnp.where(me == tiles - 1, rows - 2, rows - 1)
    inside = jnp.where((line >= first) & (line <= last), 1.0, 0.0)
    for e in range(epochs):
        values = (
            jnp.concatenate(
                [
                    spread[e, :rimmed] + edge[e, :rimmed],
                    spread[e, rimmed : count - rimmed],
                    spread[e, count - rimmed :] + edge[e, rimmed:],
                ],
                axis=0,
            )
            + dw_bias
        )
        center = jnp.mean(values, axis=-1, keepdims=True)
        centred = values - center
        variance = jnp.mean(centred * centred, axis=-1, keepdims=True)
        normed = (centred * lax.rsqrt(variance + 1e-06) * norm_gain + norm_shift).astype(BF16)
        grown = jnp.dot(normed, w_expand[...], preferred_element_type=F32) + b_expand
        reduced = jnp.dot(gelu_twice(grown).astype(BF16), w_reduce[...], preferred_element_type=F32)
        for c in range(groups):
            lanes = slice(c * LANES, (c + 1) * LANES)
            centre = jnp.concatenate(
                [
                    rim[c, e, REACH - 1, 8 : 8 + width, :],
                    frames[e, :, :, lanes].astype(F32).reshape(pixels, LANES),
                    rim[c, e, REACH, 8 : 8 + width, :],
                ],
                axis=0,
            )
            feature = centre + half_scale[:, lanes] * reduced[:, lanes]
            feature = (feature * inside).astype(BF16).astype(F32)
            before = jnp.where(across == 0, 0.0, pltpu.roll(feature, 1, 0))
            after = jnp.where(across == width - 1, 0.0, pltpu.roll(feature, count - 1, 0))
            for ox, shifted in enumerate((before, feature, after)):
                packed = shifted.astype(BF16)
                for oy in range(3):
                    at = (oy * 3 + ox) * channels + c * LANES
                    taps[e * pixels : (e + 1) * pixels, at : at + LANES] = packed[
                        oy * width : oy * width + pixels
                    ]

    state = (decay0, inflow0, keep, block, open0, open1)
    cells_of(0, 0, taps, w_first, mask, short_rows, long_rows, send, pooled, state)
    for j in range(1, early):
        gate_copies[j - 1].wait()
        cells_of(j, j, taps, w_gates.at[j - 1], mask, short_rows, long_rows, send, pooled, state)
    for copy in gate_copies[early - 1 :]:
        copy.wait()


def gates_of(preact):
    quarter = LANES // 4
    lane = lax.broadcasted_iota(jnp.int32, (preact.shape[0], LANES), 1)
    spot = lane // quarter
    within = lane - spot * quarter
    sorted_ = []
    for i in range(4):
        gate = lax.rem(spot - i + 4, 4)
        sorted_.append(
            jnp.take_along_axis(preact[:, i * LANES : (i + 1) * LANES], 4 * within + gate, axis=1)
        )
    gates = []
    for g in range(4):
        out = sorted_[0]
        for i in range(1, 4):
            out = jnp.where(spot == (g + i) % 4, sorted_[i], out)
        gates.append(out if g == 0 else pltpu.roll(out, LANES - g * quarter, 1))
    return gates


def cells_of(j, at, taps, weights, mask, short_rows, long_rows, send, pooled, state):
    decay0, inflow0, keep, block, open0, open1 = state
    pixels = keep.shape[0]
    lanes = slice(at * LANES, (at + 1) * LANES)
    bias = long_rows[1:2, j * 4 * LANES : (j + 1) * 4 * LANES]
    rate = short_rows[4:5, j * LANES : (j + 1) * LANES]
    cell = None
    for e, opens in enumerate((open0, open1)):
        rows = slice(e * pixels, (e + 1) * pixels)
        preact = jnp.dot(taps[rows, :], weights[...], preferred_element_type=F32) + bias
        gate_in, gate_keep, gate_new, gate_out = gates_of(preact)
        good = mask[rows, :] > 0.5
        decay = jnp.where(good, jnp.exp(-rate * softplus(gate_keep)), 1.0)
        inflow = jnp.where(good, sigmoid(gate_in) * jnp.tanh(gate_new), 0.0)
        opened = sigmoid(gate_out)
        opens[:, lanes] = opened
        if e == 0:
            decay0[:, lanes] = decay
            inflow0[:, lanes] = inflow
            cell = inflow
        else:
            keep[:, lanes] = decay0[:, lanes] * decay
            cell = decay * inflow0[:, lanes] + inflow
            block[:, lanes] = cell
            if send is not None:
                send[:pixels, lanes] = cell.astype(BF16)
        if pooled is not None:
            pooled[e : e + 1, lanes] = pool(opened * jnp.tanh(cell))


def later_kernel(first, turn, count, sends, *refs):
    outs = refs[count:]
    if not sends:
        outs = (None,) + outs + (None,)
    on_devices(turn, lambda: later_work(first, *refs[:6], *outs))


def later_work(
    first,
    taps,
    w_gates,
    mask,
    short_rows,
    long_rows,
    pooled_early,
    send,
    decay0,
    inflow0,
    keep,
    block,
    open0,
    open1,
    pooled,
):
    channels = short_rows.shape[1]
    state = (decay0, inflow0, keep, block, open0, open1)
    for j in range(first, channels // LANES):
        at = j - first
        cells_of(j, at, taps, w_gates.at[at], mask, short_rows, long_rows, send, pooled, state)
    if send is None:
        return
    pixels = keep.shape[0]
    both = jnp.concatenate([pooled_early[0:2, :], pooled[0:2, :]], axis=1)
    own = tokens_of(both, short_rows[5:6, :])
    tail = (send.shape[0] - pixels) * LANES // channels
    known = jnp.zeros((tail, channels), F32)
    write_tail(send, pixels, put_tokens(known, own, 0))


def write_tail(send, pixels, tokens):
    tail, channels = tokens.shape
    for c in range(channels // LANES):
        at = pixels + c * tail
        send[at : at + tail, :] = tokens[:, c * LANES : (c + 1) * LANES].astype(BF16)


def read_tail(arrived, pixels, channels):
    tail = (arrived.shape[0] - pixels) * LANES // channels
    parts = [
        arrived[pixels + c * tail : pixels + (c + 1) * tail, :].astype(F32)
        for c in range(channels // LANES)
    ]
    return jnp.concatenate(parts, axis=1)


def run_block(tiles, early, turn, staged, recv_pair, recv_next, w_gates, kept, after):
    spread, mask, short_rows, long_rows, frames, dw_kernel, w_expand, w_reduce, w_first = staged
    epochs, height, width, channels = frames.shape
    pixels = height * width
    depth = w_gates.shape[0]
    vmem = pl.BlockSpec(memory_space=pltpu.VMEM)
    hbm = pl.BlockSpec(memory_space=pltpu.HBM)
    anywhere = pl.BlockSpec(memory_space=pl.ANY)
    near = early * LANES
    far = channels - near
    sends = not kept
    sent = [
        jax.ShapeDtypeStruct((pixels, near), BF16),
        jax.ShapeDtypeStruct((8, near), F32),
    ] * sends
    state = [jax.ShapeDtypeStruct((pixels, near), F32)] * 6
    flops = 2 * epochs * pixels * (2 * w_expand.size + w_gates.size)
    out = pl.pallas_call(
        functools.partial(block_kernel, tiles, turn, 12 + len(kept) + len(after), sends),
        name="block",
        out_shape=[
            *sent,
            *state,
            jax.ShapeDtypeStruct((epochs * pixels, depth), BF16),
            jax.ShapeDtypeStruct((far // LANES, depth, 4 * LANES), BF16),
        ],
        in_specs=[vmem] * 11 + [hbm] + [vmem] * len(kept) + [anywhere] * len(after),
        out_specs=[vmem] * (len(sent) + 8),
        input_output_aliases={12 + k: len(sent) + k for k in range(len(kept))},
        scratch_shapes=[
            pltpu.VMEM((channels // LANES, epochs, 2 * REACH, width + 16, LANES), F32),
            pltpu.VMEM((epochs, 2 * REACH * width, channels), F32),
            pltpu.VMEM((max(1, early - 1), depth, 4 * LANES), BF16),
            pltpu.SemaphoreType.DMA((channels // LANES - 1,)),
        ],
        compiler_params=pltpu.CompilerParams(vmem_limit_bytes=20 * 2**20),
        cost_estimate=pl.CostEstimate(flops=flops, bytes_accessed=2 * w_gates.size, transcendentals=0),
    )(
        spread,
        recv_pair,
        recv_next,
        frames,
        mask,
        short_rows,
        long_rows,
        dw_kernel,
        w_expand,
        w_reduce,
        w_first,
        pltpu.with_memory_space_constraint(w_gates, pltpu.HBM),
        *kept,
        *after,
    )
    return out[: len(sent)], out[len(sent) : -2], out[-2:]


def run_later(early, turn, staged, pooled, weighed, tail, kept, after):
    _, mask, short_rows, long_rows = staged[:4]
    taps, w_later = weighed
    pixels = taps.shape[0] // 2
    channels = short_rows.shape[1]
    far = channels - early * LANES
    vmem = pl.BlockSpec(memory_space=pltpu.VMEM)
    anywhere = pl.BlockSpec(memory_space=pl.ANY)
    sends = not kept
    sent = [jax.ShapeDtypeStruct((pixels + tail * channels // LANES, far), BF16)] * sends
    out = pl.pallas_call(
        functools.partial(later_kernel, early, turn, 6 + len(kept) + len(after), sends),
        name="later",
        out_shape=[*sent] + [jax.ShapeDtypeStruct((pixels, far), F32)] * 6,
        in_specs=[vmem] * 6 + [vmem] * len(kept) + [anywhere] * len(after),
        out_specs=[vmem] * (len(sent) + 6),
        input_output_aliases={6 + k: len(sent) + k for k in range(len(kept))},
        scratch_shapes=[pltpu.VMEM((8, far), F32)] * sends,
        compiler_params=pltpu.CompilerParams(vmem_limit_bytes=16 * 2**20),
        cost_estimate=pl.CostEstimate(flops=10**10, bytes_accessed=0, transcendentals=0),
    )(taps, w_later, mask, short_rows, long_rows, pooled, *kept, *after)
    return out[: len(sent)], out[len(sent) :]


def pool(memory):
    return jnp.mean(memory.astype(BF16).astype(F32), axis=0, keepdims=True)


def tokens_of(both, gain):
    center = jnp.mean(both, axis=-1, keepdims=True)
    centred = both - center
    variance = jnp.mean(centred * centred, axis=-1, keepdims=True)
    return (centred * lax.rsqrt(variance + 1e-06) * gain).astype(BF16).astype(F32)


def put_tokens(known, own, at):
    line = lax.broadcasted_iota(jnp.int32, known.shape, 0)
    return jnp.where(line == at, own[0:1], jnp.where(line == at + 1, own[1:2], known))


def step_cells(arrived, decay0, inflow0, keep, block):
    state = arrived[: keep.shape[0]].astype(F32)
    return decay0[...] * state + inflow0[...], keep[...] * state + block[...]


def relay_kernel(arrived, decay0, inflow0, keep, block, open0, open1, before, send, pooled):
    cell0, cell1 = step_cells(arrived, decay0, inflow0, keep, block)
    send[...] = cell1.astype(BF16)
    pooled[0:1, :] = pool(open0[...] * jnp.tanh(cell0))
    pooled[1:2, :] = pool(open1[...] * jnp.tanh(cell1))


def relay_later_kernel(
    stage, arrived, decay0, inflow0, keep, block, open0, open1, pooled_early, short_rows, send
):
    pixels = keep.shape[0]
    cell0, cell1 = step_cells(arrived, decay0, inflow0, keep, block)
    send[:pixels] = cell1.astype(BF16)
    pooled = jnp.concatenate(
        [pool(open0[...] * jnp.tanh(cell0)), pool(open1[...] * jnp.tanh(cell1))], axis=0
    )
    both = jnp.concatenate([pooled_early[0:2, :], pooled], axis=1)
    own = tokens_of(both, short_rows[5:6, :])
    known = read_tail(arrived, pixels, short_rows.shape[1])
    write_tail(send, pixels, put_tokens(known, own, 2 * stage))


def finish(arrived, state, memory):
    decay0, inflow0, keep, block, open0, open1 = state
    pixels = keep.shape[0]
    incoming = arrived[0][:pixels].astype(F32)
    for more in arrived[1:]:
        incoming = incoming + more[:pixels].astype(F32)
    cell0 = decay0[...] * incoming + inflow0[...]
    cell1 = keep[...] * incoming + block[...]
    pooled = []
    for e, (gate, cell) in enumerate(((open0, cell0), (open1, cell1))):
        out = (gate[...] * jnp.tanh(cell)).astype(BF16)
        memory[e] = out
        pooled.append(pool(out))
    return jnp.concatenate(pooled, axis=0)


def final_early_kernel(count, *refs):
    arrived, state = refs[:count], refs[count : count + 6]
    memory_hbm, pooled, head_of, channel_of, memory, sem = refs[count + 6 :]
    pooled[0:2, :] = finish(arrived, state, memory)
    copy = pltpu.make_async_copy(memory, memory_hbm.at[:, :, pl.ds(0, memory.shape[2])], sem)
    copy.start()
    channels, heads = head_of.shape
    depth = channels // heads
    member = lax.broadcasted_iota(jnp.int32, (channels, heads), 0) // depth
    head = lax.broadcasted_iota(jnp.int32, (channels, heads), 1)
    head_of[...] = jnp.where(member == head, 1.0, 0.0).astype(BF16)
    member = lax.broadcasted_iota(jnp.int32, (heads, channels), 1) // depth
    head = lax.broadcasted_iota(jnp.int32, (heads, channels), 0)
    channel_of[...] = jnp.where(member == head, 1.0, 0.0).astype(BF16)
    copy.wait()


def final_kernel(count, *refs):
    arrived, state = refs[:count], refs[count : count + 6]
    short_rows, months, slope, w_qkv, w_out, pooled_early, head_of, channel_of = refs[count + 6 : count + 14]
    memory_hbm, change, memory, sem = refs[count + 15 :]
    epochs, pixels, far = memory.shape
    channels = short_rows.shape[1]
    total = months.shape[0]
    pooled = finish(arrived, state, memory)
    copy = pltpu.make_async_copy(memory, memory_hbm.at[:, :, pl.ds(channels - far, far)], sem)
    copy.start()
    known = read_tail(arrived[0], pixels, channels)
    for more in arrived[1:]:
        known = known + read_tail(more, pixels, channels)
    both = jnp.concatenate([pooled_early[0:2, :], pooled], axis=1)
    own = tokens_of(both, short_rows[5:6, :])
    stage = lax.axis_index("epoch")
    tokens = put_tokens(known, own, 2 * stage).astype(BF16)
    heads = slope.shape[1]
    depth = channels // heads
    qkv = jnp.dot(tokens, w_qkv[...], preferred_element_type=F32).astype(BF16).astype(F32)[:total]
    queries = qkv[:, :channels]
    keys = qkv[:, channels : 2 * channels]
    values = qkv[:, 2 * channels :]
    def exact_dot(x, zero_one):
        high = x.astype(BF16)
        rest = x - high.astype(F32)
        low = rest.astype(BF16)
        least = (rest - low.astype(F32)).astype(BF16)
        out = jnp.dot(
            jnp.concatenate([high, low, least], axis=0), zero_one[...], preferred_element_type=F32
        )
        count = x.shape[0]
        return out[:count] + out[count : 2 * count] + out[2 * count :]

    line = lax.broadcasted_iota(jnp.int32, (total, channels), 0)
    key_index = lax.broadcasted_iota(jnp.int32, (total, heads), 0)
    month = months[:, :heads]
    places = [epochs * stage + step for step in range(epochs)]
    products = []
    for mine in places:
        query = jnp.sum(jnp.where(line == mine, queries, 0.0), axis=0, keepdims=True)
        products.append(query * keys)
    raw = exact_dot(jnp.concatenate(products, axis=0), head_of)
    weights = []
    for step, mine in enumerate(places):
        now = jnp.sum(jnp.where(key_index == mine, month, 0.0), axis=0, keepdims=True)
        scores = raw[step * total : (step + 1) * total] / math.sqrt(depth) - slope[...] * (now - month)
        scores = jnp.where(key_index <= mine, scores, -1e30)
        expo = jnp.exp(scores - jnp.max(scores, axis=0, keepdims=True))
        weights.append(expo / jnp.sum(expo, axis=0, keepdims=True))
    wide = exact_dot(jnp.concatenate(weights, axis=0), channel_of)
    results = [
        jnp.sum(wide[step * total : (step + 1) * total] * values, axis=0, keepdims=True)
        for step in range(epochs)
    ]
    mixed = jnp.concatenate(results, axis=0).astype(BF16)
    change[...] = jnp.dot(mixed, w_out[...], preferred_element_type=F32).astype(BF16)
    copy.wait()


def pairs(count, start):
    links = []
    for i in range(start, count - 1, 2):
        links += [(i, i + 1), (i + 1, i)]
    return links


def body(
    frames,
    valid,
    days,
    dw_kernel,
    dw_bias,
    norm_gain,
    norm_shift,
    w_expand,
    b_expand,
    w_reduce,
    layer_scale,
    w_gates,
    b_gates,
    forget_rate,
    attn_gain,
    w_query,
    w_key,
    w_value,
    w_out,
    head_slope,
):

    epochs, height, width, channels = frames.shape
    pixels = height * width
    tiles = lax.axis_size("tile")
    stages = lax.axis_size("epoch")
    total = epochs * stages
    tail = -(-total // 16) * 16
    gate_weights = w_gates.reshape(9 * channels, -1)
    near, to_pair, to_next = run_near(
        [
            frames,
            dw_kernel,
            valid,
            days,
            head_slope,
            b_expand,
            b_gates,
            dw_bias,
            norm_gain,
            norm_shift,
            layer_scale,
            forget_rate,
            attn_gain,
        ]
    )
    recv_pair = lax.ppermute(to_pair, "tile", pairs(tiles, 0))
    recv_next = lax.ppermute(to_next, "tile", pairs(tiles, 1))
    (
        spread,
        mask,
        short_rows,
        long_rows,
        months,
        slope,
        expand_near,
        reduce_near,
        w_first,
        qkv_near,
        out_near,
    ) = run_stage(near, w_expand, w_reduce, gate_weights, [w_query, w_key, w_value, w_out])
    early = max(1, channels // LANES - 1)
    staged = (spread, mask, short_rows, long_rows, near[0], near[1], expand_near, reduce_near, w_first)

    def blocks(turn, kept, after):
        return run_block(
            tiles, early, turn, staged, recv_pair, recv_next, gate_weights, kept, after
        )

    short_chain = 1 < stages <= 8
    first = (0, 1) if short_chain else None
    (send, pooled), state_near, weighed = blocks(first, [], [])
    (send_far,), state_far = run_later(early, first, staged, pooled, weighed, tail, [], [send])
    if short_chain:
        _, state_near, weighed = blocks((1, stages), state_near, [send_far])
        _, state_far = run_later(early, (1, 2), staged, pooled, weighed, tail, state_far, [])
    vmem = pl.BlockSpec(memory_space=pltpu.VMEM)
    params = pltpu.CompilerParams(vmem_limit_bytes=16 * 2**20)
    cost = pl.CostEstimate(flops=10**10, bytes_accessed=0, transcendentals=0)

    def relay(arrived, before):
        return pl.pallas_call(
            relay_kernel,
            name="relay",
            out_shape=[
                jax.ShapeDtypeStruct((pixels, early * LANES), BF16),
                jax.ShapeDtypeStruct((8, early * LANES), F32),
            ],
            in_specs=[vmem] * 7 + [pl.BlockSpec(memory_space=pl.ANY)],
            out_specs=[vmem] * 2,
            compiler_params=params,
            cost_estimate=cost,
        )(arrived, *state_near, before)

    def relay_later(stage, arrived, pooled, state_far):
        return pl.pallas_call(
            functools.partial(relay_later_kernel, stage),
            name="relay_later",
            out_shape=jax.ShapeDtypeStruct(send_far.shape, BF16),
            in_specs=[vmem] * 9,
            out_specs=vmem,
            compiler_params=params,
            cost_estimate=cost,
        )(arrived, *state_far, pooled, short_rows)

    arrived = []
    arrived_far = []
    if stages <= 8:
        for stage in range(stages - 1):
            link = [(stage, stage + 1)]
            if stage > 0:
                send, pooled = relay(arrived[-1], send_far)
                if stage == 1 and stages > 2:
                    _, state_far = run_later(
                        early, (2, stages), staged, pooled, weighed, tail, state_far, [send]
                    )
                send_far = relay_later(stage, arrived_far[-1], pooled, state_far)
            arrived.append(lax.ppermute(send, "epoch", link))
            arrived_far.append(lax.ppermute(send_far, "epoch", link))
    else:
        chain = [(i, i + 1) for i in range(stages - 1)]

        def along(state, width):
            keep, block = state[2], state[3]

            def turn(_, arriving):
                out = (keep * arriving.astype(F32) + block).astype(BF16)
                return lax.ppermute(out, "epoch", chain)

            return lax.fori_loop(0, stages - 1, turn, jnp.zeros((pixels, width), BF16))

        def unfold(tokens):
            parts = jnp.split(tokens, channels // LANES, axis=1)
            return jnp.concatenate(parts, axis=0)

        incoming = along(state_near, early * LANES)
        incoming_far = along(state_far, channels - early * LANES)
        _, pooled = relay(incoming, send_far)
        blank = jnp.zeros((tail * channels // LANES, LANES), BF16)
        told = relay_later(0, jnp.concatenate([incoming_far, blank]), pooled, state_far)[pixels:]
        told = jnp.concatenate(jnp.split(told, channels // LANES, axis=0), axis=1)
        known = lax.all_gather(told[:epochs], "epoch", axis=0, tiled=True)
        known = jnp.concatenate([known, jnp.zeros((tail - total, channels), BF16)])
        arrived.append(incoming)
        arrived_far.append(jnp.concatenate([incoming_far, unfold(known)]))

    hbm = pl.BlockSpec(memory_space=pltpu.HBM)
    heads = head_slope.size
    memory, pooled, head_of, channel_of = pl.pallas_call(
        functools.partial(final_early_kernel, len(arrived)),
        name="final_early",
        out_shape=[
            jax.ShapeDtypeStruct((epochs, pixels, channels), BF16),
            jax.ShapeDtypeStruct((8, early * LANES), F32),
            jax.ShapeDtypeStruct((channels, heads), BF16),
            jax.ShapeDtypeStruct((heads, channels), BF16),
        ],
        in_specs=[vmem] * (len(arrived) + 6),
        out_specs=[hbm] + [vmem] * 3,
        scratch_shapes=[
            pltpu.VMEM((epochs, pixels, early * LANES), BF16),
            pltpu.SemaphoreType.DMA,
        ],
        compiler_params=params,
        cost_estimate=cost,
    )(*arrived, *state_near)
    memory, change = pl.pallas_call(
        functools.partial(final_kernel, len(arrived)),
        name="final",
        out_shape=[
            jax.ShapeDtypeStruct((epochs, pixels, channels), BF16),
            jax.ShapeDtypeStruct((epochs, channels), BF16),
        ],
        in_specs=[vmem] * (len(arrived) + 14) + [hbm],
        out_specs=[hbm, vmem],
        input_output_aliases={len(arrived) + 14: 0},
        scratch_shapes=[
            pltpu.VMEM((epochs, pixels, channels - early * LANES), BF16),
            pltpu.SemaphoreType.DMA,
        ],
        compiler_params=pltpu.CompilerParams(vmem_limit_bytes=24 * 2**20),
    )(
        *arrived_far,
        *state_far,
        short_rows,
        months,
        slope,
        qkv_near,
        out_near,
        pooled,
        head_of,
        channel_of,
        pltpu.with_memory_space_constraint(memory, pltpu.HBM),
    )
    return (
        memory.reshape(epochs, height, width, channels),
        change.reshape(epochs, 1, 1, channels),
    )


def solution(mesh):
    placed = (
        P("epoch", ("groups", "tile"), None, None),
        P("epoch", ("groups", "tile"), None),
        P("groups"),
    ) + (P(),) * 17
    return jax.shard_map(
        body,
        mesh=mesh,
        in_specs=placed,
        out_specs=(
            P("epoch", ("groups", "tile"), None, None),
            P("epoch", ("groups", "tile"), None, None),
        ),
        check_vma=False,
    )
```

```python
import functools
import math

import jax
import jax.numpy as jnp
from jax import lax
from jax.experimental import pallas as pl
from jax.experimental.pallas import tpu as pltpu
from jax.sharding import PartitionSpec as P

PATCH = 16
REACH = 4
LANES = 128
F32 = jnp.float32
BF16 = jnp.bfloat16


def sigmoid(x):
    return 0.5 * jnp.tanh(0.5 * x) + 0.5


def softplus(x):
    return jnp.maximum(x, 0.0) + jnp.log(1.0 + jnp.exp(-jnp.abs(x)))


def gelu_twice(x):
    inner = x * (0.7978845608028654 + (0.7978845608028654 * 0.044715) * (x * x))
    return x + x * jnp.tanh(inner)


def near_kernel(*refs):
    count = len(refs) // 2 - 1
    sources, outs = refs[:count], refs[count : 2 * count]
    to_pair, to_next, sems = refs[2 * count :]
    copies = [pltpu.make_async_copy(a, b, sems.at[i]) for i, (a, b) in enumerate(zip(sources, outs))]
    for copy in copies:
        copy.start()
    copies[0].wait()
    frames = outs[0]
    bottom = frames.shape[1] - REACH
    odd = lax.rem(lax.axis_index("tile"), 2)
    to_pair[...] = frames[:, pl.ds((1 - odd) * bottom, REACH)]
    to_next[...] = frames[:, pl.ds(odd * bottom, REACH)]
    for copy in copies[1:]:
        copy.wait()


def run_near(arrays):
    frames = arrays[0]
    rim = jax.ShapeDtypeStruct((frames.shape[0], REACH) + frames.shape[2:], frames.dtype)
    hbm = pl.BlockSpec(memory_space=pltpu.HBM)
    vmem = pl.BlockSpec(memory_space=pltpu.VMEM)
    out = pl.pallas_call(
        near_kernel,
        name="near",
        out_shape=[jax.ShapeDtypeStruct(x.shape, x.dtype) for x in arrays] + [rim] * 2,
        in_specs=[hbm] * len(arrays),
        out_specs=[vmem] * (len(arrays) + 2),
        scratch_shapes=[pltpu.SemaphoreType.DMA((len(arrays),))],
        compiler_params=pltpu.CompilerParams(vmem_limit_bytes=16 * 2**20),
    )(*[pltpu.with_memory_space_constraint(x, pltpu.HBM) for x in arrays])
    return out[: len(arrays)], out[-2], out[-1]


def stage_kernel(
    frames,
    dw_kernel,
    valid,
    days,
    slope_line,
    b_expand,
    b_gates,
    dw_bias,
    norm_gain,
    norm_shift,
    layer_scale,
    forget_rate,
    attn_gain,
    w_expand_hbm,
    w_reduce_hbm,
    w_gates_hbm,
    w_query_hbm,
    w_key_hbm,
    w_value_hbm,
    w_out_hbm,
    spread,
    mask,
    short_rows,
    long_rows,
    months,
    slope,
    w_expand,
    w_reduce,
    w_first,
    w_qkv,
    w_out,
    padded,
    sems,
):
    epochs, height, width, channels = frames.shape
    groups = channels // LANES
    rows = height + 2
    pixels = height * width
    moves = [
        (w_expand_hbm, w_expand),
        (w_reduce_hbm, w_reduce),
        (w_gates_hbm.at[:, pl.ds(0, w_first.shape[1])], w_first),
        (w_query_hbm, w_qkv.at[:, pl.ds(0, channels)]),
        (w_key_hbm, w_qkv.at[:, pl.ds(channels, channels)]),
        (w_value_hbm, w_qkv.at[:, pl.ds(2 * channels, channels)]),
        (w_out_hbm, w_out),
    ]
    copies = [pltpu.make_async_copy(a, b, sems.at[i]) for i, (a, b) in enumerate(moves)]
    for copy in copies:
        copy.start()

    for c in range(groups):
        for e in range(epochs):
            lanes = slice(c * LANES, (c + 1) * LANES)
            padded[c, e, :, 0:8, :] = jnp.zeros((height, 8, LANES), F32)
            padded[c, e, :, 8 + width : 16 + width, :] = jnp.zeros((height, 8, LANES), F32)
            padded[c, e, :, 8 : 8 + width, :] = frames[e, :, :, lanes].astype(F32)

    half = rows // 2

    def depthwise(index, carry):
        c = index // epochs
        e = index - c * epochs
        lanes = pl.ds(pl.multiple_of(c * LANES, LANES), LANES)
        for part in range(2):
            total = [None] * half
            for ox in range(7):
                factors = [dw_kernel[oy, pl.ds(ox, 1), lanes] for oy in range(7)]
                for r in range(height):
                    at = [(y, r + REACH - (part * half + y)) for y in range(half)]
                    at = [(y, oy) for y, oy in at if 0 <= oy < 7]
                    if not at:
                        continue
                    window = padded[c, e, r, pl.ds(5 + ox, width), :]
                    for y, oy in at:
                        term = window * factors[oy]
                        total[y] = term if total[y] is None else total[y] + term
            for y in range(half):
                line = (part * half + y) * width
                spread[e, pl.ds(line, width), lanes] = total[y]
        return carry

    lax.fori_loop(0, groups * epochs, depthwise, 0)

    short = (dw_bias, norm_gain, norm_shift, layer_scale, forget_rate, attn_gain)
    for k, line in enumerate(short):
        short_rows[k : k + 1, :] = line[...].reshape(1, -1)
    for k, line in enumerate((b_expand, b_gates)):
        long_rows[k : k + 1, :] = line[...].reshape(1, -1)
    slope[...] = slope_line[...].reshape(1, -1)
    total = days.shape[0]
    eye = lax.broadcasted_iota(jnp.int32, (total, total), 0) == lax.broadcasted_iota(
        jnp.int32, (total, total), 1
    )
    month = days[...].astype(F32).reshape(1, -1) / 30.0
    months[...] = jnp.broadcast_to(
        jnp.sum(jnp.where(eye, month, 0.0), axis=1, keepdims=True), months.shape
    )
    down = lax.broadcasted_iota(jnp.int32, (pixels, height), 0) // width
    pick = jnp.where(down == lax.broadcasted_iota(jnp.int32, (pixels, height), 1), 1.0, 0.0).astype(BF16)
    side = lax.rem(lax.broadcasted_iota(jnp.int32, (pixels, width), 0), width)
    place = side == lax.broadcasted_iota(jnp.int32, (pixels, width), 1)
    ones = jnp.ones((width, LANES), BF16)
    for e in range(epochs):
        plane = jnp.where(valid[e] > 0, 1.0, 0.0).astype(BF16)
        lines = jnp.dot(pick, plane, preferred_element_type=F32)
        mask[e * pixels : (e + 1) * pixels, :] = jnp.dot(
            jnp.where(place, lines, 0.0).astype(BF16), ones, preferred_element_type=F32
        )
    for copy in copies:
        copy.wait()


def run_stage(near, w_expand, w_reduce, w_gates, w_qkvo):
    frames, dw_kernel, valid, days, slope = near[:5]
    epochs, height, width, channels = frames.shape
    pixels = height * width
    total = days.shape[0]
    far = [w_expand, w_reduce, w_gates, *w_qkvo]
    hbm = pl.BlockSpec(memory_space=pltpu.HBM)
    vmem = pl.BlockSpec(memory_space=pltpu.VMEM)
    out_shape = [
        jax.ShapeDtypeStruct((epochs, (height + 2) * width, channels), F32),
        jax.ShapeDtypeStruct((epochs * pixels, LANES), F32),
        jax.ShapeDtypeStruct((8, channels), F32),
        jax.ShapeDtypeStruct((8, w_gates.shape[1]), F32),
        jax.ShapeDtypeStruct((total, LANES), F32),
        jax.ShapeDtypeStruct((1, slope.size), F32),
        jax.ShapeDtypeStruct(w_expand.shape, BF16),
        jax.ShapeDtypeStruct(w_reduce.shape, BF16),
        jax.ShapeDtypeStruct((w_gates.shape[0], 4 * LANES), BF16),
        jax.ShapeDtypeStruct((channels, 3 * channels), BF16),
        jax.ShapeDtypeStruct((channels, channels), BF16),
    ]
    return pl.pallas_call(
        stage_kernel,
        name="stage",
        out_shape=out_shape,
        in_specs=[vmem] * len(near) + [hbm] * len(far),
        out_specs=[vmem] * len(out_shape),
        scratch_shapes=[
            pltpu.VMEM((channels // LANES, epochs, height, width + 16, LANES), F32),
            pltpu.SemaphoreType.DMA((len(far),)),
        ],
        compiler_params=pltpu.CompilerParams(vmem_limit_bytes=24 * 2**20),
        cost_estimate=pl.CostEstimate(
            flops=10**10, bytes_accessed=8 * w_expand.size, transcendentals=0
        ),
    )(*near, *[pltpu.with_memory_space_constraint(x, pltpu.HBM) for x in far])


def on_devices(turn, work):
    if turn is None:
        work()
    else:
        stage = lax.axis_index("epoch")
        pl.when((stage >= turn[0]) & (stage < turn[1]))(work)


def block_kernel(tiles, turn, count, sends, *refs):
    outs = refs[count:]
    if not sends:
        outs = (None, None) + outs
    on_devices(turn, lambda: block_work(tiles, *refs[:12], *outs))


def block_work(
    tiles,
    spread,
    recv_pair,
    recv_next,
    frames,
    mask,
    short_rows,
    long_rows,
    dw_kernel,
    w_expand,
    w_reduce,
    w_first,
    w_gates_hbm,
    send,
    pooled,
    decay0,
    inflow0,
    keep,
    block,
    open0,
    open1,
    taps,
    w_later,
    rim,
    edge,
    w_gates,
    sems,
):
    epochs, height, width, channels = frames.shape
    groups = channels // LANES
    rows = height + 2
    pixels = height * width
    wide = 4 * LANES

    early = keep.shape[1] // LANES
    places = [w_gates.at[j] for j in range(early - 1)] + [w_later.at[j] for j in range(groups - early)]
    gate_copies = [
        pltpu.make_async_copy(w_gates_hbm.at[:, pl.ds((j + 1) * wide, wide)], place, sems.at[j])
        for j, place in enumerate(places)
    ]
    for copy in gate_copies:
        copy.start()

    dw_bias = short_rows[0:1, :]
    norm_gain = short_rows[1:2, :]
    norm_shift = short_rows[2:3, :]
    half_scale = 0.5 * short_rows[3:4, :]
    b_expand = long_rows[0:1, :]

    me = lax.axis_index("tile")
    odd = lax.rem(me, 2)
    pair_row = (1 - odd) * REACH
    next_row = odd * REACH

    for c in range(groups):
        lanes = slice(c * LANES, (c + 1) * LANES)
        for e in range(epochs):
            rim[c, e, :, 0:8, :] = jnp.zeros((2 * REACH, 8, LANES), F32)
            rim[c, e, :, 8 + width : 16 + width, :] = jnp.zeros((2 * REACH, 8, LANES), F32)
            rim[c, e, pl.ds(pair_row, REACH), 8 : 8 + width, :] = recv_pair[e, :, :, lanes].astype(F32)
            rim[c, e, pl.ds(next_row, REACH), 8 : 8 + width, :] = recv_next[e, :, :, lanes].astype(F32)

    def depthwise(index, carry):
        c = index // epochs
        e = index - c * epochs
        lanes = pl.ds(pl.multiple_of(c * LANES, LANES), LANES)
        total = [None] * (2 * REACH)
        for ox in range(7):
            factors = [dw_kernel[oy, pl.ds(ox, 1), lanes] for oy in range(7)]
            for k in range(REACH):
                above = rim[c, e, k, pl.ds(5 + ox, width), :]
                below = rim[c, e, REACH + k, pl.ds(5 + ox, width), :]
                for y in range(k + 1):
                    term = above * factors[k - y]
                    total[y] = term if total[y] is None else total[y] + term
                for y in range(k, REACH):
                    term = below * factors[6 + k - y]
                    at = REACH + y
                    total[at] = term if total[at] is None else total[at] + term
        for y in range(2 * REACH):
            edge[e, pl.ds(y * width, width), lanes] = total[y]
        return carry

    lax.fori_loop(0, groups * epochs, depthwise, 0)

    count = rows * width
    rimmed = REACH * width
    column = lax.broadcasted_iota(jnp.int32, (count, LANES), 0)
    across = lax.rem(column, width)
    line = column // width
    first = jnp.where(me == 0, 1, 0)
    last = jnp.where(me == tiles - 1, rows - 2, rows - 1)
    inside = jnp.where((line >= first) & (line <= last), 1.0, 0.0)
    for e in range(epochs):
        values = (
            jnp.concatenate(
                [
                    spread[e, :rimmed] + edge[e, :rimmed],
                    spread[e, rimmed : count - rimmed],
                    spread[e, count - rimmed :] + edge[e, rimmed:],
                ],
                axis=0,
            )
            + dw_bias
        )
        center = jnp.mean(values, axis=-1, keepdims=True)
        centred = values - center
        variance = jnp.mean(centred * centred, axis=-1, keepdims=True)
        normed = (centred * lax.rsqrt(variance + 1e-06) * norm_gain + norm_shift).astype(BF16)
        grown = jnp.dot(normed, w_expand[...], preferred_element_type=F32) + b_expand
        reduced = jnp.dot(gelu_twice(grown).astype(BF16), w_reduce[...], preferred_element_type=F32)
        for c in range(groups):
            lanes = slice(c * LANES, (c + 1) * LANES)
            centre = jnp.concatenate(
                [
                    rim[c, e, REACH - 1, 8 : 8 + width, :],
                    frames[e, :, :, lanes].astype(F32).reshape(pixels, LANES),
                    rim[c, e, REACH, 8 : 8 + width, :],
                ],
                axis=0,
            )
            feature = centre + half_scale[:, lanes] * reduced[:, lanes]
            feature = (feature * inside).astype(BF16).astype(F32)
            before = jnp.where(across == 0, 0.0, pltpu.roll(feature, 1, 0))
            after = jnp.where(across == width - 1, 0.0, pltpu.roll(feature, count - 1, 0))
            for ox, shifted in enumerate((before, feature, after)):
                packed = shifted.astype(BF16)
                for oy in range(3):
                    at = (oy * 3 + ox) * channels + c * LANES
                    taps[e * pixels : (e + 1) * pixels, at : at + LANES] = packed[
                        oy * width : oy * width + pixels
                    ]

    state = (decay0, inflow0, keep, block, open0, open1)
    cells_of(0, 0, taps, w_first, mask, short_rows, long_rows, send, pooled, state)
    for j in range(1, early):
        gate_copies[j - 1].wait()
        cells_of(j, j, taps, w_gates.at[j - 1], mask, short_rows, long_rows, send, pooled, state)
    for copy in gate_copies[early - 1 :]:
        copy.wait()


def gates_of(preact):
    quarter = LANES // 4
    lane = lax.broadcasted_iota(jnp.int32, (preact.shape[0], LANES), 1)
    spot = lane // quarter
    within = lane - spot * quarter
    sorted_ = []
    for i in range(4):
        gate = lax.rem(spot - i + 4, 4)
        sorted_.append(
            jnp.take_along_axis(preact[:, i * LANES : (i + 1) * LANES], 4 * within + gate, axis=1)
        )
    gates = []
    for g in range(4):
        out = sorted_[0]
        for i in range(1, 4):
            out = jnp.where(spot == (g + i) % 4, sorted_[i], out)
        gates.append(out if g == 0 else pltpu.roll(out, LANES - g * quarter, 1))
    return gates


def cells_of(j, at, taps, weights, mask, short_rows, long_rows, send, pooled, state):
    decay0, inflow0, keep, block, open0, open1 = state
    pixels = keep.shape[0]
    lanes = slice(at * LANES, (at + 1) * LANES)
    bias = long_rows[1:2, j * 4 * LANES : (j + 1) * 4 * LANES]
    rate = short_rows[4:5, j * LANES : (j + 1) * LANES]
    cell = None
    for e, opens in enumerate((open0, open1)):
        rows = slice(e * pixels, (e + 1) * pixels)
        preact = jnp.dot(taps[rows, :], weights[...], preferred_element_type=F32) + bias
        gate_in, gate_keep, gate_new, gate_out = gates_of(preact)
        good = mask[rows, :] > 0.5
        decay = jnp.where(good, jnp.exp(-rate * softplus(gate_keep)), 1.0)
        inflow = jnp.where(good, sigmoid(gate_in) * jnp.tanh(gate_new), 0.0)
        opened = sigmoid(gate_out)
        opens[:, lanes] = opened
        if e == 0:
            decay0[:, lanes] = decay
            inflow0[:, lanes] = inflow
            cell = inflow
        else:
            keep[:, lanes] = decay0[:, lanes] * decay
            cell = decay * inflow0[:, lanes] + inflow
            block[:, lanes] = cell
            if send is not None:
                send[:pixels, lanes] = cell.astype(BF16)
        if pooled is not None:
            pooled[e : e + 1, lanes] = pool(opened * jnp.tanh(cell))


def later_kernel(first, turn, count, sends, *refs):
    outs = refs[count:]
    if not sends:
        outs = (None,) + outs + (None,)
    on_devices(turn, lambda: later_work(first, *refs[:6], *outs))


def later_work(
    first,
    taps,
    w_gates,
    mask,
    short_rows,
    long_rows,
    pooled_early,
    send,
    decay0,
    inflow0,
    keep,
    block,
    open0,
    open1,
    pooled,
):
    channels = short_rows.shape[1]
    state = (decay0, inflow0, keep, block, open0, open1)
    for j in range(first, channels // LANES):
        at = j - first
        cells_of(j, at, taps, w_gates.at[at], mask, short_rows, long_rows, send, pooled, state)
    if send is None:
        return
    pixels = keep.shape[0]
    both = jnp.concatenate([pooled_early[0:2, :], pooled[0:2, :]], axis=1)
    own = tokens_of(both, short_rows[5:6, :])
    tail = (send.shape[0] - pixels) * LANES // channels
    known = jnp.zeros((tail, channels), F32)
    write_tail(send, pixels, put_tokens(known, own, 0))


def write_tail(send, pixels, tokens):
    tail, channels = tokens.shape
    for c in range(channels // LANES):
        at = pixels + c * tail
        send[at : at + tail, :] = tokens[:, c * LANES : (c + 1) * LANES].astype(BF16)


def read_tail(arrived, pixels, channels):
    tail = (arrived.shape[0] - pixels) * LANES // channels
    parts = [
        arrived[pixels + c * tail : pixels + (c + 1) * tail, :].astype(F32)
        for c in range(channels // LANES)
    ]
    return jnp.concatenate(parts, axis=1)


def run_block(tiles, early, turn, staged, recv_pair, recv_next, w_gates, kept, after):
    spread, mask, short_rows, long_rows, frames, dw_kernel, w_expand, w_reduce, w_first = staged
    epochs, height, width, channels = frames.shape
    pixels = height * width
    depth = w_gates.shape[0]
    vmem = pl.BlockSpec(memory_space=pltpu.VMEM)
    hbm = pl.BlockSpec(memory_space=pltpu.HBM)
    anywhere = pl.BlockSpec(memory_space=pl.ANY)
    near = early * LANES
    far = channels - near
    sends = not kept
    sent = [
        jax.ShapeDtypeStruct((pixels, near), BF16),
        jax.ShapeDtypeStruct((8, near), F32),
    ] * sends
    state = [jax.ShapeDtypeStruct((pixels, near), F32)] * 6
    flops = 2 * epochs * pixels * (2 * w_expand.size + w_gates.size)
    out = pl.pallas_call(
        functools.partial(block_kernel, tiles, turn, 12 + len(kept) + len(after), sends),
        name="block",
        out_shape=[
            *sent,
            *state,
            jax.ShapeDtypeStruct((epochs * pixels, depth), BF16),
            jax.ShapeDtypeStruct((far // LANES, depth, 4 * LANES), BF16),
        ],
        in_specs=[vmem] * 11 + [hbm] + [vmem] * len(kept) + [anywhere] * len(after),
        out_specs=[vmem] * (len(sent) + 8),
        input_output_aliases={12 + k: len(sent) + k for k in range(len(kept))},
        scratch_shapes=[
            pltpu.VMEM((channels // LANES, epochs, 2 * REACH, width + 16, LANES), F32),
            pltpu.VMEM((epochs, 2 * REACH * width, channels), F32),
            pltpu.VMEM((max(1, early - 1), depth, 4 * LANES), BF16),
            pltpu.SemaphoreType.DMA((channels // LANES - 1,)),
        ],
        compiler_params=pltpu.CompilerParams(vmem_limit_bytes=20 * 2**20),
        cost_estimate=pl.CostEstimate(flops=flops, bytes_accessed=2 * w_gates.size, transcendentals=0),
    )(
        spread,
        recv_pair,
        recv_next,
        frames,
        mask,
        short_rows,
        long_rows,
        dw_kernel,
        w_expand,
        w_reduce,
        w_first,
        pltpu.with_memory_space_constraint(w_gates, pltpu.HBM),
        *kept,
        *after,
    )
    return out[: len(sent)], out[len(sent) : -2], out[-2:]


def run_later(early, turn, staged, pooled, weighed, tail, kept, after):
    _, mask, short_rows, long_rows = staged[:4]
    taps, w_later = weighed
    pixels = taps.shape[0] // 2
    channels = short_rows.shape[1]
    far = channels - early * LANES
    vmem = pl.BlockSpec(memory_space=pltpu.VMEM)
    anywhere = pl.BlockSpec(memory_space=pl.ANY)
    sends = not kept
    sent = [jax.ShapeDtypeStruct((pixels + tail * channels // LANES, far), BF16)] * sends
    out = pl.pallas_call(
        functools.partial(later_kernel, early, turn, 6 + len(kept) + len(after), sends),
        name="later",
        out_shape=[*sent] + [jax.ShapeDtypeStruct((pixels, far), F32)] * 6,
        in_specs=[vmem] * 6 + [vmem] * len(kept) + [anywhere] * len(after),
        out_specs=[vmem] * (len(sent) + 6),
        input_output_aliases={6 + k: len(sent) + k for k in range(len(kept))},
        scratch_shapes=[pltpu.VMEM((8, far), F32)] * sends,
        compiler_params=pltpu.CompilerParams(vmem_limit_bytes=16 * 2**20),
        cost_estimate=pl.CostEstimate(flops=10**10, bytes_accessed=0, transcendentals=0),
    )(taps, w_later, mask, short_rows, long_rows, pooled, *kept, *after)
    return out[: len(sent)], out[len(sent) :]


def pool(memory):
    return jnp.mean(memory.astype(BF16).astype(F32), axis=0, keepdims=True)


def tokens_of(both, gain):
    center = jnp.mean(both, axis=-1, keepdims=True)
    centred = both - center
    variance = jnp.mean(centred * centred, axis=-1, keepdims=True)
    return (centred * lax.rsqrt(variance + 1e-06) * gain).astype(BF16).astype(F32)


def put_tokens(known, own, at):
    line = lax.broadcasted_iota(jnp.int32, known.shape, 0)
    return jnp.where(line == at, own[0:1], jnp.where(line == at + 1, own[1:2], known))


def step_cells(arrived, decay0, inflow0, keep, block):
    state = arrived[: keep.shape[0]].astype(F32)
    return decay0[...] * state + inflow0[...], keep[...] * state + block[...]


def relay_kernel(arrived, decay0, inflow0, keep, block, open0, open1, before, send, pooled):
    cell0, cell1 = step_cells(arrived, decay0, inflow0, keep, block)
    send[...] = cell1.astype(BF16)
    pooled[0:1, :] = pool(open0[...] * jnp.tanh(cell0))
    pooled[1:2, :] = pool(open1[...] * jnp.tanh(cell1))


def relay_later_kernel(
    stage, arrived, decay0, inflow0, keep, block, open0, open1, pooled_early, short_rows, send
):
    pixels = keep.shape[0]
    cell0, cell1 = step_cells(arrived, decay0, inflow0, keep, block)
    send[:pixels] = cell1.astype(BF16)
    pooled = jnp.concatenate(
        [pool(open0[...] * jnp.tanh(cell0)), pool(open1[...] * jnp.tanh(cell1))], axis=0
    )
    both = jnp.concatenate([pooled_early[0:2, :], pooled], axis=1)
    own = tokens_of(both, short_rows[5:6, :])
    known = read_tail(arrived, pixels, short_rows.shape[1])
    write_tail(send, pixels, put_tokens(known, own, 2 * stage))


def finish(arrived, state, memory):
    decay0, inflow0, keep, block, open0, open1 = state
    pixels = keep.shape[0]
    incoming = arrived[0][:pixels].astype(F32)
    for more in arrived[1:]:
        incoming = incoming + more[:pixels].astype(F32)
    cell0 = decay0[...] * incoming + inflow0[...]
    cell1 = keep[...] * incoming + block[...]
    pooled = []
    for e, (gate, cell) in enumerate(((open0, cell0), (open1, cell1))):
        out = (gate[...] * jnp.tanh(cell)).astype(BF16)
        memory[e] = out
        pooled.append(pool(out))
    return jnp.concatenate(pooled, axis=0)


def final_early_kernel(count, *refs):
    arrived, state = refs[:count], refs[count : count + 6]
    memory_hbm, pooled, head_of, channel_of, memory, sem = refs[count + 6 :]
    pooled[0:2, :] = finish(arrived, state, memory)
    copy = pltpu.make_async_copy(memory, memory_hbm.at[:, :, pl.ds(0, memory.shape[2])], sem)
    copy.start()
    channels, heads = head_of.shape
    depth = channels // heads
    member = lax.broadcasted_iota(jnp.int32, (channels, heads), 0) // depth
    head = lax.broadcasted_iota(jnp.int32, (channels, heads), 1)
    head_of[...] = jnp.where(member == head, 1.0, 0.0).astype(BF16)
    member = lax.broadcasted_iota(jnp.int32, (heads, channels), 1) // depth
    head = lax.broadcasted_iota(jnp.int32, (heads, channels), 0)
    channel_of[...] = jnp.where(member == head, 1.0, 0.0).astype(BF16)
    copy.wait()


def final_kernel(count, *refs):
    arrived, state = refs[:count], refs[count : count + 6]
    short_rows, months, slope, w_qkv, w_out, pooled_early, head_of, channel_of = refs[count + 6 : count + 14]
    memory_hbm, change, memory, sem = refs[count + 15 :]
    epochs, pixels, far = memory.shape
    channels = short_rows.shape[1]
    total = months.shape[0]
    pooled = finish(arrived, state, memory)
    copy = pltpu.make_async_copy(memory, memory_hbm.at[:, :, pl.ds(channels - far, far)], sem)
    copy.start()
    known = read_tail(arrived[0], pixels, channels)
    for more in arrived[1:]:
        known = known + read_tail(more, pixels, channels)
    both = jnp.concatenate([pooled_early[0:2, :], pooled], axis=1)
    own = tokens_of(both, short_rows[5:6, :])
    stage = lax.axis_index("epoch")
    tokens = put_tokens(known, own, 2 * stage).astype(BF16)
    heads = slope.shape[1]
    depth = channels // heads
    qkv = jnp.dot(tokens, w_qkv[...], preferred_element_type=F32).astype(BF16).astype(F32)[:total]
    queries = qkv[:, :channels]
    keys = qkv[:, channels : 2 * channels]
    values = qkv[:, 2 * channels :]
    def exact_dot(x, zero_one):
        high = x.astype(BF16)
        rest = x - high.astype(F32)
        low = rest.astype(BF16)
        least = (rest - low.astype(F32)).astype(BF16)
        out = jnp.dot(
            jnp.concatenate([high, low, least], axis=0), zero_one[...], preferred_element_type=F32
        )
        count = x.shape[0]
        return out[:count] + out[count : 2 * count] + out[2 * count :]

    line = lax.broadcasted_iota(jnp.int32, (total, channels), 0)
    key_index = lax.broadcasted_iota(jnp.int32, (total, heads), 0)
    month = months[:, :heads]
    places = [epochs * stage + step for step in range(epochs)]
    products = []
    for mine in places:
        query = jnp.sum(jnp.where(line == mine, queries, 0.0), axis=0, keepdims=True)
        products.append(query * keys)
    raw = exact_dot(jnp.concatenate(products, axis=0), head_of)
    weights = []
    for step, mine in enumerate(places):
        now = jnp.sum(jnp.where(key_index == mine, month, 0.0), axis=0, keepdims=True)
        scores = raw[step * total : (step + 1) * total] / math.sqrt(depth) - slope[...] * (now - month)
        scores = jnp.where(key_index <= mine, scores, -1e30)
        expo = jnp.exp(scores - jnp.max(scores, axis=0, keepdims=True))
        weights.append(expo / jnp.sum(expo, axis=0, keepdims=True))
    wide = exact_dot(jnp.concatenate(weights, axis=0), channel_of)
    results = [
        jnp.sum(wide[step * total : (step + 1) * total] * values, axis=0, keepdims=True)
        for step in range(epochs)
    ]
    mixed = jnp.concatenate(results, axis=0).astype(BF16)
    change[...] = jnp.dot(mixed, w_out[...], preferred_element_type=F32).astype(BF16)
    copy.wait()


def pairs(count, start):
    links = []
    for i in range(start, count - 1, 2):
        links += [(i, i + 1), (i + 1, i)]
    return links


def body(
    frames,
    valid,
    days,
    dw_kernel,
    dw_bias,
    norm_gain,
    norm_shift,
    w_expand,
    b_expand,
    w_reduce,
    layer_scale,
    w_gates,
    b_gates,
    forget_rate,
    attn_gain,
    w_query,
    w_key,
    w_value,
    w_out,
    head_slope,
):

    epochs, height, width, channels = frames.shape
    pixels = height * width
    tiles = lax.axis_size("tile")
    stages = lax.axis_size("epoch")
    total = epochs * stages
    tail = -(-total // 16) * 16
    gate_weights = w_gates.reshape(9 * channels, -1)
    near, to_pair, to_next = run_near(
        [
            frames,
            dw_kernel,
            valid,
            days,
            head_slope,
            b_expand,
            b_gates,
            dw_bias,
            norm_gain,
            norm_shift,
            layer_scale,
            forget_rate,
            attn_gain,
        ]
    )
    recv_pair = lax.ppermute(to_pair, "tile", pairs(tiles, 0))
    recv_next = lax.ppermute(to_next, "tile", pairs(tiles, 1))
    (
        spread,
        mask,
        short_rows,
        long_rows,
        months,
        slope,
        expand_near,
        reduce_near,
        w_first,
        qkv_near,
        out_near,
    ) = run_stage(near, w_expand, w_reduce, gate_weights, [w_query, w_key, w_value, w_out])
    early = max(1, channels // LANES - 1)
    staged = (spread, mask, short_rows, long_rows, near[0], near[1], expand_near, reduce_near, w_first)

    def blocks(turn, kept, after):
        return run_block(
            tiles, early, turn, staged, recv_pair, recv_next, gate_weights, kept, after
        )

    short_chain = 1 < stages <= 8
    first = (0, 1) if short_chain else None
    (send, pooled), state_near, weighed = blocks(first, [], [])
    (send_far,), state_far = run_later(early, first, staged, pooled, weighed, tail, [], [send])
    if short_chain:
        _, state_near, weighed = blocks((1, 2), state_near, [send_far])
    vmem = pl.BlockSpec(memory_space=pltpu.VMEM)
    params = pltpu.CompilerParams(vmem_limit_bytes=16 * 2**20)
    cost = pl.CostEstimate(flops=10**10, bytes_accessed=0, transcendentals=0)

    def relay(arrived, before):
        return pl.pallas_call(
            relay_kernel,
            name="relay",
            out_shape=[
                jax.ShapeDtypeStruct((pixels, early * LANES), BF16),
                jax.ShapeDtypeStruct((8, early * LANES), F32),
            ],
            in_specs=[vmem] * 7 + [pl.BlockSpec(memory_space=pl.ANY)],
            out_specs=[vmem] * 2,
            compiler_params=params,
            cost_estimate=cost,
        )(arrived, *state_near, before)

    def relay_later(stage, arrived, pooled, state_far):
        return pl.pallas_call(
            functools.partial(relay_later_kernel, stage),
            name="relay_later",
            out_shape=jax.ShapeDtypeStruct(send_far.shape, BF16),
            in_specs=[vmem] * 9,
            out_specs=vmem,
            compiler_params=params,
            cost_estimate=cost,
        )(arrived, *state_far, pooled, short_rows)

    arrived = []
    arrived_far = []
    if stages <= 8:
        for stage in range(stages - 1):
            link = [(stage, stage + 1)]
            if stage > 0:
                send, pooled = relay(arrived[-1], send_far)
                if stage == 1:
                    _, state_far = run_later(
                        early, (1, 2), staged, pooled, weighed, tail, state_far, [send]
                    )
                if stage == 1 and stages > 2:
                    turn = (2, stages)
                    _, state_near, weighed = blocks(turn, state_near, [send])
                    _, state_far = run_later(
                        early, turn, staged, pooled, weighed, tail, state_far, []
                    )
                send_far = relay_later(stage, arrived_far[-1], pooled, state_far)
            arrived.append(lax.ppermute(send, "epoch", link))
            arrived_far.append(lax.ppermute(send_far, "epoch", link))
    else:
        chain = [(i, i + 1) for i in range(stages - 1)]

        def along(state, width):
            keep, block = state[2], state[3]

            def turn(_, arriving):
                out = (keep * arriving.astype(F32) + block).astype(BF16)
                return lax.ppermute(out, "epoch", chain)

            return lax.fori_loop(0, stages - 1, turn, jnp.zeros((pixels, width), BF16))

        def unfold(tokens):
            parts = jnp.split(tokens, channels // LANES, axis=1)
            return jnp.concatenate(parts, axis=0)

        incoming = along(state_near, early * LANES)
        incoming_far = along(state_far, channels - early * LANES)
        _, pooled = relay(incoming, send_far)
        blank = jnp.zeros((tail * channels // LANES, LANES), BF16)
        told = relay_later(0, jnp.concatenate([incoming_far, blank]), pooled, state_far)[pixels:]
        told = jnp.concatenate(jnp.split(told, channels // LANES, axis=0), axis=1)
        known = lax.all_gather(told[:epochs], "epoch", axis=0, tiled=True)
        known = jnp.concatenate([known, jnp.zeros((tail - total, channels), BF16)])
        arrived.append(incoming)
        arrived_far.append(jnp.concatenate([incoming_far, unfold(known)]))

    hbm = pl.BlockSpec(memory_space=pltpu.HBM)
    heads = head_slope.size
    memory, pooled, head_of, channel_of = pl.pallas_call(
        functools.partial(final_early_kernel, len(arrived)),
        name="final_early",
        out_shape=[
            jax.ShapeDtypeStruct((epochs, pixels, channels), BF16),
            jax.ShapeDtypeStruct((8, early * LANES), F32),
            jax.ShapeDtypeStruct((channels, heads), BF16),
            jax.ShapeDtypeStruct((heads, channels), BF16),
        ],
        in_specs=[vmem] * (len(arrived) + 6),
        out_specs=[hbm] + [vmem] * 3,
        scratch_shapes=[
            pltpu.VMEM((epochs, pixels, early * LANES), BF16),
            pltpu.SemaphoreType.DMA,
        ],
        compiler_params=params,
        cost_estimate=cost,
    )(*arrived, *state_near)
    memory, change = pl.pallas_call(
        functools.partial(final_kernel, len(arrived)),
        name="final",
        out_shape=[
            jax.ShapeDtypeStruct((epochs, pixels, channels), BF16),
            jax.ShapeDtypeStruct((epochs, channels), BF16),
        ],
        in_specs=[vmem] * (len(arrived) + 14) + [hbm],
        out_specs=[hbm, vmem],
        input_output_aliases={len(arrived) + 14: 0},
        scratch_shapes=[
            pltpu.VMEM((epochs, pixels, channels - early * LANES), BF16),
            pltpu.SemaphoreType.DMA,
        ],
        compiler_params=pltpu.CompilerParams(vmem_limit_bytes=24 * 2**20),
    )(
        *arrived_far,
        *state_far,
        short_rows,
        months,
        slope,
        qkv_near,
        out_near,
        pooled,
        head_of,
        channel_of,
        pltpu.with_memory_space_constraint(memory, pltpu.HBM),
    )
    return (
        memory.reshape(epochs, height, width, channels),
        change.reshape(epochs, 1, 1, channels),
    )


def solution(mesh):
    placed = (
        P("epoch", ("groups", "tile"), None, None),
        P("epoch", ("groups", "tile"), None),
        P("groups"),
    ) + (P(),) * 17
    return jax.shard_map(
        body,
        mesh=mesh,
        in_specs=placed,
        out_specs=(
            P("epoch", ("groups", "tile"), None, None),
            P("epoch", ("groups", "tile"), None, None),
        ),
        check_vma=False,
    )
```

```python
import functools
import math

import jax
import jax.numpy as jnp
from jax import lax
from jax.experimental import pallas as pl
from jax.experimental.pallas import tpu as pltpu
from jax.sharding import PartitionSpec as P

PATCH = 16
REACH = 4
LANES = 128
F32 = jnp.float32
BF16 = jnp.bfloat16


def sigmoid(x):
    return 0.5 * jnp.tanh(0.5 * x) + 0.5


def softplus(x):
    return jnp.maximum(x, 0.0) + jnp.log(1.0 + jnp.exp(-jnp.abs(x)))


def gelu_twice(x):
    inner = x * (0.7978845608028654 + (0.7978845608028654 * 0.044715) * (x * x))
    return x + x * jnp.tanh(inner)


def near_kernel(*refs):
    count = len(refs) // 2 - 1
    sources, outs = refs[:count], refs[count : 2 * count]
    to_pair, to_next, sems = refs[2 * count :]
    copies = [pltpu.make_async_copy(a, b, sems.at[i]) for i, (a, b) in enumerate(zip(sources, outs))]
    for copy in copies:
        copy.start()
    copies[0].wait()
    frames = outs[0]
    bottom = frames.shape[1] - REACH
    odd = lax.rem(lax.axis_index("tile"), 2)
    to_pair[...] = frames[:, pl.ds((1 - odd) * bottom, REACH)]
    to_next[...] = frames[:, pl.ds(odd * bottom, REACH)]
    for copy in copies[1:]:
        copy.wait()


def run_near(arrays):
    frames = arrays[0]
    rim = jax.ShapeDtypeStruct((frames.shape[0], REACH) + frames.shape[2:], frames.dtype)
    hbm = pl.BlockSpec(memory_space=pltpu.HBM)
    vmem = pl.BlockSpec(memory_space=pltpu.VMEM)
    out = pl.pallas_call(
        near_kernel,
        name="near",
        out_shape=[jax.ShapeDtypeStruct(x.shape, x.dtype) for x in arrays] + [rim] * 2,
        in_specs=[hbm] * len(arrays),
        out_specs=[vmem] * (len(arrays) + 2),
        scratch_shapes=[pltpu.SemaphoreType.DMA((len(arrays),))],
        compiler_params=pltpu.CompilerParams(vmem_limit_bytes=16 * 2**20),
    )(*[pltpu.with_memory_space_constraint(x, pltpu.HBM) for x in arrays])
    return out[: len(arrays)], out[-2], out[-1]


def stage_kernel(
    frames,
    dw_kernel,
    valid,
    days,
    slope_line,
    b_expand,
    b_gates,
    dw_bias,
    norm_gain,
    norm_shift,
    layer_scale,
    forget_rate,
    attn_gain,
    w_expand_hbm,
    w_reduce_hbm,
    w_gates_hbm,
    w_query_hbm,
    w_key_hbm,
    w_value_hbm,
    w_out_hbm,
    spread,
    mask,
    short_rows,
    long_rows,
    months,
    slope,
    w_expand,
    w_reduce,
    w_first,
    w_qkv,
    w_out,
    padded,
    sems,
):
    epochs, height, width, channels = frames.shape
    groups = channels // LANES
    rows = height + 2
    pixels = height * width
    moves = [
        (w_expand_hbm, w_expand),
        (w_reduce_hbm, w_reduce),
        (w_gates_hbm.at[:, pl.ds(0, w_first.shape[1])], w_first),
        (w_query_hbm, w_qkv.at[:, pl.ds(0, channels)]),
        (w_key_hbm, w_qkv.at[:, pl.ds(channels, channels)]),
        (w_value_hbm, w_qkv.at[:, pl.ds(2 * channels, channels)]),
        (w_out_hbm, w_out),
    ]
    copies = [pltpu.make_async_copy(a, b, sems.at[i]) for i, (a, b) in enumerate(moves)]
    for copy in copies:
        copy.start()

    for c in range(groups):
        for e in range(epochs):
            lanes = slice(c * LANES, (c + 1) * LANES)
            padded[c, e, :, 0:8, :] = jnp.zeros((height, 8, LANES), F32)
            padded[c, e, :, 8 + width : 16 + width, :] = jnp.zeros((height, 8, LANES), F32)
            padded[c, e, :, 8 : 8 + width, :] = frames[e, :, :, lanes].astype(F32)

    half = rows // 2

    def depthwise(index, carry):
        c = index // epochs
        e = index - c * epochs
        lanes = pl.ds(pl.multiple_of(c * LANES, LANES), LANES)
        for part in range(2):
            total = [None] * half
            for ox in range(7):
                factors = [dw_kernel[oy, pl.ds(ox, 1), lanes] for oy in range(7)]
                for r in range(height):
                    at = [(y, r + REACH - (part * half + y)) for y in range(half)]
                    at = [(y, oy) for y, oy in at if 0 <= oy < 7]
                    if not at:
                        continue
                    window = padded[c, e, r, pl.ds(5 + ox, width), :]
                    for y, oy in at:
                        term = window * factors[oy]
                        total[y] = term if total[y] is None else total[y] + term
            for y in range(half):
                line = (part * half + y) * width
                spread[e, pl.ds(line, width), lanes] = total[y]
        return carry

    lax.fori_loop(0, groups * epochs, depthwise, 0)

    short = (dw_bias, norm_gain, norm_shift, layer_scale, forget_rate, attn_gain)
    for k, line in enumerate(short):
        short_rows[k : k + 1, :] = line[...].reshape(1, -1)
    for k, line in enumerate((b_expand, b_gates)):
        long_rows[k : k + 1, :] = line[...].reshape(1, -1)
    slope[...] = slope_line[...].reshape(1, -1)
    total = days.shape[0]
    eye = lax.broadcasted_iota(jnp.int32, (total, total), 0) == lax.broadcasted_iota(
        jnp.int32, (total, total), 1
    )
    month = days[...].astype(F32).reshape(1, -1) / 30.0
    months[...] = jnp.broadcast_to(
        jnp.sum(jnp.where(eye, month, 0.0), axis=1, keepdims=True), months.shape
    )
    down = lax.broadcasted_iota(jnp.int32, (pixels, height), 0) // width
    pick = jnp.where(down == lax.broadcasted_iota(jnp.int32, (pixels, height), 1), 1.0, 0.0).astype(BF16)
    side = lax.rem(lax.broadcasted_iota(jnp.int32, (pixels, width), 0), width)
    place = side == lax.broadcasted_iota(jnp.int32, (pixels, width), 1)
    ones = jnp.ones((width, LANES), BF16)
    for e in range(epochs):
        plane = jnp.where(valid[e] > 0, 1.0, 0.0).astype(BF16)
        lines = jnp.dot(pick, plane, preferred_element_type=F32)
        mask[e * pixels : (e + 1) * pixels, :] = jnp.dot(
            jnp.where(place, lines, 0.0).astype(BF16), ones, preferred_element_type=F32
        )
    for copy in copies:
        copy.wait()


def run_stage(near, w_expand, w_reduce, w_gates, w_qkvo):
    frames, dw_kernel, valid, days, slope = near[:5]
    epochs, height, width, channels = frames.shape
    pixels = height * width
    total = days.shape[0]
    far = [w_expand, w_reduce, w_gates, *w_qkvo]
    hbm = pl.BlockSpec(memory_space=pltpu.HBM)
    vmem = pl.BlockSpec(memory_space=pltpu.VMEM)
    out_shape = [
        jax.ShapeDtypeStruct((epochs, (height + 2) * width, channels), F32),
        jax.ShapeDtypeStruct((epochs * pixels, LANES), F32),
        jax.ShapeDtypeStruct((8, channels), F32),
        jax.ShapeDtypeStruct((8, w_gates.shape[1]), F32),
        jax.ShapeDtypeStruct((total, LANES), F32),
        jax.ShapeDtypeStruct((1, slope.size), F32),
        jax.ShapeDtypeStruct(w_expand.shape, BF16),
        jax.ShapeDtypeStruct(w_reduce.shape, BF16),
        jax.ShapeDtypeStruct((w_gates.shape[0], 4 * LANES), BF16),
        jax.ShapeDtypeStruct((channels, 3 * channels), BF16),
        jax.ShapeDtypeStruct((channels, channels), BF16),
    ]
    return pl.pallas_call(
        stage_kernel,
        name="stage",
        out_shape=out_shape,
        in_specs=[vmem] * len(near) + [hbm] * len(far),
        out_specs=[vmem] * len(out_shape),
        scratch_shapes=[
            pltpu.VMEM((channels // LANES, epochs, height, width + 16, LANES), F32),
            pltpu.SemaphoreType.DMA((len(far),)),
        ],
        compiler_params=pltpu.CompilerParams(vmem_limit_bytes=24 * 2**20),
        cost_estimate=pl.CostEstimate(
            flops=10**10, bytes_accessed=8 * w_expand.size, transcendentals=0
        ),
    )(*near, *[pltpu.with_memory_space_constraint(x, pltpu.HBM) for x in far])


def on_devices(turn, work):
    if turn is None:
        work()
    else:
        stage = lax.axis_index("epoch")
        pl.when((stage >= turn[0]) & (stage < turn[1]))(work)


def block_kernel(tiles, turn, count, sends, *refs):
    outs = refs[count:]
    if not sends:
        outs = (None, None) + outs
    on_devices(turn, lambda: block_work(tiles, *refs[:12], *outs))


def block_work(
    tiles,
    spread,
    recv_pair,
    recv_next,
    frames,
    mask,
    short_rows,
    long_rows,
    dw_kernel,
    w_expand,
    w_reduce,
    w_first,
    w_gates_hbm,
    send,
    pooled,
    decay0,
    inflow0,
    keep,
    block,
    open0,
    open1,
    taps,
    w_later,
    rim,
    edge,
    w_gates,
    sems,
):
    epochs, height, width, channels = frames.shape
    groups = channels // LANES
    rows = height + 2
    pixels = height * width
    wide = 4 * LANES

    early = keep.shape[1] // LANES
    places = [w_gates.at[j] for j in range(early - 1)] + [w_later.at[j] for j in range(groups - early)]
    gate_copies = [
        pltpu.make_async_copy(w_gates_hbm.at[:, pl.ds((j + 1) * wide, wide)], place, sems.at[j])
        for j, place in enumerate(places)
    ]
    for copy in gate_copies:
        copy.start()

    dw_bias = short_rows[0:1, :]
    norm_gain = short_rows[1:2, :]
    norm_shift = short_rows[2:3, :]
    half_scale = 0.5 * short_rows[3:4, :]
    b_expand = long_rows[0:1, :]

    me = lax.axis_index("tile")
    odd = lax.rem(me, 2)
    pair_row = (1 - odd) * REACH
    next_row = odd * REACH

    for c in range(groups):
        lanes = slice(c * LANES, (c + 1) * LANES)
        for e in range(epochs):
            rim[c, e, :, 0:8, :] = jnp.zeros((2 * REACH, 8, LANES), F32)
            rim[c, e, :, 8 + width : 16 + width, :] = jnp.zeros((2 * REACH, 8, LANES), F32)
            rim[c, e, pl.ds(pair_row, REACH), 8 : 8 + width, :] = recv_pair[e, :, :, lanes].astype(F32)
            rim[c, e, pl.ds(next_row, REACH), 8 : 8 + width, :] = recv_next[e, :, :, lanes].astype(F32)

    def depthwise(index, carry):
        c = index // epochs
        e = index - c * epochs
        lanes = pl.ds(pl.multiple_of(c * LANES, LANES), LANES)
        total = [None] * (2 * REACH)
        for ox in range(7):
            factors = [dw_kernel[oy, pl.ds(ox, 1), lanes] for oy in range(7)]
            for k in range(REACH):
                above = rim[c, e, k, pl.ds(5 + ox, width), :]
                below = rim[c, e, REACH + k, pl.ds(5 + ox, width), :]
                for y in range(k + 1):
                    term = above * factors[k - y]
                    total[y] = term if total[y] is None else total[y] + term
                for y in range(k, REACH):
                    term = below * factors[6 + k - y]
                    at = REACH + y
                    total[at] = term if total[at] is None else total[at] + term
        for y in range(2 * REACH):
            edge[e, pl.ds(y * width, width), lanes] = total[y]
        return carry

    lax.fori_loop(0, groups * epochs, depthwise, 0)

    count = rows * width
    rimmed = REACH * width
    column = lax.broadcasted_iota(jnp.int32, (count, LANES), 0)
    across = lax.rem(column, width)
    line = column // width
    first = jnp.where(me == 0, 1, 0)
    last = jnp.where(me == tiles - 1, rows - 2, rows - 1)
    inside = jnp.where((line >= first) & (line <= last), 1.0, 0.0)
    for e in range(epochs):
        values = (
            jnp.concatenate(
                [
                    spread[e, :rimmed] + edge[e, :rimmed],
                    spread[e, rimmed : count - rimmed],
                    spread[e, count - rimmed :] + edge[e, rimmed:],
                ],
                axis=0,
            )
            + dw_bias
        )
        center = jnp.mean(values, axis=-1, keepdims=True)
        centred = values - center
        variance = jnp.mean(centred * centred, axis=-1, keepdims=True)
        normed = (centred * lax.rsqrt(variance + 1e-06) * norm_gain + norm_shift).astype(BF16)
        grown = jnp.dot(normed, w_expand[...], preferred_element_type=F32) + b_expand
        reduced = jnp.dot(gelu_twice(grown).astype(BF16), w_reduce[...], preferred_element_type=F32)
        for c in range(groups):
            lanes = slice(c * LANES, (c + 1) * LANES)
            centre = jnp.concatenate(
                [
                    rim[c, e, REACH - 1, 8 : 8 + width, :],
                    frames[e, :, :, lanes].astype(F32).reshape(pixels, LANES),
                    rim[c, e, REACH, 8 : 8 + width, :],
                ],
                axis=0,
            )
            feature = centre + half_scale[:, lanes] * reduced[:, lanes]
            feature = (feature * inside).astype(BF16).astype(F32)
            before = jnp.where(across == 0, 0.0, pltpu.roll(feature, 1, 0))
            after = jnp.where(across == width - 1, 0.0, pltpu.roll(feature, count - 1, 0))
            for ox, shifted in enumerate((before, feature, after)):
                packed = shifted.astype(BF16)
                for oy in range(3):
                    at = (oy * 3 + ox) * channels + c * LANES
                    taps[e * pixels : (e + 1) * pixels, at : at + LANES] = packed[
                        oy * width : oy * width + pixels
                    ]

    state = (decay0, inflow0, keep, block, open0, open1)
    for copy in gate_copies:
        copy.wait()
    cells_of(0, 0, taps, w_first, mask, short_rows, long_rows, send, pooled, state)
    for j in range(1, early):
        cells_of(j, j, taps, w_gates.at[j - 1], mask, short_rows, long_rows, send, pooled, state)


def gates_of(preact):
    quarter = LANES // 4
    lane = lax.broadcasted_iota(jnp.int32, (preact.shape[0], LANES), 1)
    spot = lane // quarter
    within = lane - spot * quarter
    sorted_ = []
    for i in range(4):
        gate = lax.rem(spot - i + 4, 4)
        sorted_.append(
            jnp.take_along_axis(preact[:, i * LANES : (i + 1) * LANES], 4 * within + gate, axis=1)
        )
    gates = []
    for g in range(4):
        out = sorted_[0]
        for i in range(1, 4):
            out = jnp.where(spot == (g + i) % 4, sorted_[i], out)
        gates.append(out if g == 0 else pltpu.roll(out, LANES - g * quarter, 1))
    return gates


def cells_of(j, at, taps, weights, mask, short_rows, long_rows, send, pooled, state):
    decay0, inflow0, keep, block, open0, open1 = state
    pixels = keep.shape[0]
    lanes = slice(at * LANES, (at + 1) * LANES)
    bias = long_rows[1:2, j * 4 * LANES : (j + 1) * 4 * LANES]
    rate = short_rows[4:5, j * LANES : (j + 1) * LANES]
    cell = None
    for e, opens in enumerate((open0, open1)):
        rows = slice(e * pixels, (e + 1) * pixels)
        preact = jnp.dot(taps[rows, :], weights[...], preferred_element_type=F32) + bias
        gate_in, gate_keep, gate_new, gate_out = gates_of(preact)
        good = mask[rows, :] > 0.5
        decay = jnp.where(good, jnp.exp(-rate * softplus(gate_keep)), 1.0)
        inflow = jnp.where(good, sigmoid(gate_in) * jnp.tanh(gate_new), 0.0)
        opened = sigmoid(gate_out)
        opens[:, lanes] = opened
        if e == 0:
            decay0[:, lanes] = decay
            inflow0[:, lanes] = inflow
            cell = inflow
        else:
            keep[:, lanes] = decay0[:, lanes] * decay
            cell = decay * inflow0[:, lanes] + inflow
            block[:, lanes] = cell
            if send is not None:
                send[:pixels, lanes] = cell.astype(BF16)
        if pooled is not None:
            pooled[e : e + 1, lanes] = pool(opened * jnp.tanh(cell))


def later_kernel(first, turn, count, sends, *refs):
    outs = refs[count:]
    if not sends:
        outs = (None,) + outs + (None,)
    on_devices(turn, lambda: later_work(first, *refs[:6], *outs))


def later_work(
    first,
    taps,
    w_gates,
    mask,
    short_rows,
    long_rows,
    pooled_early,
    send,
    decay0,
    inflow0,
    keep,
    block,
    open0,
    open1,
    pooled,
):
    channels = short_rows.shape[1]
    state = (decay0, inflow0, keep, block, open0, open1)
    for j in range(first, channels // LANES):
        at = j - first
        cells_of(j, at, taps, w_gates.at[at], mask, short_rows, long_rows, send, pooled, state)
    if send is None:
        return
    pixels = keep.shape[0]
    both = jnp.concatenate([pooled_early[0:2, :], pooled[0:2, :]], axis=1)
    own = tokens_of(both, short_rows[5:6, :])
    tail = (send.shape[0] - pixels) * LANES // channels
    known = jnp.zeros((tail, channels), F32)
    write_tail(send, pixels, put_tokens(known, own, 0))


def write_tail(send, pixels, tokens):
    tail, channels = tokens.shape
    for c in range(channels // LANES):
        at = pixels + c * tail
        send[at : at + tail, :] = tokens[:, c * LANES : (c + 1) * LANES].astype(BF16)


def read_tail(arrived, pixels, channels):
    tail = (arrived.shape[0] - pixels) * LANES // channels
    parts = [
        arrived[pixels + c * tail : pixels + (c + 1) * tail, :].astype(F32)
        for c in range(channels // LANES)
    ]
    return jnp.concatenate(parts, axis=1)


def run_block(tiles, early, turn, staged, recv_pair, recv_next, w_gates, kept, after):
    spread, mask, short_rows, long_rows, frames, dw_kernel, w_expand, w_reduce, w_first = staged
    epochs, height, width, channels = frames.shape
    pixels = height * width
    depth = w_gates.shape[0]
    vmem = pl.BlockSpec(memory_space=pltpu.VMEM)
    hbm = pl.BlockSpec(memory_space=pltpu.HBM)
    anywhere = pl.BlockSpec(memory_space=pl.ANY)
    near = early * LANES
    far = channels - near
    sends = not kept
    sent = [
        jax.ShapeDtypeStruct((pixels, near), BF16),
        jax.ShapeDtypeStruct((8, near), F32),
    ] * sends
    state = [jax.ShapeDtypeStruct((pixels, near), F32)] * 6
    flops = 2 * epochs * pixels * (2 * w_expand.size + w_gates.size)
    out = pl.pallas_call(
        functools.partial(block_kernel, tiles, turn, 12 + len(kept) + len(after), sends),
        name="block",
        out_shape=[
            *sent,
            *state,
            jax.ShapeDtypeStruct((epochs * pixels, depth), BF16),
            jax.ShapeDtypeStruct((far // LANES, depth, 4 * LANES), BF16),
        ],
        in_specs=[vmem] * 11 + [hbm] + [vmem] * len(kept) + [anywhere] * len(after),
        out_specs=[vmem] * (len(sent) + 8),
        input_output_aliases={12 + k: len(sent) + k for k in range(len(kept))},
        scratch_shapes=[
            pltpu.VMEM((channels // LANES, epochs, 2 * REACH, width + 16, LANES), F32),
            pltpu.VMEM((epochs, 2 * REACH * width, channels), F32),
            pltpu.VMEM((max(1, early - 1), depth, 4 * LANES), BF16),
            pltpu.SemaphoreType.DMA((channels // LANES - 1,)),
        ],
        compiler_params=pltpu.CompilerParams(vmem_limit_bytes=20 * 2**20),
        cost_estimate=pl.CostEstimate(flops=flops, bytes_accessed=2 * w_gates.size, transcendentals=0),
    )(
        spread,
        recv_pair,
        recv_next,
        frames,
        mask,
        short_rows,
        long_rows,
        dw_kernel,
        w_expand,
        w_reduce,
        w_first,
        pltpu.with_memory_space_constraint(w_gates, pltpu.HBM),
        *kept,
        *after,
    )
    return out[: len(sent)], out[len(sent) : -2], out[-2:]


def run_later(early, turn, staged, pooled, weighed, tail, kept, after):
    _, mask, short_rows, long_rows = staged[:4]
    taps, w_later = weighed
    pixels = taps.shape[0] // 2
    channels = short_rows.shape[1]
    far = channels - early * LANES
    vmem = pl.BlockSpec(memory_space=pltpu.VMEM)
    anywhere = pl.BlockSpec(memory_space=pl.ANY)
    sends = not kept
    sent = [jax.ShapeDtypeStruct((pixels + tail * channels // LANES, far), BF16)] * sends
    out = pl.pallas_call(
        functools.partial(later_kernel, early, turn, 6 + len(kept) + len(after), sends),
        name="later",
        out_shape=[*sent] + [jax.ShapeDtypeStruct((pixels, far), F32)] * 6,
        in_specs=[vmem] * 6 + [vmem] * len(kept) + [anywhere] * len(after),
        out_specs=[vmem] * (len(sent) + 6),
        input_output_aliases={6 + k: len(sent) + k for k in range(len(kept))},
        scratch_shapes=[pltpu.VMEM((8, far), F32)] * sends,
        compiler_params=pltpu.CompilerParams(vmem_limit_bytes=16 * 2**20),
        cost_estimate=pl.CostEstimate(flops=10**10, bytes_accessed=0, transcendentals=0),
    )(taps, w_later, mask, short_rows, long_rows, pooled, *kept, *after)
    return out[: len(sent)], out[len(sent) :]


def pool(memory):
    return jnp.mean(memory.astype(BF16).astype(F32), axis=0, keepdims=True)


def tokens_of(both, gain):
    center = jnp.mean(both, axis=-1, keepdims=True)
    centred = both - center
    variance = jnp.mean(centred * centred, axis=-1, keepdims=True)
    return (centred * lax.rsqrt(variance + 1e-06) * gain).astype(BF16).astype(F32)


def put_tokens(known, own, at):
    line = lax.broadcasted_iota(jnp.int32, known.shape, 0)
    return jnp.where(line == at, own[0:1], jnp.where(line == at + 1, own[1:2], known))


def step_cells(arrived, decay0, inflow0, keep, block):
    state = arrived[: keep.shape[0]].astype(F32)
    return decay0[...] * state + inflow0[...], keep[...] * state + block[...]


def relay_kernel(arrived, decay0, inflow0, keep, block, open0, open1, before, send, pooled):
    cell0, cell1 = step_cells(arrived, decay0, inflow0, keep, block)
    send[...] = cell1.astype(BF16)
    pooled[0:1, :] = pool(open0[...] * jnp.tanh(cell0))
    pooled[1:2, :] = pool(open1[...] * jnp.tanh(cell1))


def relay_later_kernel(
    stage, arrived, decay0, inflow0, keep, block, open0, open1, pooled_early, short_rows, send
):
    pixels = keep.shape[0]
    cell0, cell1 = step_cells(arrived, decay0, inflow0, keep, block)
    send[:pixels] = cell1.astype(BF16)
    pooled = jnp.concatenate(
        [pool(open0[...] * jnp.tanh(cell0)), pool(open1[...] * jnp.tanh(cell1))], axis=0
    )
    both = jnp.concatenate([pooled_early[0:2, :], pooled], axis=1)
    own = tokens_of(both, short_rows[5:6, :])
    known = read_tail(arrived, pixels, short_rows.shape[1])
    write_tail(send, pixels, put_tokens(known, own, 2 * stage))


def finish(arrived, state, memory):
    decay0, inflow0, keep, block, open0, open1 = state
    pixels = keep.shape[0]
    incoming = arrived[0][:pixels].astype(F32)
    for more in arrived[1:]:
        incoming = incoming + more[:pixels].astype(F32)
    cell0 = decay0[...] * incoming + inflow0[...]
    cell1 = keep[...] * incoming + block[...]
    pooled = []
    for e, (gate, cell) in enumerate(((open0, cell0), (open1, cell1))):
        out = (gate[...] * jnp.tanh(cell)).astype(BF16)
        memory[e] = out
        pooled.append(pool(out))
    return jnp.concatenate(pooled, axis=0)


def final_early_kernel(count, *refs):
    arrived, state = refs[:count], refs[count : count + 6]
    memory_hbm, pooled, head_of, channel_of, memory, sem = refs[count + 6 :]
    pooled[0:2, :] = finish(arrived, state, memory)
    copy = pltpu.make_async_copy(memory, memory_hbm.at[:, :, pl.ds(0, memory.shape[2])], sem)
    copy.start()
    channels, heads = head_of.shape
    depth = channels // heads
    member = lax.broadcasted_iota(jnp.int32, (channels, heads), 0) // depth
    head = lax.broadcasted_iota(jnp.int32, (channels, heads), 1)
    head_of[...] = jnp.where(member == head, 1.0, 0.0).astype(BF16)
    member = lax.broadcasted_iota(jnp.int32, (heads, channels), 1) // depth
    head = lax.broadcasted_iota(jnp.int32, (heads, channels), 0)
    channel_of[...] = jnp.where(member == head, 1.0, 0.0).astype(BF16)
    copy.wait()


def final_kernel(count, *refs):
    arrived, state = refs[:count], refs[count : count + 6]
    short_rows, months, slope, w_qkv, w_out, pooled_early, head_of, channel_of = refs[count + 6 : count + 14]
    memory_hbm, change, memory, sem = refs[count + 15 :]
    epochs, pixels, far = memory.shape
    channels = short_rows.shape[1]
    total = months.shape[0]
    pooled = finish(arrived, state, memory)
    copy = pltpu.make_async_copy(memory, memory_hbm.at[:, :, pl.ds(channels - far, far)], sem)
    copy.start()
    known = read_tail(arrived[0], pixels, channels)
    for more in arrived[1:]:
        known = known + read_tail(more, pixels, channels)
    both = jnp.concatenate([pooled_early[0:2, :], pooled], axis=1)
    own = tokens_of(both, short_rows[5:6, :])
    stage = lax.axis_index("epoch")
    tokens = put_tokens(known, own, 2 * stage).astype(BF16)
    heads = slope.shape[1]
    depth = channels // heads
    qkv = jnp.dot(tokens, w_qkv[...], preferred_element_type=F32).astype(BF16).astype(F32)[:total]
    queries = qkv[:, :channels]
    keys = qkv[:, channels : 2 * channels]
    values = qkv[:, 2 * channels :]
    def exact_dot(x, zero_one):
        high = x.astype(BF16)
        rest = x - high.astype(F32)
        low = rest.astype(BF16)
        least = (rest - low.astype(F32)).astype(BF16)
        out = jnp.dot(
            jnp.concatenate([high, low, least], axis=0), zero_one[...], preferred_element_type=F32
        )
        count = x.shape[0]
        return out[:count] + out[count : 2 * count] + out[2 * count :]

    line = lax.broadcasted_iota(jnp.int32, (total, channels), 0)
    key_index = lax.broadcasted_iota(jnp.int32, (total, heads), 0)
    month = months[:, :heads]
    places = [epochs * stage + step for step in range(epochs)]
    products = []
    for mine in places:
        query = jnp.sum(jnp.where(line == mine, queries, 0.0), axis=0, keepdims=True)
        products.append(query * keys)
    raw = exact_dot(jnp.concatenate(products, axis=0), head_of)
    weights = []
    for step, mine in enumerate(places):
        now = jnp.sum(jnp.where(key_index == mine, month, 0.0), axis=0, keepdims=True)
        scores = raw[step * total : (step + 1) * total] / math.sqrt(depth) - slope[...] * (now - month)
        scores = jnp.where(key_index <= mine, scores, -1e30)
        expo = jnp.exp(scores - jnp.max(scores, axis=0, keepdims=True))
        weights.append(expo / jnp.sum(expo, axis=0, keepdims=True))
    wide = exact_dot(jnp.concatenate(weights, axis=0), channel_of)
    results = [
        jnp.sum(wide[step * total : (step + 1) * total] * values, axis=0, keepdims=True)
        for step in range(epochs)
    ]
    mixed = jnp.concatenate(results, axis=0).astype(BF16)
    change[...] = jnp.dot(mixed, w_out[...], preferred_element_type=F32).astype(BF16)
    copy.wait()


def pairs(count, start):
    links = []
    for i in range(start, count - 1, 2):
        links += [(i, i + 1), (i + 1, i)]
    return links


def body(
    frames,
    valid,
    days,
    dw_kernel,
    dw_bias,
    norm_gain,
    norm_shift,
    w_expand,
    b_expand,
    w_reduce,
    layer_scale,
    w_gates,
    b_gates,
    forget_rate,
    attn_gain,
    w_query,
    w_key,
    w_value,
    w_out,
    head_slope,
):

    epochs, height, width, channels = frames.shape
    pixels = height * width
    tiles = lax.axis_size("tile")
    stages = lax.axis_size("epoch")
    total = epochs * stages
    tail = -(-total // 16) * 16
    gate_weights = w_gates.reshape(9 * channels, -1)
    near, to_pair, to_next = run_near(
        [
            frames,
            dw_kernel,
            valid,
            days,
            head_slope,
            b_expand,
            b_gates,
            dw_bias,
            norm_gain,
            norm_shift,
            layer_scale,
            forget_rate,
            attn_gain,
        ]
    )
    recv_pair = lax.ppermute(to_pair, "tile", pairs(tiles, 0))
    recv_next = lax.ppermute(to_next, "tile", pairs(tiles, 1))
    (
        spread,
        mask,
        short_rows,
        long_rows,
        months,
        slope,
        expand_near,
        reduce_near,
        w_first,
        qkv_near,
        out_near,
    ) = run_stage(near, w_expand, w_reduce, gate_weights, [w_query, w_key, w_value, w_out])
    early = max(1, channels // LANES - 1)
    staged = (spread, mask, short_rows, long_rows, near[0], near[1], expand_near, reduce_near, w_first)

    def blocks(turn, kept, after):
        return run_block(
            tiles, early, turn, staged, recv_pair, recv_next, gate_weights, kept, after
        )

    short_chain = 1 < stages <= 8
    first = (0, 1) if short_chain else None
    (send, pooled), state_near, weighed = blocks(first, [], [])
    (send_far,), state_far = run_later(early, first, staged, pooled, weighed, tail, [], [send])
    if short_chain:
        _, state_near, weighed = blocks((1, stages), state_near, [send_far])
        _, state_far = run_later(early, (1, 2), staged, pooled, weighed, tail, state_far, [])
    vmem = pl.BlockSpec(memory_space=pltpu.VMEM)
    params = pltpu.CompilerParams(vmem_limit_bytes=16 * 2**20)
    cost = pl.CostEstimate(flops=10**10, bytes_accessed=0, transcendentals=0)

    def relay(arrived, before):
        return pl.pallas_call(
            relay_kernel,
            name="relay",
            out_shape=[
                jax.ShapeDtypeStruct((pixels, early * LANES), BF16),
                jax.ShapeDtypeStruct((8, early * LANES), F32),
            ],
            in_specs=[vmem] * 7 + [pl.BlockSpec(memory_space=pl.ANY)],
            out_specs=[vmem] * 2,
            compiler_params=params,
            cost_estimate=cost,
        )(arrived, *state_near, before)

    def relay_later(stage, arrived, pooled, state_far):
        return pl.pallas_call(
            functools.partial(relay_later_kernel, stage),
            name="relay_later",
            out_shape=jax.ShapeDtypeStruct(send_far.shape, BF16),
            in_specs=[vmem] * 9,
            out_specs=vmem,
            compiler_params=params,
            cost_estimate=cost,
        )(arrived, *state_far, pooled, short_rows)

    arrived = []
    arrived_far = []
    if stages <= 8:
        for stage in range(stages - 1):
            link = [(stage, stage + 1)]
            if stage > 0:
                send, pooled = relay(arrived[-1], send_far)
                if stage == 1 and stages > 2:
                    _, state_far = run_later(
                        early, (2, stages), staged, pooled, weighed, tail, state_far, [send]
                    )
                send_far = relay_later(stage, arrived_far[-1], pooled, state_far)
            arrived.append(lax.ppermute(send, "epoch", link))
            arrived_far.append(lax.ppermute(send_far, "epoch", link))
    else:
        chain = [(i, i + 1) for i in range(stages - 1)]

        def along(state, width):
            keep, block = state[2], state[3]

            def turn(_, arriving):
                out = (keep * arriving.astype(F32) + block).astype(BF16)
                return lax.ppermute(out, "epoch", chain)

            return lax.fori_loop(0, stages - 1, turn, jnp.zeros((pixels, width), BF16))

        def unfold(tokens):
            parts = jnp.split(tokens, channels // LANES, axis=1)
            return jnp.concatenate(parts, axis=0)

        incoming = along(state_near, early * LANES)
        incoming_far = along(state_far, channels - early * LANES)
        _, pooled = relay(incoming, send_far)
        blank = jnp.zeros((tail * channels // LANES, LANES), BF16)
        told = relay_later(0, jnp.concatenate([incoming_far, blank]), pooled, state_far)[pixels:]
        told = jnp.concatenate(jnp.split(told, channels // LANES, axis=0), axis=1)
        known = lax.all_gather(told[:epochs], "epoch", axis=0, tiled=True)
        known = jnp.concatenate([known, jnp.zeros((tail - total, channels), BF16)])
        arrived.append(incoming)
        arrived_far.append(jnp.concatenate([incoming_far, unfold(known)]))

    hbm = pl.BlockSpec(memory_space=pltpu.HBM)
    heads = head_slope.size
    memory, pooled, head_of, channel_of = pl.pallas_call(
        functools.partial(final_early_kernel, len(arrived)),
        name="final_early",
        out_shape=[
            jax.ShapeDtypeStruct((epochs, pixels, channels), BF16),
            jax.ShapeDtypeStruct((8, early * LANES), F32),
            jax.ShapeDtypeStruct((channels, heads), BF16),
            jax.ShapeDtypeStruct((heads, channels), BF16),
        ],
        in_specs=[vmem] * (len(arrived) + 6),
        out_specs=[hbm] + [vmem] * 3,
        scratch_shapes=[
            pltpu.VMEM((epochs, pixels, early * LANES), BF16),
            pltpu.SemaphoreType.DMA,
        ],
        compiler_params=params,
        cost_estimate=cost,
    )(*arrived, *state_near)
    memory, change = pl.pallas_call(
        functools.partial(final_kernel, len(arrived)),
        name="final",
        out_shape=[
            jax.ShapeDtypeStruct((epochs, pixels, channels), BF16),
            jax.ShapeDtypeStruct((epochs, channels), BF16),
        ],
        in_specs=[vmem] * (len(arrived) + 14) + [hbm],
        out_specs=[hbm, vmem],
        input_output_aliases={len(arrived) + 14: 0},
        scratch_shapes=[
            pltpu.VMEM((epochs, pixels, channels - early * LANES), BF16),
            pltpu.SemaphoreType.DMA,
        ],
        compiler_params=pltpu.CompilerParams(vmem_limit_bytes=24 * 2**20),
    )(
        *arrived_far,
        *state_far,
        short_rows,
        months,
        slope,
        qkv_near,
        out_near,
        pooled,
        head_of,
        channel_of,
        pltpu.with_memory_space_constraint(memory, pltpu.HBM),
    )
    return (
        memory.reshape(epochs, height, width, channels),
        change.reshape(epochs, 1, 1, channels),
    )


def solution(mesh):
    placed = (
        P("epoch", ("groups", "tile"), None, None),
        P("epoch", ("groups", "tile"), None),
        P("groups"),
    ) + (P(),) * 17
    return jax.shard_map(
        body,
        mesh=mesh,
        in_specs=placed,
        out_specs=(
            P("epoch", ("groups", "tile"), None, None),
            P("epoch", ("groups", "tile"), None, None),
        ),
        check_vma=False,
    )
```

```python
import functools
import math

import jax
import jax.numpy as jnp
from jax import lax
from jax.experimental import pallas as pl
from jax.experimental.pallas import tpu as pltpu
from jax.sharding import PartitionSpec as P

PATCH = 16
REACH = 4
LANES = 128
F32 = jnp.float32
BF16 = jnp.bfloat16


def sigmoid(x):
    return 0.5 * jnp.tanh(0.5 * x) + 0.5


def softplus(x):
    return jnp.maximum(x, 0.0) + jnp.log(1.0 + jnp.exp(-jnp.abs(x)))


def gelu_twice(x):
    inner = x * (0.7978845608028654 + (0.7978845608028654 * 0.044715) * (x * x))
    return x + x * jnp.tanh(inner)


def near_kernel(*refs):
    count = len(refs) // 2 - 1
    sources, outs = refs[:count], refs[count : 2 * count]
    to_pair, to_next, sems = refs[2 * count :]
    copies = [pltpu.make_async_copy(a, b, sems.at[i]) for i, (a, b) in enumerate(zip(sources, outs))]
    for copy in copies:
        copy.start()
    copies[0].wait()
    frames = outs[0]
    bottom = frames.shape[1] - REACH
    odd = lax.rem(lax.axis_index("tile"), 2)
    to_pair[...] = frames[:, pl.ds((1 - odd) * bottom, REACH)]
    to_next[...] = frames[:, pl.ds(odd * bottom, REACH)]
    for copy in copies[1:]:
        copy.wait()


def run_near(arrays):
    frames = arrays[0]
    rim = jax.ShapeDtypeStruct((frames.shape[0], REACH) + frames.shape[2:], frames.dtype)
    hbm = pl.BlockSpec(memory_space=pltpu.HBM)
    vmem = pl.BlockSpec(memory_space=pltpu.VMEM)
    out = pl.pallas_call(
        near_kernel,
        name="near",
        out_shape=[jax.ShapeDtypeStruct(x.shape, x.dtype) for x in arrays] + [rim] * 2,
        in_specs=[hbm] * len(arrays),
        out_specs=[vmem] * (len(arrays) + 2),
        scratch_shapes=[pltpu.SemaphoreType.DMA((len(arrays),))],
        compiler_params=pltpu.CompilerParams(vmem_limit_bytes=16 * 2**20),
    )(*[pltpu.with_memory_space_constraint(x, pltpu.HBM) for x in arrays])
    return out[: len(arrays)], out[-2], out[-1]


def stage_kernel(
    frames,
    dw_kernel,
    valid,
    days,
    slope_line,
    b_expand,
    b_gates,
    dw_bias,
    norm_gain,
    norm_shift,
    layer_scale,
    forget_rate,
    attn_gain,
    w_expand_hbm,
    w_reduce_hbm,
    w_gates_hbm,
    w_query_hbm,
    w_key_hbm,
    w_value_hbm,
    w_out_hbm,
    spread,
    mask,
    short_rows,
    long_rows,
    months,
    slope,
    w_expand,
    w_reduce,
    w_first,
    w_qkv,
    w_out,
    padded,
    sems,
):
    epochs, height, width, channels = frames.shape
    groups = channels // LANES
    rows = height + 2
    pixels = height * width
    moves = [
        (w_expand_hbm, w_expand),
        (w_reduce_hbm, w_reduce),
        (w_gates_hbm.at[:, pl.ds(0, w_first.shape[1])], w_first),
        (w_query_hbm, w_qkv.at[:, pl.ds(0, channels)]),
        (w_key_hbm, w_qkv.at[:, pl.ds(channels, channels)]),
        (w_value_hbm, w_qkv.at[:, pl.ds(2 * channels, channels)]),
        (w_out_hbm, w_out),
    ]
    copies = [pltpu.make_async_copy(a, b, sems.at[i]) for i, (a, b) in enumerate(moves)]
    for copy in copies:
        copy.start()

    for c in range(groups):
        for e in range(epochs):
            lanes = slice(c * LANES, (c + 1) * LANES)
            padded[c, e, :, 0:8, :] = jnp.zeros((height, 8, LANES), F32)
            padded[c, e, :, 8 + width : 16 + width, :] = jnp.zeros((height, 8, LANES), F32)
            padded[c, e, :, 8 : 8 + width, :] = frames[e, :, :, lanes].astype(F32)

    half = rows // 2

    def depthwise(index, carry):
        c = index // epochs
        e = index - c * epochs
        lanes = pl.ds(pl.multiple_of(c * LANES, LANES), LANES)
        for part in range(2):
            total = [None] * half
            for ox in range(7):
                factors = [dw_kernel[oy, pl.ds(ox, 1), lanes] for oy in range(7)]
                for r in range(height):
                    at = [(y, r + REACH - (part * half + y)) for y in range(half)]
                    at = [(y, oy) for y, oy in at if 0 <= oy < 7]
                    if not at:
                        continue
                    window = padded[c, e, r, pl.ds(5 + ox, width), :]
                    for y, oy in at:
                        term = window * factors[oy]
                        total[y] = term if total[y] is None else total[y] + term
            for y in range(half):
                line = (part * half + y) * width
                spread[e, pl.ds(line, width), lanes] = total[y]
        return carry

    lax.fori_loop(0, groups * epochs, depthwise, 0)

    short = (dw_bias, norm_gain, norm_shift, layer_scale, forget_rate, attn_gain)
    for k, line in enumerate(short):
        short_rows[k : k + 1, :] = line[...].reshape(1, -1)
    for k, line in enumerate((b_expand, b_gates)):
        long_rows[k : k + 1, :] = line[...].reshape(1, -1)
    slope[...] = slope_line[...].reshape(1, -1)
    total = days.shape[0]
    eye = lax.broadcasted_iota(jnp.int32, (total, total), 0) == lax.broadcasted_iota(
        jnp.int32, (total, total), 1
    )
    month = days[...].astype(F32).reshape(1, -1) / 30.0
    months[...] = jnp.broadcast_to(
        jnp.sum(jnp.where(eye, month, 0.0), axis=1, keepdims=True), months.shape
    )
    down = lax.broadcasted_iota(jnp.int32, (pixels, height), 0) // width
    pick = jnp.where(down == lax.broadcasted_iota(jnp.int32, (pixels, height), 1), 1.0, 0.0).astype(BF16)
    side = lax.rem(lax.broadcasted_iota(jnp.int32, (pixels, width), 0), width)
    place = side == lax.broadcasted_iota(jnp.int32, (pixels, width), 1)
    ones = jnp.ones((width, LANES), BF16)
    for e in range(epochs):
        plane = jnp.where(valid[e] > 0, 1.0, 0.0).astype(BF16)
        lines = jnp.dot(pick, plane, preferred_element_type=F32)
        mask[e * pixels : (e + 1) * pixels, :] = jnp.dot(
            jnp.where(place, lines, 0.0).astype(BF16), ones, preferred_element_type=F32
        )
    for copy in copies:
        copy.wait()


def run_stage(near, w_expand, w_reduce, w_gates, w_qkvo):
    frames, dw_kernel, valid, days, slope = near[:5]
    epochs, height, width, channels = frames.shape
    pixels = height * width
    total = days.shape[0]
    far = [w_expand, w_reduce, w_gates, *w_qkvo]
    hbm = pl.BlockSpec(memory_space=pltpu.HBM)
    vmem = pl.BlockSpec(memory_space=pltpu.VMEM)
    out_shape = [
        jax.ShapeDtypeStruct((epochs, (height + 2) * width, channels), F32),
        jax.ShapeDtypeStruct((epochs * pixels, LANES), F32),
        jax.ShapeDtypeStruct((8, channels), F32),
        jax.ShapeDtypeStruct((8, w_gates.shape[1]), F32),
        jax.ShapeDtypeStruct((total, LANES), F32),
        jax.ShapeDtypeStruct((1, slope.size), F32),
        jax.ShapeDtypeStruct(w_expand.shape, BF16),
        jax.ShapeDtypeStruct(w_reduce.shape, BF16),
        jax.ShapeDtypeStruct((w_gates.shape[0], 4 * LANES), BF16),
        jax.ShapeDtypeStruct((channels, 3 * channels), BF16),
        jax.ShapeDtypeStruct((channels, channels), BF16),
    ]
    return pl.pallas_call(
        stage_kernel,
        name="stage",
        out_shape=out_shape,
        in_specs=[vmem] * len(near) + [hbm] * len(far),
        out_specs=[vmem] * len(out_shape),
        scratch_shapes=[
            pltpu.VMEM((channels // LANES, epochs, height, width + 16, LANES), F32),
            pltpu.SemaphoreType.DMA((len(far),)),
        ],
        compiler_params=pltpu.CompilerParams(vmem_limit_bytes=24 * 2**20),
        cost_estimate=pl.CostEstimate(
            flops=10**10, bytes_accessed=8 * w_expand.size, transcendentals=0
        ),
    )(*near, *[pltpu.with_memory_space_constraint(x, pltpu.HBM) for x in far])


def on_devices(turn, work):
    if turn is None:
        work()
    else:
        stage = lax.axis_index("epoch")
        pl.when((stage >= turn[0]) & (stage < turn[1]))(work)


def block_kernel(tiles, turn, count, sends, *refs):
    outs = refs[count:]
    if not sends:
        outs = (None, None) + outs
    on_devices(turn, lambda: block_work(tiles, *refs[:12], *outs))


def block_work(
    tiles,
    spread,
    recv_pair,
    recv_next,
    frames,
    mask,
    short_rows,
    long_rows,
    dw_kernel,
    w_expand,
    w_reduce,
    w_first,
    w_gates_hbm,
    send,
    pooled,
    decay0,
    inflow0,
    keep,
    block,
    open0,
    open1,
    taps,
    w_later,
    rim,
    edge,
    w_gates,
    sems,
):
    epochs, height, width, channels = frames.shape
    groups = channels // LANES
    rows = height + 2
    pixels = height * width
    wide = 4 * LANES

    early = keep.shape[1] // LANES
    places = [w_gates.at[j] for j in range(early - 1)] + [w_later.at[j] for j in range(groups - early)]
    gate_copies = [
        pltpu.make_async_copy(w_gates_hbm.at[:, pl.ds((j + 1) * wide, wide)], place, sems.at[j])
        for j, place in enumerate(places)
    ]
    for copy in gate_copies:
        copy.start()

    dw_bias = short_rows[0:1, :]
    norm_gain = short_rows[1:2, :]
    norm_shift = short_rows[2:3, :]
    half_scale = 0.5 * short_rows[3:4, :]
    b_expand = long_rows[0:1, :]

    me = lax.axis_index("tile")
    odd = lax.rem(me, 2)
    pair_row = (1 - odd) * REACH
    next_row = odd * REACH

    for c in range(groups):
        lanes = slice(c * LANES, (c + 1) * LANES)
        for e in range(epochs):
            rim[c, e, :, 0:8, :] = jnp.zeros((2 * REACH, 8, LANES), F32)
            rim[c, e, :, 8 + width : 16 + width, :] = jnp.zeros((2 * REACH, 8, LANES), F32)
            rim[c, e, pl.ds(pair_row, REACH), 8 : 8 + width, :] = recv_pair[e, :, :, lanes].astype(F32)
            rim[c, e, pl.ds(next_row, REACH), 8 : 8 + width, :] = recv_next[e, :, :, lanes].astype(F32)

    def depthwise(index, carry):
        c = index // epochs
        e = index - c * epochs
        lanes = pl.ds(pl.multiple_of(c * LANES, LANES), LANES)
        total = [None] * (2 * REACH)
        for ox in range(7):
            factors = [dw_kernel[oy, pl.ds(ox, 1), lanes] for oy in range(7)]
            for k in range(REACH):
                above = rim[c, e, k, pl.ds(5 + ox, width), :]
                below = rim[c, e, REACH + k, pl.ds(5 + ox, width), :]
                for y in range(k + 1):
                    term = above * factors[k - y]
                    total[y] = term if total[y] is None else total[y] + term
                for y in range(k, REACH):
                    term = below * factors[6 + k - y]
                    at = REACH + y
                    total[at] = term if total[at] is None else total[at] + term
        for y in range(2 * REACH):
            edge[e, pl.ds(y * width, width), lanes] = total[y]
        return carry

    lax.fori_loop(0, groups * epochs, depthwise, 0)

    count = rows * width
    rimmed = REACH * width
    column = lax.broadcasted_iota(jnp.int32, (count, LANES), 0)
    across = lax.rem(column, width)
    line = column // width
    first = jnp.where(me == 0, 1, 0)
    last = jnp.where(me == tiles - 1, rows - 2, rows - 1)
    inside = jnp.where((line >= first) & (line <= last), 1.0, 0.0)
    for e in range(epochs):
        values = (
            jnp.concatenate(
                [
                    spread[e, :rimmed] + edge[e, :rimmed],
                    spread[e, rimmed : count - rimmed],
                    spread[e, count - rimmed :] + edge[e, rimmed:],
                ],
                axis=0,
            )
            + dw_bias
        )
        center = jnp.mean(values, axis=-1, keepdims=True)
        centred = values - center
        variance = jnp.mean(centred * centred, axis=-1, keepdims=True)
        normed = (centred * lax.rsqrt(variance + 1e-06) * norm_gain + norm_shift).astype(BF16)
        grown = jnp.dot(normed, w_expand[...], preferred_element_type=F32) + b_expand
        reduced = jnp.dot(gelu_twice(grown.astype(BF16)), w_reduce[...], preferred_element_type=F32)
        for c in range(groups):
            lanes = slice(c * LANES, (c + 1) * LANES)
            centre = jnp.concatenate(
                [
                    rim[c, e, REACH - 1, 8 : 8 + width, :],
                    frames[e, :, :, lanes].astype(F32).reshape(pixels, LANES),
                    rim[c, e, REACH, 8 : 8 + width, :],
                ],
                axis=0,
            )
            feature = centre + half_scale[:, lanes] * reduced[:, lanes]
            feature = (feature * inside).astype(BF16).astype(F32)
            before = jnp.where(across == 0, 0.0, pltpu.roll(feature, 1, 0))
            after = jnp.where(across == width - 1, 0.0, pltpu.roll(feature, count - 1, 0))
            for ox, shifted in enumerate((before, feature, after)):
                packed = shifted.astype(BF16)
                for oy in range(3):
                    at = (oy * 3 + ox) * channels + c * LANES
                    taps[e * pixels : (e + 1) * pixels, at : at + LANES] = packed[
                        oy * width : oy * width + pixels
                    ]

    state = (decay0, inflow0, keep, block, open0, open1)
    for copy in gate_copies:
        copy.wait()
    cells_of(0, 0, taps, w_first, mask, short_rows, long_rows, send, pooled, state)
    for j in range(1, early):
        cells_of(j, j, taps, w_gates.at[j - 1], mask, short_rows, long_rows, send, pooled, state)


def gates_of(preact):
    quarter = LANES // 4
    lane = lax.broadcasted_iota(jnp.int32, (preact.shape[0], LANES), 1)
    spot = lane // quarter
    within = lane - spot * quarter
    sorted_ = []
    for i in range(4):
        gate = lax.rem(spot - i + 4, 4)
        sorted_.append(
            jnp.take_along_axis(preact[:, i * LANES : (i + 1) * LANES], 4 * within + gate, axis=1)
        )
    gates = []
    for g in range(4):
        out = sorted_[0]
        for i in range(1, 4):
            out = jnp.where(spot == (g + i) % 4, sorted_[i], out)
        gates.append(out if g == 0 else pltpu.roll(out, LANES - g * quarter, 1))
    return gates


def cells_of(j, at, taps, weights, mask, short_rows, long_rows, send, pooled, state):
    decay0, inflow0, keep, block, open0, open1 = state
    pixels = keep.shape[0]
    lanes = slice(at * LANES, (at + 1) * LANES)
    bias = long_rows[1:2, j * 4 * LANES : (j + 1) * 4 * LANES]
    rate = short_rows[4:5, j * LANES : (j + 1) * LANES]
    cell = None
    for e, opens in enumerate((open0, open1)):
        rows = slice(e * pixels, (e + 1) * pixels)
        preact = jnp.dot(taps[rows, :], weights[...], preferred_element_type=F32) + bias
        gate_in, gate_keep, gate_new, gate_out = gates_of(preact)
        good = mask[rows, :] > 0.5
        decay = jnp.where(good, jnp.exp(-rate * softplus(gate_keep)), 1.0)
        inflow = jnp.where(good, sigmoid(gate_in) * jnp.tanh(gate_new), 0.0)
        opened = sigmoid(gate_out)
        opens[:, lanes] = opened
        if e == 0:
            decay0[:, lanes] = decay
            inflow0[:, lanes] = inflow
            cell = inflow
        else:
            keep[:, lanes] = decay0[:, lanes] * decay
            cell = decay * inflow0[:, lanes] + inflow
            block[:, lanes] = cell
            if send is not None:
                send[:pixels, lanes] = cell.astype(BF16)
        if pooled is not None:
            pooled[e : e + 1, lanes] = pool(opened * jnp.tanh(cell))


def later_kernel(first, turn, count, sends, *refs):
    outs = refs[count:]
    if not sends:
        outs = (None,) + outs + (None,)
    on_devices(turn, lambda: later_work(first, *refs[:6], *outs))


def later_work(
    first,
    taps,
    w_gates,
    mask,
    short_rows,
    long_rows,
    pooled_early,
    send,
    decay0,
    inflow0,
    keep,
    block,
    open0,
    open1,
    pooled,
):
    channels = short_rows.shape[1]
    state = (decay0, inflow0, keep, block, open0, open1)
    for j in range(first, channels // LANES):
        at = j - first
        cells_of(j, at, taps, w_gates.at[at], mask, short_rows, long_rows, send, pooled, state)
    if send is None:
        return
    pixels = keep.shape[0]
    both = jnp.concatenate([pooled_early[0:2, :], pooled[0:2, :]], axis=1)
    own = tokens_of(both, short_rows[5:6, :])
    tail = (send.shape[0] - pixels) * LANES // channels
    known = jnp.zeros((tail, channels), F32)
    write_tail(send, pixels, put_tokens(known, own, 0))


def write_tail(send, pixels, tokens):
    tail, channels = tokens.shape
    for c in range(channels // LANES):
        at = pixels + c * tail
        send[at : at + tail, :] = tokens[:, c * LANES : (c + 1) * LANES].astype(BF16)


def read_tail(arrived, pixels, channels):
    tail = (arrived.shape[0] - pixels) * LANES // channels
    parts = [
        arrived[pixels + c * tail : pixels + (c + 1) * tail, :].astype(F32)
        for c in range(channels // LANES)
    ]
    return jnp.concatenate(parts, axis=1)


def run_block(tiles, early, turn, staged, recv_pair, recv_next, w_gates, kept, after):
    spread, mask, short_rows, long_rows, frames, dw_kernel, w_expand, w_reduce, w_first = staged
    epochs, height, width, channels = frames.shape
    pixels = height * width
    depth = w_gates.shape[0]
    vmem = pl.BlockSpec(memory_space=pltpu.VMEM)
    hbm = pl.BlockSpec(memory_space=pltpu.HBM)
    anywhere = pl.BlockSpec(memory_space=pl.ANY)
    near = early * LANES
    far = channels - near
    sends = not kept
    sent = [
        jax.ShapeDtypeStruct((pixels, near), BF16),
        jax.ShapeDtypeStruct((8, near), F32),
    ] * sends
    state = [jax.ShapeDtypeStruct((pixels, near), F32)] * 6
    flops = 2 * epochs * pixels * (2 * w_expand.size + w_gates.size)
    out = pl.pallas_call(
        functools.partial(block_kernel, tiles, turn, 12 + len(kept) + len(after), sends),
        name="block",
        out_shape=[
            *sent,
            *state,
            jax.ShapeDtypeStruct((epochs * pixels, depth), BF16),
            jax.ShapeDtypeStruct((far // LANES, depth, 4 * LANES), BF16),
        ],
        in_specs=[vmem] * 11 + [hbm] + [vmem] * len(kept) + [anywhere] * len(after),
        out_specs=[vmem] * (len(sent) + 8),
        input_output_aliases={12 + k: len(sent) + k for k in range(len(kept))},
        scratch_shapes=[
            pltpu.VMEM((channels // LANES, epochs, 2 * REACH, width + 16, LANES), F32),
            pltpu.VMEM((epochs, 2 * REACH * width, channels), F32),
            pltpu.VMEM((max(1, early - 1), depth, 4 * LANES), BF16),
            pltpu.SemaphoreType.DMA((channels // LANES - 1,)),
        ],
        compiler_params=pltpu.CompilerParams(vmem_limit_bytes=20 * 2**20),
        cost_estimate=pl.CostEstimate(flops=flops, bytes_accessed=2 * w_gates.size, transcendentals=0),
    )(
        spread,
        recv_pair,
        recv_next,
        frames,
        mask,
        short_rows,
        long_rows,
        dw_kernel,
        w_expand,
        w_reduce,
        w_first,
        pltpu.with_memory_space_constraint(w_gates, pltpu.HBM),
        *kept,
        *after,
    )
    return out[: len(sent)], out[len(sent) : -2], out[-2:]


def run_later(early, turn, staged, pooled, weighed, tail, kept, after):
    _, mask, short_rows, long_rows = staged[:4]
    taps, w_later = weighed
    pixels = taps.shape[0] // 2
    channels = short_rows.shape[1]
    far = channels - early * LANES
    vmem = pl.BlockSpec(memory_space=pltpu.VMEM)
    anywhere = pl.BlockSpec(memory_space=pl.ANY)
    sends = not kept
    sent = [jax.ShapeDtypeStruct((pixels + tail * channels // LANES, far), BF16)] * sends
    out = pl.pallas_call(
        functools.partial(later_kernel, early, turn, 6 + len(kept) + len(after), sends),
        name="later",
        out_shape=[*sent] + [jax.ShapeDtypeStruct((pixels, far), F32)] * 6,
        in_specs=[vmem] * 6 + [vmem] * len(kept) + [anywhere] * len(after),
        out_specs=[vmem] * (len(sent) + 6),
        input_output_aliases={6 + k: len(sent) + k for k in range(len(kept))},
        scratch_shapes=[pltpu.VMEM((8, far), F32)] * sends,
        compiler_params=pltpu.CompilerParams(vmem_limit_bytes=16 * 2**20),
        cost_estimate=pl.CostEstimate(flops=10**10, bytes_accessed=0, transcendentals=0),
    )(taps, w_later, mask, short_rows, long_rows, pooled, *kept, *after)
    return out[: len(sent)], out[len(sent) :]


def pool(memory):
    return jnp.mean(memory.astype(BF16).astype(F32), axis=0, keepdims=True)


def tokens_of(both, gain):
    center = jnp.mean(both, axis=-1, keepdims=True)
    centred = both - center
    variance = jnp.mean(centred * centred, axis=-1, keepdims=True)
    return (centred * lax.rsqrt(variance + 1e-06) * gain).astype(BF16).astype(F32)


def put_tokens(known, own, at):
    line = lax.broadcasted_iota(jnp.int32, known.shape, 0)
    return jnp.where(line == at, own[0:1], jnp.where(line == at + 1, own[1:2], known))


def step_cells(arrived, decay0, inflow0, keep, block):
    state = arrived[: keep.shape[0]].astype(F32)
    return decay0[...] * state + inflow0[...], keep[...] * state + block[...]


def relay_kernel(arrived, decay0, inflow0, keep, block, open0, open1, before, send, pooled):
    cell0, cell1 = step_cells(arrived, decay0, inflow0, keep, block)
    send[...] = cell1.astype(BF16)
    pooled[0:1, :] = pool(open0[...] * jnp.tanh(cell0))
    pooled[1:2, :] = pool(open1[...] * jnp.tanh(cell1))


def relay_later_kernel(
    stage, arrived, decay0, inflow0, keep, block, open0, open1, pooled_early, short_rows, send
):
    pixels = keep.shape[0]
    cell0, cell1 = step_cells(arrived, decay0, inflow0, keep, block)
    send[:pixels] = cell1.astype(BF16)
    pooled = jnp.concatenate(
        [pool(open0[...] * jnp.tanh(cell0)), pool(open1[...] * jnp.tanh(cell1))], axis=0
    )
    both = jnp.concatenate([pooled_early[0:2, :], pooled], axis=1)
    own = tokens_of(both, short_rows[5:6, :])
    known = read_tail(arrived, pixels, short_rows.shape[1])
    write_tail(send, pixels, put_tokens(known, own, 2 * stage))


def finish(arrived, state, memory):
    decay0, inflow0, keep, block, open0, open1 = state
    pixels = keep.shape[0]
    incoming = arrived[0][:pixels].astype(F32)
    for more in arrived[1:]:
        incoming = incoming + more[:pixels].astype(F32)
    cell0 = decay0[...] * incoming + inflow0[...]
    cell1 = keep[...] * incoming + block[...]
    pooled = []
    for e, (gate, cell) in enumerate(((open0, cell0), (open1, cell1))):
        out = (gate[...] * jnp.tanh(cell)).astype(BF16)
        memory[e] = out
        pooled.append(pool(out))
    return jnp.concatenate(pooled, axis=0)


def final_early_kernel(count, *refs):
    arrived, state = refs[:count], refs[count : count + 6]
    memory_hbm, pooled, head_of, channel_of, memory, sem = refs[count + 6 :]
    pooled[0:2, :] = finish(arrived, state, memory)
    copy = pltpu.make_async_copy(memory, memory_hbm.at[:, :, pl.ds(0, memory.shape[2])], sem)
    copy.start()
    channels, heads = head_of.shape
    depth = channels // heads
    member = lax.broadcasted_iota(jnp.int32, (channels, heads), 0) // depth
    head = lax.broadcasted_iota(jnp.int32, (channels, heads), 1)
    head_of[...] = jnp.where(member == head, 1.0, 0.0).astype(BF16)
    member = lax.broadcasted_iota(jnp.int32, (heads, channels), 1) // depth
    head = lax.broadcasted_iota(jnp.int32, (heads, channels), 0)
    channel_of[...] = jnp.where(member == head, 1.0, 0.0).astype(BF16)
    copy.wait()


def final_kernel(count, *refs):
    arrived, state = refs[:count], refs[count : count + 6]
    short_rows, months, slope, w_qkv, w_out, pooled_early, head_of, channel_of = refs[count + 6 : count + 14]
    memory_hbm, change, memory, sem = refs[count + 15 :]
    epochs, pixels, far = memory.shape
    channels = short_rows.shape[1]
    total = months.shape[0]
    pooled = finish(arrived, state, memory)
    copy = pltpu.make_async_copy(memory, memory_hbm.at[:, :, pl.ds(channels - far, far)], sem)
    copy.start()
    known = read_tail(arrived[0], pixels, channels)
    for more in arrived[1:]:
        known = known + read_tail(more, pixels, channels)
    both = jnp.concatenate([pooled_early[0:2, :], pooled], axis=1)
    own = tokens_of(both, short_rows[5:6, :])
    stage = lax.axis_index("epoch")
    tokens = put_tokens(known, own, 2 * stage).astype(BF16)
    heads = slope.shape[1]
    depth = channels // heads
    qkv = jnp.dot(tokens, w_qkv[...], preferred_element_type=F32).astype(BF16).astype(F32)[:total]
    queries = qkv[:, :channels]
    keys = qkv[:, channels : 2 * channels]
    values = qkv[:, 2 * channels :]
    def exact_dot(x, zero_one):
        high = x.astype(BF16)
        rest = x - high.astype(F32)
        low = rest.astype(BF16)
        least = (rest - low.astype(F32)).astype(BF16)
        out = jnp.dot(
            jnp.concatenate([high, low, least], axis=0), zero_one[...], preferred_element_type=F32
        )
        count = x.shape[0]
        return out[:count] + out[count : 2 * count] + out[2 * count :]

    line = lax.broadcasted_iota(jnp.int32, (total, channels), 0)
    key_index = lax.broadcasted_iota(jnp.int32, (total, heads), 0)
    month = months[:, :heads]
    places = [epochs * stage + step for step in range(epochs)]
    products = []
    for mine in places:
        query = jnp.sum(jnp.where(line == mine, queries, 0.0), axis=0, keepdims=True)
        products.append(query * keys)
    raw = exact_dot(jnp.concatenate(products, axis=0), head_of)
    weights = []
    for step, mine in enumerate(places):
        now = jnp.sum(jnp.where(key_index == mine, month, 0.0), axis=0, keepdims=True)
        scores = raw[step * total : (step + 1) * total] / math.sqrt(depth) - slope[...] * (now - month)
        scores = jnp.where(key_index <= mine, scores, -1e30)
        expo = jnp.exp(scores - jnp.max(scores, axis=0, keepdims=True))
        weights.append(expo / jnp.sum(expo, axis=0, keepdims=True))
    wide = exact_dot(jnp.concatenate(weights, axis=0), channel_of)
    results = [
        jnp.sum(wide[step * total : (step + 1) * total] * values, axis=0, keepdims=True)
        for step in range(epochs)
    ]
    mixed = jnp.concatenate(results, axis=0).astype(BF16)
    change[...] = jnp.dot(mixed, w_out[...], preferred_element_type=F32).astype(BF16)
    copy.wait()


def pairs(count, start):
    links = []
    for i in range(start, count - 1, 2):
        links += [(i, i + 1), (i + 1, i)]
    return links


def body(
    frames,
    valid,
    days,
    dw_kernel,
    dw_bias,
    norm_gain,
    norm_shift,
    w_expand,
    b_expand,
    w_reduce,
    layer_scale,
    w_gates,
    b_gates,
    forget_rate,
    attn_gain,
    w_query,
    w_key,
    w_value,
    w_out,
    head_slope,
):

    epochs, height, width, channels = frames.shape
    pixels = height * width
    tiles = lax.axis_size("tile")
    stages = lax.axis_size("epoch")
    total = epochs * stages
    tail = -(-total // 16) * 16
    gate_weights = w_gates.reshape(9 * channels, -1)
    near, to_pair, to_next = run_near(
        [
            frames,
            dw_kernel,
            valid,
            days,
            head_slope,
            b_expand,
            b_gates,
            dw_bias,
            norm_gain,
            norm_shift,
            layer_scale,
            forget_rate,
            attn_gain,
        ]
    )
    recv_pair = lax.ppermute(to_pair, "tile", pairs(tiles, 0))
    recv_next = lax.ppermute(to_next, "tile", pairs(tiles, 1))
    (
        spread,
        mask,
        short_rows,
        long_rows,
        months,
        slope,
        expand_near,
        reduce_near,
        w_first,
        qkv_near,
        out_near,
    ) = run_stage(near, w_expand, w_reduce, gate_weights, [w_query, w_key, w_value, w_out])
    early = max(1, channels // LANES - 1)
    staged = (spread, mask, short_rows, long_rows, near[0], near[1], expand_near, reduce_near, w_first)

    def blocks(turn, kept, after):
        return run_block(
            tiles, early, turn, staged, recv_pair, recv_next, gate_weights, kept, after
        )

    short_chain = 1 < stages <= 8
    first = (0, 1) if short_chain else None
    (send, pooled), state_near, weighed = blocks(first, [], [])
    (send_far,), state_far = run_later(early, first, staged, pooled, weighed, tail, [], [send])
    if short_chain:
        _, state_near, weighed = blocks((1, stages), state_near, [send_far])
        _, state_far = run_later(early, (1, 2), staged, pooled, weighed, tail, state_far, [])
    vmem = pl.BlockSpec(memory_space=pltpu.VMEM)
    params = pltpu.CompilerParams(vmem_limit_bytes=16 * 2**20)
    cost = pl.CostEstimate(flops=10**10, bytes_accessed=0, transcendentals=0)

    def relay(arrived, before):
        return pl.pallas_call(
            relay_kernel,
            name="relay",
            out_shape=[
                jax.ShapeDtypeStruct((pixels, early * LANES), BF16),
                jax.ShapeDtypeStruct((8, early * LANES), F32),
            ],
            in_specs=[vmem] * 7 + [pl.BlockSpec(memory_space=pl.ANY)],
            out_specs=[vmem] * 2,
            compiler_params=params,
            cost_estimate=cost,
        )(arrived, *state_near, before)

    def relay_later(stage, arrived, pooled, state_far):
        return pl.pallas_call(
            functools.partial(relay_later_kernel, stage),
            name="relay_later",
            out_shape=jax.ShapeDtypeStruct(send_far.shape, BF16),
            in_specs=[vmem] * 9,
            out_specs=vmem,
            compiler_params=params,
            cost_estimate=cost,
        )(arrived, *state_far, pooled, short_rows)

    arrived = []
    arrived_far = []
    if stages <= 8:
        for stage in range(stages - 1):
            link = [(stage, stage + 1)]
            if stage > 0:
                send, pooled = relay(arrived[-1], send_far)
                if stage == 1 and stages > 2:
                    _, state_far = run_later(
                        early, (2, stages), staged, pooled, weighed, tail, state_far, [send]
                    )
                send_far = relay_later(stage, arrived_far[-1], pooled, state_far)
            arrived.append(lax.ppermute(send, "epoch", link))
            arrived_far.append(lax.ppermute(send_far, "epoch", link))
    else:
        chain = [(i, i + 1) for i in range(stages - 1)]

        def along(state, width):
            keep, block = state[2], state[3]

            def turn(_, arriving):
                out = (keep * arriving.astype(F32) + block).astype(BF16)
                return lax.ppermute(out, "epoch", chain)

            return lax.fori_loop(0, stages - 1, turn, jnp.zeros((pixels, width), BF16))

        def unfold(tokens):
            parts = jnp.split(tokens, channels // LANES, axis=1)
            return jnp.concatenate(parts, axis=0)

        incoming = along(state_near, early * LANES)
        incoming_far = along(state_far, channels - early * LANES)
        _, pooled = relay(incoming, send_far)
        blank = jnp.zeros((tail * channels // LANES, LANES), BF16)
        told = relay_later(0, jnp.concatenate([incoming_far, blank]), pooled, state_far)[pixels:]
        told = jnp.concatenate(jnp.split(told, channels // LANES, axis=0), axis=1)
        known = lax.all_gather(told[:epochs], "epoch", axis=0, tiled=True)
        known = jnp.concatenate([known, jnp.zeros((tail - total, channels), BF16)])
        arrived.append(incoming)
        arrived_far.append(jnp.concatenate([incoming_far, unfold(known)]))

    hbm = pl.BlockSpec(memory_space=pltpu.HBM)
    heads = head_slope.size
    memory, pooled, head_of, channel_of = pl.pallas_call(
        functools.partial(final_early_kernel, len(arrived)),
        name="final_early",
        out_shape=[
            jax.ShapeDtypeStruct((epochs, pixels, channels), BF16),
            jax.ShapeDtypeStruct((8, early * LANES), F32),
            jax.ShapeDtypeStruct((channels, heads), BF16),
            jax.ShapeDtypeStruct((heads, channels), BF16),
        ],
        in_specs=[vmem] * (len(arrived) + 6),
        out_specs=[hbm] + [vmem] * 3,
        scratch_shapes=[
            pltpu.VMEM((epochs, pixels, early * LANES), BF16),
            pltpu.SemaphoreType.DMA,
        ],
        compiler_params=params,
        cost_estimate=cost,
    )(*arrived, *state_near)
    memory, change = pl.pallas_call(
        functools.partial(final_kernel, len(arrived)),
        name="final",
        out_shape=[
            jax.ShapeDtypeStruct((epochs, pixels, channels), BF16),
            jax.ShapeDtypeStruct((epochs, channels), BF16),
        ],
        in_specs=[vmem] * (len(arrived) + 14) + [hbm],
        out_specs=[hbm, vmem],
        input_output_aliases={len(arrived) + 14: 0},
        scratch_shapes=[
            pltpu.VMEM((epochs, pixels, channels - early * LANES), BF16),
            pltpu.SemaphoreType.DMA,
        ],
        compiler_params=pltpu.CompilerParams(vmem_limit_bytes=24 * 2**20),
    )(
        *arrived_far,
        *state_far,
        short_rows,
        months,
        slope,
        qkv_near,
        out_near,
        pooled,
        head_of,
        channel_of,
        pltpu.with_memory_space_constraint(memory, pltpu.HBM),
    )
    return (
        memory.reshape(epochs, height, width, channels),
        change.reshape(epochs, 1, 1, channels),
    )


def solution(mesh):
    placed = (
        P("epoch", ("groups", "tile"), None, None),
        P("epoch", ("groups", "tile"), None),
        P("groups"),
    ) + (P(),) * 17
    return jax.shard_map(
        body,
        mesh=mesh,
        in_specs=placed,
        out_specs=(
            P("epoch", ("groups", "tile"), None, None),
            P("epoch", ("groups", "tile"), None, None),
        ),
        check_vma=False,
    )
```

```python
import functools
import math

import jax
import jax.numpy as jnp
from jax import lax
from jax.experimental import pallas as pl
from jax.experimental.pallas import tpu as pltpu
from jax.sharding import PartitionSpec as P

PATCH = 16
REACH = 4
LANES = 128
F32 = jnp.float32
BF16 = jnp.bfloat16


def sigmoid(x):
    return 0.5 * jnp.tanh(0.5 * x) + 0.5


def softplus(x):
    return jnp.maximum(x, 0.0) + jnp.log(1.0 + jnp.exp(-jnp.abs(x)))


def gelu_twice(x):
    inner = x * (0.7978845608028654 + (0.7978845608028654 * 0.044715) * (x * x))
    return x + x * jnp.tanh(inner)


def near_kernel(*refs):
    count = len(refs) // 2 - 1
    sources, outs = refs[:count], refs[count : 2 * count]
    to_pair, to_next, sems = refs[2 * count :]
    copies = [pltpu.make_async_copy(a, b, sems.at[i]) for i, (a, b) in enumerate(zip(sources, outs))]
    for copy in copies:
        copy.start()
    copies[0].wait()
    frames = outs[0]
    bottom = frames.shape[1] - REACH
    odd = lax.rem(lax.axis_index("tile"), 2)
    to_pair[...] = frames[:, pl.ds((1 - odd) * bottom, REACH)]
    to_next[...] = frames[:, pl.ds(odd * bottom, REACH)]
    for copy in copies[1:]:
        copy.wait()


def run_near(arrays):
    frames = arrays[0]
    rim = jax.ShapeDtypeStruct((frames.shape[0], REACH) + frames.shape[2:], frames.dtype)
    hbm = pl.BlockSpec(memory_space=pltpu.HBM)
    vmem = pl.BlockSpec(memory_space=pltpu.VMEM)
    out = pl.pallas_call(
        near_kernel,
        name="near",
        out_shape=[jax.ShapeDtypeStruct(x.shape, x.dtype) for x in arrays] + [rim] * 2,
        in_specs=[hbm] * len(arrays),
        out_specs=[vmem] * (len(arrays) + 2),
        scratch_shapes=[pltpu.SemaphoreType.DMA((len(arrays),))],
        compiler_params=pltpu.CompilerParams(vmem_limit_bytes=16 * 2**20),
    )(*[pltpu.with_memory_space_constraint(x, pltpu.HBM) for x in arrays])
    return out[: len(arrays)], out[-2], out[-1]


def stage_kernel(
    frames,
    dw_kernel,
    valid,
    days,
    slope_line,
    b_expand,
    b_gates,
    dw_bias,
    norm_gain,
    norm_shift,
    layer_scale,
    forget_rate,
    attn_gain,
    w_expand_hbm,
    w_reduce_hbm,
    w_gates_hbm,
    w_query_hbm,
    w_key_hbm,
    w_value_hbm,
    w_out_hbm,
    spread,
    mask,
    short_rows,
    long_rows,
    months,
    slope,
    w_expand,
    w_reduce,
    w_first,
    w_qkv,
    w_out,
    padded,
    sems,
):
    epochs, height, width, channels = frames.shape
    groups = channels // LANES
    rows = height + 2
    pixels = height * width
    moves = [
        (w_expand_hbm, w_expand),
        (w_reduce_hbm, w_reduce),
        (w_gates_hbm.at[:, pl.ds(0, w_first.shape[1])], w_first),
        (w_query_hbm, w_qkv.at[:, pl.ds(0, channels)]),
        (w_key_hbm, w_qkv.at[:, pl.ds(channels, channels)]),
        (w_value_hbm, w_qkv.at[:, pl.ds(2 * channels, channels)]),
        (w_out_hbm, w_out),
    ]
    copies = [pltpu.make_async_copy(a, b, sems.at[i]) for i, (a, b) in enumerate(moves)]
    for copy in copies:
        copy.start()

    for c in range(groups):
        for e in range(epochs):
            lanes = slice(c * LANES, (c + 1) * LANES)
            padded[c, e, :, 0:8, :] = jnp.zeros((height, 8, LANES), F32)
            padded[c, e, :, 8 + width : 16 + width, :] = jnp.zeros((height, 8, LANES), F32)
            padded[c, e, :, 8 : 8 + width, :] = frames[e, :, :, lanes].astype(F32)

    half = rows // 2

    def depthwise(index, carry):
        c = index // epochs
        e = index - c * epochs
        lanes = pl.ds(pl.multiple_of(c * LANES, LANES), LANES)
        for part in range(2):
            total = [None] * half
            for ox in range(7):
                factors = [dw_kernel[oy, pl.ds(ox, 1), lanes] for oy in range(7)]
                for r in range(height):
                    at = [(y, r + REACH - (part * half + y)) for y in range(half)]
                    at = [(y, oy) for y, oy in at if 0 <= oy < 7]
                    if not at:
                        continue
                    window = padded[c, e, r, pl.ds(5 + ox, width), :]
                    for y, oy in at:
                        term = window * factors[oy]
                        total[y] = term if total[y] is None else total[y] + term
            for y in range(half):
                line = (part * half + y) * width
                spread[e, pl.ds(line, width), lanes] = total[y]
        return carry

    lax.fori_loop(0, groups * epochs, depthwise, 0)

    short = (dw_bias, norm_gain, norm_shift, layer_scale, forget_rate, attn_gain)
    for k, line in enumerate(short):
        short_rows[k : k + 1, :] = line[...].reshape(1, -1)
    for k, line in enumerate((b_expand, b_gates)):
        long_rows[k : k + 1, :] = line[...].reshape(1, -1)
    slope[...] = slope_line[...].reshape(1, -1)
    total = days.shape[0]
    eye = lax.broadcasted_iota(jnp.int32, (total, total), 0) == lax.broadcasted_iota(
        jnp.int32, (total, total), 1
    )
    month = days[...].astype(F32).reshape(1, -1) / 30.0
    months[...] = jnp.broadcast_to(
        jnp.sum(jnp.where(eye, month, 0.0), axis=1, keepdims=True), months.shape
    )
    down = lax.broadcasted_iota(jnp.int32, (pixels, height), 0) // width
    pick = jnp.where(down == lax.broadcasted_iota(jnp.int32, (pixels, height), 1), 1.0, 0.0).astype(BF16)
    side = lax.rem(lax.broadcasted_iota(jnp.int32, (pixels, width), 0), width)
    place = side == lax.broadcasted_iota(jnp.int32, (pixels, width), 1)
    ones = jnp.ones((width, LANES), BF16)
    for e in range(epochs):
        plane = jnp.where(valid[e] > 0, 1.0, 0.0).astype(BF16)
        lines = jnp.dot(pick, plane, preferred_element_type=F32)
        mask[e * pixels : (e + 1) * pixels, :] = jnp.dot(
            jnp.where(place, lines, 0.0).astype(BF16), ones, preferred_element_type=F32
        )
    for copy in copies:
        copy.wait()


def run_stage(near, w_expand, w_reduce, w_gates, w_qkvo):
    frames, dw_kernel, valid, days, slope = near[:5]
    epochs, height, width, channels = frames.shape
    pixels = height * width
    total = days.shape[0]
    far = [w_expand, w_reduce, w_gates, *w_qkvo]
    hbm = pl.BlockSpec(memory_space=pltpu.HBM)
    vmem = pl.BlockSpec(memory_space=pltpu.VMEM)
    out_shape = [
        jax.ShapeDtypeStruct((epochs, (height + 2) * width, channels), F32),
        jax.ShapeDtypeStruct((epochs * pixels, LANES), F32),
        jax.ShapeDtypeStruct((8, channels), F32),
        jax.ShapeDtypeStruct((8, w_gates.shape[1]), F32),
        jax.ShapeDtypeStruct((total, LANES), F32),
        jax.ShapeDtypeStruct((1, slope.size), F32),
        jax.ShapeDtypeStruct(w_expand.shape, BF16),
        jax.ShapeDtypeStruct(w_reduce.shape, BF16),
        jax.ShapeDtypeStruct((w_gates.shape[0], 4 * LANES), BF16),
        jax.ShapeDtypeStruct((channels, 3 * channels), BF16),
        jax.ShapeDtypeStruct((channels, channels), BF16),
    ]
    return pl.pallas_call(
        stage_kernel,
        name="stage",
        out_shape=out_shape,
        in_specs=[vmem] * len(near) + [hbm] * len(far),
        out_specs=[vmem] * len(out_shape),
        scratch_shapes=[
            pltpu.VMEM((channels // LANES, epochs, height, width + 16, LANES), F32),
            pltpu.SemaphoreType.DMA((len(far),)),
        ],
        compiler_params=pltpu.CompilerParams(vmem_limit_bytes=24 * 2**20),
        cost_estimate=pl.CostEstimate(
            flops=10**10, bytes_accessed=8 * w_expand.size, transcendentals=0
        ),
    )(*near, *[pltpu.with_memory_space_constraint(x, pltpu.HBM) for x in far])


def on_devices(turn, work):
    if turn is None:
        work()
    else:
        stage = lax.axis_index("epoch")
        pl.when((stage >= turn[0]) & (stage < turn[1]))(work)


def block_kernel(tiles, turn, count, sends, *refs):
    outs = refs[count:]
    if not sends:
        outs = (None, None) + outs
    on_devices(turn, lambda: block_work(tiles, *refs[:12], *outs))


def block_work(
    tiles,
    spread,
    recv_pair,
    recv_next,
    frames,
    mask,
    short_rows,
    long_rows,
    dw_kernel,
    w_expand,
    w_reduce,
    w_first,
    w_gates_hbm,
    send,
    pooled,
    decay0,
    inflow0,
    keep,
    block,
    open0,
    open1,
    taps,
    w_later,
    rim,
    edge,
    w_gates,
    sems,
):
    epochs, height, width, channels = frames.shape
    groups = channels // LANES
    rows = height + 2
    pixels = height * width
    wide = 4 * LANES

    early = keep.shape[1] // LANES
    places = [w_gates.at[j] for j in range(early - 1)] + [w_later.at[j] for j in range(groups - early)]
    gate_copies = [
        pltpu.make_async_copy(w_gates_hbm.at[:, pl.ds((j + 1) * wide, wide)], place, sems.at[j])
        for j, place in enumerate(places)
    ]
    for copy in gate_copies:
        copy.start()

    dw_bias = short_rows[0:1, :]
    norm_gain = short_rows[1:2, :]
    norm_shift = short_rows[2:3, :]
    half_scale = 0.5 * short_rows[3:4, :]
    b_expand = long_rows[0:1, :]

    me = lax.axis_index("tile")
    odd = lax.rem(me, 2)
    pair_row = (1 - odd) * REACH
    next_row = odd * REACH

    for c in range(groups):
        lanes = slice(c * LANES, (c + 1) * LANES)
        for e in range(epochs):
            rim[c, e, :, 0:8, :] = jnp.zeros((2 * REACH, 8, LANES), F32)
            rim[c, e, :, 8 + width : 16 + width, :] = jnp.zeros((2 * REACH, 8, LANES), F32)
            rim[c, e, pl.ds(pair_row, REACH), 8 : 8 + width, :] = recv_pair[e, :, :, lanes].astype(F32)
            rim[c, e, pl.ds(next_row, REACH), 8 : 8 + width, :] = recv_next[e, :, :, lanes].astype(F32)

    def depthwise(index, carry):
        c = index // epochs
        e = index - c * epochs
        lanes = pl.ds(pl.multiple_of(c * LANES, LANES), LANES)
        total = [None] * (2 * REACH)
        for ox in range(7):
            factors = [dw_kernel[oy, pl.ds(ox, 1), lanes] for oy in range(7)]
            for k in range(REACH):
                above = rim[c, e, k, pl.ds(5 + ox, width), :]
                below = rim[c, e, REACH + k, pl.ds(5 + ox, width), :]
                for y in range(k + 1):
                    term = above * factors[k - y]
                    total[y] = term if total[y] is None else total[y] + term
                for y in range(k, REACH):
                    term = below * factors[6 + k - y]
                    at = REACH + y
                    total[at] = term if total[at] is None else total[at] + term
        for y in range(2 * REACH):
            edge[e, pl.ds(y * width, width), lanes] = total[y]
        return carry

    lax.fori_loop(0, groups * epochs, depthwise, 0)

    count = rows * width
    rimmed = REACH * width
    column = lax.broadcasted_iota(jnp.int32, (count, LANES), 0)
    across = lax.rem(column, width)
    line = column // width
    first = jnp.where(me == 0, 1, 0)
    last = jnp.where(me == tiles - 1, rows - 2, rows - 1)
    inside = jnp.where((line >= first) & (line <= last), 1.0, 0.0)
    for e in range(epochs):
        values = (
            jnp.concatenate(
                [
                    spread[e, :rimmed] + edge[e, :rimmed],
                    spread[e, rimmed : count - rimmed],
                    spread[e, count - rimmed :] + edge[e, rimmed:],
                ],
                axis=0,
            )
            + dw_bias
        )
        center = jnp.mean(values, axis=-1, keepdims=True)
        centred = values - center
        variance = jnp.mean(centred * centred, axis=-1, keepdims=True)
        normed = (centred * lax.rsqrt(variance + 1e-06) * norm_gain + norm_shift).astype(BF16)
        grown = jnp.dot(normed, w_expand[...], preferred_element_type=F32) + b_expand
        reduced = jnp.dot(gelu_twice(grown.astype(BF16)), w_reduce[...], preferred_element_type=F32)
        for c in range(groups):
            lanes = slice(c * LANES, (c + 1) * LANES)
            centre = jnp.concatenate(
                [
                    rim[c, e, REACH - 1, 8 : 8 + width, :],
                    frames[e, :, :, lanes].astype(F32).reshape(pixels, LANES),
                    rim[c, e, REACH, 8 : 8 + width, :],
                ],
                axis=0,
            )
            feature = centre + half_scale[:, lanes] * reduced[:, lanes]
            feature = (feature * inside).astype(BF16).astype(F32)
            before = jnp.where(across == 0, 0.0, pltpu.roll(feature, 1, 0))
            after = jnp.where(across == width - 1, 0.0, pltpu.roll(feature, count - 1, 0))
            for ox, shifted in enumerate((before, feature, after)):
                packed = shifted.astype(BF16)
                for oy in range(3):
                    at = (oy * 3 + ox) * channels + c * LANES
                    taps[e * pixels : (e + 1) * pixels, at : at + LANES] = packed[
                        oy * width : oy * width + pixels
                    ]

    state = (decay0, inflow0, keep, block, open0, open1)
    for copy in gate_copies:
        copy.wait()
    cells_of(0, 0, taps, w_first, mask, short_rows, long_rows, send, pooled, state)
    for j in range(1, early):
        cells_of(j, j, taps, w_gates.at[j - 1], mask, short_rows, long_rows, send, pooled, state)


def gates_of(preact):
    quarter = LANES // 4
    lane = lax.broadcasted_iota(jnp.int32, (preact.shape[0], LANES), 1)
    spot = lane // quarter
    within = lane - spot * quarter
    sorted_ = []
    for i in range(4):
        gate = lax.rem(spot - i + 4, 4)
        sorted_.append(
            jnp.take_along_axis(preact[:, i * LANES : (i + 1) * LANES], 4 * within + gate, axis=1)
        )
    gates = []
    for g in range(4):
        out = sorted_[0]
        for i in range(1, 4):
            out = jnp.where(spot == (g + i) % 4, sorted_[i], out)
        gates.append(out if g == 0 else pltpu.roll(out, LANES - g * quarter, 1))
    return gates


def cells_of(j, at, taps, weights, mask, short_rows, long_rows, send, pooled, state):
    decay0, inflow0, keep, block, open0, open1 = state
    pixels = keep.shape[0]
    lanes = slice(at * LANES, (at + 1) * LANES)
    bias = long_rows[1:2, j * 4 * LANES : (j + 1) * 4 * LANES]
    rate = short_rows[4:5, j * LANES : (j + 1) * LANES]
    cell = None
    for e, opens in enumerate((open0, open1)):
        rows = slice(e * pixels, (e + 1) * pixels)
        pieces = []
        for part in range(2):
            at_rows = slice(e * pixels + part * pixels // 2, e * pixels + (part + 1) * pixels // 2)
            preact = jnp.dot(taps[at_rows, :], weights[...], preferred_element_type=F32) + bias
            pieces.append(gates_of(preact))
        gate_in, gate_keep, gate_new, gate_out = [
            jnp.concatenate(both, axis=0) for both in zip(*pieces)
        ]
        good = mask[rows, :] > 0.5
        decay = jnp.where(good, jnp.exp(-rate * softplus(gate_keep)), 1.0)
        inflow = jnp.where(good, sigmoid(gate_in) * jnp.tanh(gate_new), 0.0)
        opened = sigmoid(gate_out)
        opens[:, lanes] = opened
        if e == 0:
            decay0[:, lanes] = decay
            inflow0[:, lanes] = inflow
            cell = inflow
        else:
            keep[:, lanes] = decay0[:, lanes] * decay
            cell = decay * inflow0[:, lanes] + inflow
            block[:, lanes] = cell
            if send is not None:
                send[:pixels, lanes] = cell.astype(BF16)
        if pooled is not None:
            pooled[e : e + 1, lanes] = pool(opened * jnp.tanh(cell))


def later_kernel(first, turn, count, sends, *refs):
    outs = refs[count:]
    if not sends:
        outs = (None,) + outs + (None,)
    on_devices(turn, lambda: later_work(first, *refs[:6], *outs))


def later_work(
    first,
    taps,
    w_gates,
    mask,
    short_rows,
    long_rows,
    pooled_early,
    send,
    decay0,
    inflow0,
    keep,
    block,
    open0,
    open1,
    pooled,
):
    channels = short_rows.shape[1]
    state = (decay0, inflow0, keep, block, open0, open1)
    for j in range(first, channels // LANES):
        at = j - first
        cells_of(j, at, taps, w_gates.at[at], mask, short_rows, long_rows, send, pooled, state)
    if send is None:
        return
    pixels = keep.shape[0]
    both = jnp.concatenate([pooled_early[0:2, :], pooled[0:2, :]], axis=1)
    own = tokens_of(both, short_rows[5:6, :])
    tail = (send.shape[0] - pixels) * LANES // channels
    known = jnp.zeros((tail, channels), F32)
    write_tail(send, pixels, put_tokens(known, own, 0))


def write_tail(send, pixels, tokens):
    tail, channels = tokens.shape
    for c in range(channels // LANES):
        at = pixels + c * tail
        send[at : at + tail, :] = tokens[:, c * LANES : (c + 1) * LANES].astype(BF16)


def read_tail(arrived, pixels, channels):
    tail = (arrived.shape[0] - pixels) * LANES // channels
    parts = [
        arrived[pixels + c * tail : pixels + (c + 1) * tail, :].astype(F32)
        for c in range(channels // LANES)
    ]
    return jnp.concatenate(parts, axis=1)


def run_block(tiles, early, turn, staged, recv_pair, recv_next, w_gates, kept, after):
    spread, mask, short_rows, long_rows, frames, dw_kernel, w_expand, w_reduce, w_first = staged
    epochs, height, width, channels = frames.shape
    pixels = height * width
    depth = w_gates.shape[0]
    vmem = pl.BlockSpec(memory_space=pltpu.VMEM)
    hbm = pl.BlockSpec(memory_space=pltpu.HBM)
    anywhere = pl.BlockSpec(memory_space=pl.ANY)
    near = early * LANES
    far = channels - near
    sends = not kept
    sent = [
        jax.ShapeDtypeStruct((pixels, near), BF16),
        jax.ShapeDtypeStruct((8, near), F32),
    ] * sends
    state = [jax.ShapeDtypeStruct((pixels, near), F32)] * 6
    flops = 2 * epochs * pixels * (2 * w_expand.size + w_gates.size)
    out = pl.pallas_call(
        functools.partial(block_kernel, tiles, turn, 12 + len(kept) + len(after), sends),
        name="block",
        out_shape=[
            *sent,
            *state,
            jax.ShapeDtypeStruct((epochs * pixels, depth), BF16),
            jax.ShapeDtypeStruct((far // LANES, depth, 4 * LANES), BF16),
        ],
        in_specs=[vmem] * 11 + [hbm] + [vmem] * len(kept) + [anywhere] * len(after),
        out_specs=[vmem] * (len(sent) + 8),
        input_output_aliases={12 + k: len(sent) + k for k in range(len(kept))},
        scratch_shapes=[
            pltpu.VMEM((channels // LANES, epochs, 2 * REACH, width + 16, LANES), F32),
            pltpu.VMEM((epochs, 2 * REACH * width, channels), F32),
            pltpu.VMEM((max(1, early - 1), depth, 4 * LANES), BF16),
            pltpu.SemaphoreType.DMA((channels // LANES - 1,)),
        ],
        compiler_params=pltpu.CompilerParams(vmem_limit_bytes=20 * 2**20),
        cost_estimate=pl.CostEstimate(flops=flops, bytes_accessed=2 * w_gates.size, transcendentals=0),
    )(
        spread,
        recv_pair,
        recv_next,
        frames,
        mask,
        short_rows,
        long_rows,
        dw_kernel,
        w_expand,
        w_reduce,
        w_first,
        pltpu.with_memory_space_constraint(w_gates, pltpu.HBM),
        *kept,
        *after,
    )
    return out[: len(sent)], out[len(sent) : -2], out[-2:]


def run_later(early, turn, staged, pooled, weighed, tail, kept, after):
    _, mask, short_rows, long_rows = staged[:4]
    taps, w_later = weighed
    pixels = taps.shape[0] // 2
    channels = short_rows.shape[1]
    far = channels - early * LANES
    vmem = pl.BlockSpec(memory_space=pltpu.VMEM)
    anywhere = pl.BlockSpec(memory_space=pl.ANY)
    sends = not kept
    sent = [jax.ShapeDtypeStruct((pixels + tail * channels // LANES, far), BF16)] * sends
    out = pl.pallas_call(
        functools.partial(later_kernel, early, turn, 6 + len(kept) + len(after), sends),
        name="later",
        out_shape=[*sent] + [jax.ShapeDtypeStruct((pixels, far), F32)] * 6,
        in_specs=[vmem] * 6 + [vmem] * len(kept) + [anywhere] * len(after),
        out_specs=[vmem] * (len(sent) + 6),
        input_output_aliases={6 + k: len(sent) + k for k in range(len(kept))},
        scratch_shapes=[pltpu.VMEM((8, far), F32)] * sends,
        compiler_params=pltpu.CompilerParams(vmem_limit_bytes=16 * 2**20),
        cost_estimate=pl.CostEstimate(flops=10**10, bytes_accessed=0, transcendentals=0),
    )(taps, w_later, mask, short_rows, long_rows, pooled, *kept, *after)
    return out[: len(sent)], out[len(sent) :]


def pool(memory):
    return jnp.mean(memory.astype(BF16).astype(F32), axis=0, keepdims=True)


def tokens_of(both, gain):
    center = jnp.mean(both, axis=-1, keepdims=True)
    centred = both - center
    variance = jnp.mean(centred * centred, axis=-1, keepdims=True)
    return (centred * lax.rsqrt(variance + 1e-06) * gain).astype(BF16).astype(F32)


def put_tokens(known, own, at):
    line = lax.broadcasted_iota(jnp.int32, known.shape, 0)
    return jnp.where(line == at, own[0:1], jnp.where(line == at + 1, own[1:2], known))


def step_cells(arrived, decay0, inflow0, keep, block):
    state = arrived[: keep.shape[0]].astype(F32)
    return decay0[...] * state + inflow0[...], keep[...] * state + block[...]


def relay_kernel(arrived, decay0, inflow0, keep, block, open0, open1, before, send, pooled):
    cell0, cell1 = step_cells(arrived, decay0, inflow0, keep, block)
    send[...] = cell1.astype(BF16)
    pooled[0:1, :] = pool(open0[...] * jnp.tanh(cell0))
    pooled[1:2, :] = pool(open1[...] * jnp.tanh(cell1))


def relay_later_kernel(
    stage, arrived, decay0, inflow0, keep, block, open0, open1, pooled_early, short_rows, send
):
    pixels = keep.shape[0]
    cell0, cell1 = step_cells(arrived, decay0, inflow0, keep, block)
    send[:pixels] = cell1.astype(BF16)
    pooled = jnp.concatenate(
        [pool(open0[...] * jnp.tanh(cell0)), pool(open1[...] * jnp.tanh(cell1))], axis=0
    )
    both = jnp.concatenate([pooled_early[0:2, :], pooled], axis=1)
    own = tokens_of(both, short_rows[5:6, :])
    known = read_tail(arrived, pixels, short_rows.shape[1])
    write_tail(send, pixels, put_tokens(known, own, 2 * stage))


def finish(arrived, state, memory):
    decay0, inflow0, keep, block, open0, open1 = state
    pixels = keep.shape[0]
    incoming = arrived[0][:pixels].astype(F32)
    for more in arrived[1:]:
        incoming = incoming + more[:pixels].astype(F32)
    cell0 = decay0[...] * incoming + inflow0[...]
    cell1 = keep[...] * incoming + block[...]
    pooled = []
    for e, (gate, cell) in enumerate(((open0, cell0), (open1, cell1))):
        out = (gate[...] * jnp.tanh(cell)).astype(BF16)
        memory[e] = out
        pooled.append(pool(out))
    return jnp.concatenate(pooled, axis=0)


def final_early_kernel(count, *refs):
    arrived, state = refs[:count], refs[count : count + 6]
    memory_hbm, pooled, head_of, channel_of, memory, sem = refs[count + 6 :]
    pooled[0:2, :] = finish(arrived, state, memory)
    copy = pltpu.make_async_copy(memory, memory_hbm.at[:, :, pl.ds(0, memory.shape[2])], sem)
    copy.start()
    channels, heads = head_of.shape
    depth = channels // heads
    member = lax.broadcasted_iota(jnp.int32, (channels, heads), 0) // depth
    head = lax.broadcasted_iota(jnp.int32, (channels, heads), 1)
    head_of[...] = jnp.where(member == head, 1.0, 0.0).astype(BF16)
    member = lax.broadcasted_iota(jnp.int32, (heads, channels), 1) // depth
    head = lax.broadcasted_iota(jnp.int32, (heads, channels), 0)
    channel_of[...] = jnp.where(member == head, 1.0, 0.0).astype(BF16)
    copy.wait()


def final_kernel(count, *refs):
    arrived, state = refs[:count], refs[count : count + 6]
    short_rows, months, slope, w_qkv, w_out, pooled_early, head_of, channel_of = refs[count + 6 : count + 14]
    memory_hbm, change, memory, sem = refs[count + 15 :]
    epochs, pixels, far = memory.shape
    channels = short_rows.shape[1]
    total = months.shape[0]
    pooled = finish(arrived, state, memory)
    copy = pltpu.make_async_copy(memory, memory_hbm.at[:, :, pl.ds(channels - far, far)], sem)
    copy.start()
    known = read_tail(arrived[0], pixels, channels)
    for more in arrived[1:]:
        known = known + read_tail(more, pixels, channels)
    both = jnp.concatenate([pooled_early[0:2, :], pooled], axis=1)
    own = tokens_of(both, short_rows[5:6, :])
    stage = lax.axis_index("epoch")
    tokens = put_tokens(known, own, 2 * stage).astype(BF16)
    heads = slope.shape[1]
    depth = channels // heads
    qkv = jnp.dot(tokens, w_qkv[...], preferred_element_type=F32).astype(BF16).astype(F32)[:total]
    queries = qkv[:, :channels]
    keys = qkv[:, channels : 2 * channels]
    values = qkv[:, 2 * channels :]
    def exact_dot(x, zero_one):
        high = x.astype(BF16)
        rest = x - high.astype(F32)
        low = rest.astype(BF16)
        least = (rest - low.astype(F32)).astype(BF16)
        out = jnp.dot(
            jnp.concatenate([high, low, least], axis=0), zero_one[...], preferred_element_type=F32
        )
        count = x.shape[0]
        return out[:count] + out[count : 2 * count] + out[2 * count :]

    line = lax.broadcasted_iota(jnp.int32, (total, channels), 0)
    key_index = lax.broadcasted_iota(jnp.int32, (total, heads), 0)
    month = months[:, :heads]
    places = [epochs * stage + step for step in range(epochs)]
    products = []
    for mine in places:
        query = jnp.sum(jnp.where(line == mine, queries, 0.0), axis=0, keepdims=True)
        products.append(query * keys)
    raw = exact_dot(jnp.concatenate(products, axis=0), head_of)
    weights = []
    for step, mine in enumerate(places):
        now = jnp.sum(jnp.where(key_index == mine, month, 0.0), axis=0, keepdims=True)
        scores = raw[step * total : (step + 1) * total] / math.sqrt(depth) - slope[...] * (now - month)
        scores = jnp.where(key_index <= mine, scores, -1e30)
        expo = jnp.exp(scores - jnp.max(scores, axis=0, keepdims=True))
        weights.append(expo / jnp.sum(expo, axis=0, keepdims=True))
    wide = exact_dot(jnp.concatenate(weights, axis=0), channel_of)
    results = [
        jnp.sum(wide[step * total : (step + 1) * total] * values, axis=0, keepdims=True)
        for step in range(epochs)
    ]
    mixed = jnp.concatenate(results, axis=0).astype(BF16)
    change[...] = jnp.dot(mixed, w_out[...], preferred_element_type=F32).astype(BF16)
    copy.wait()


def pairs(count, start):
    links = []
    for i in range(start, count - 1, 2):
        links += [(i, i + 1), (i + 1, i)]
    return links


def body(
    frames,
    valid,
    days,
    dw_kernel,
    dw_bias,
    norm_gain,
    norm_shift,
    w_expand,
    b_expand,
    w_reduce,
    layer_scale,
    w_gates,
    b_gates,
    forget_rate,
    attn_gain,
    w_query,
    w_key,
    w_value,
    w_out,
    head_slope,
):

    epochs, height, width, channels = frames.shape
    pixels = height * width
    tiles = lax.axis_size("tile")
    stages = lax.axis_size("epoch")
    total = epochs * stages
    tail = -(-total // 16) * 16
    gate_weights = w_gates.reshape(9 * channels, -1)
    near, to_pair, to_next = run_near(
        [
            frames,
            dw_kernel,
            valid,
            days,
            head_slope,
            b_expand,
            b_gates,
            dw_bias,
            norm_gain,
            norm_shift,
            layer_scale,
            forget_rate,
            attn_gain,
        ]
    )
    recv_pair = lax.ppermute(to_pair, "tile", pairs(tiles, 0))
    recv_next = lax.ppermute(to_next, "tile", pairs(tiles, 1))
    (
        spread,
        mask,
        short_rows,
        long_rows,
        months,
        slope,
        expand_near,
        reduce_near,
        w_first,
        qkv_near,
        out_near,
    ) = run_stage(near, w_expand, w_reduce, gate_weights, [w_query, w_key, w_value, w_out])
    early = max(1, channels // LANES - 1)
    staged = (spread, mask, short_rows, long_rows, near[0], near[1], expand_near, reduce_near, w_first)

    def blocks(turn, kept, after):
        return run_block(
            tiles, early, turn, staged, recv_pair, recv_next, gate_weights, kept, after
        )

    short_chain = 1 < stages <= 8
    first = (0, 1) if short_chain else None
    (send, pooled), state_near, weighed = blocks(first, [], [])
    (send_far,), state_far = run_later(early, first, staged, pooled, weighed, tail, [], [send])
    if short_chain:
        _, state_near, weighed = blocks((1, stages), state_near, [send_far])
        _, state_far = run_later(early, (1, 2), staged, pooled, weighed, tail, state_far, [])
    vmem = pl.BlockSpec(memory_space=pltpu.VMEM)
    params = pltpu.CompilerParams(vmem_limit_bytes=16 * 2**20)
    cost = pl.CostEstimate(flops=10**10, bytes_accessed=0, transcendentals=0)

    def relay(arrived, before):
        return pl.pallas_call(
            relay_kernel,
            name="relay",
            out_shape=[
                jax.ShapeDtypeStruct((pixels, early * LANES), BF16),
                jax.ShapeDtypeStruct((8, early * LANES), F32),
            ],
            in_specs=[vmem] * 7 + [pl.BlockSpec(memory_space=pl.ANY)],
            out_specs=[vmem] * 2,
            compiler_params=params,
            cost_estimate=cost,
        )(arrived, *state_near, before)

    def relay_later(stage, arrived, pooled, state_far):
        return pl.pallas_call(
            functools.partial(relay_later_kernel, stage),
            name="relay_later",
            out_shape=jax.ShapeDtypeStruct(send_far.shape, BF16),
            in_specs=[vmem] * 9,
            out_specs=vmem,
            compiler_params=params,
            cost_estimate=cost,
        )(arrived, *state_far, pooled, short_rows)

    arrived = []
    arrived_far = []
    if stages <= 8:
        for stage in range(stages - 1):
            link = [(stage, stage + 1)]
            if stage > 0:
                send, pooled = relay(arrived[-1], send_far)
                if stage == 1 and stages > 2:
                    _, state_far = run_later(
                        early, (2, stages), staged, pooled, weighed, tail, state_far, [send]
                    )
                send_far = relay_later(stage, arrived_far[-1], pooled, state_far)
            arrived.append(lax.ppermute(send, "epoch", link))
            arrived_far.append(lax.ppermute(send_far, "epoch", link))
    else:
        chain = [(i, i + 1) for i in range(stages - 1)]

        def along(state, width):
            keep, block = state[2], state[3]

            def turn(_, arriving):
                out = (keep * arriving.astype(F32) + block).astype(BF16)
                return lax.ppermute(out, "epoch", chain)

            return lax.fori_loop(0, stages - 1, turn, jnp.zeros((pixels, width), BF16))

        def unfold(tokens):
            parts = jnp.split(tokens, channels // LANES, axis=1)
            return jnp.concatenate(parts, axis=0)

        incoming = along(state_near, early * LANES)
        incoming_far = along(state_far, channels - early * LANES)
        _, pooled = relay(incoming, send_far)
        blank = jnp.zeros((tail * channels // LANES, LANES), BF16)
        told = relay_later(0, jnp.concatenate([incoming_far, blank]), pooled, state_far)[pixels:]
        told = jnp.concatenate(jnp.split(told, channels // LANES, axis=0), axis=1)
        known = lax.all_gather(told[:epochs], "epoch", axis=0, tiled=True)
        known = jnp.concatenate([known, jnp.zeros((tail - total, channels), BF16)])
        arrived.append(incoming)
        arrived_far.append(jnp.concatenate([incoming_far, unfold(known)]))

    hbm = pl.BlockSpec(memory_space=pltpu.HBM)
    heads = head_slope.size
    memory, pooled, head_of, channel_of = pl.pallas_call(
        functools.partial(final_early_kernel, len(arrived)),
        name="final_early",
        out_shape=[
            jax.ShapeDtypeStruct((epochs, pixels, channels), BF16),
            jax.ShapeDtypeStruct((8, early * LANES), F32),
            jax.ShapeDtypeStruct((channels, heads), BF16),
            jax.ShapeDtypeStruct((heads, channels), BF16),
        ],
        in_specs=[vmem] * (len(arrived) + 6),
        out_specs=[hbm] + [vmem] * 3,
        scratch_shapes=[
            pltpu.VMEM((epochs, pixels, early * LANES), BF16),
            pltpu.SemaphoreType.DMA,
        ],
        compiler_params=params,
        cost_estimate=cost,
    )(*arrived, *state_near)
    memory, change = pl.pallas_call(
        functools.partial(final_kernel, len(arrived)),
        name="final",
        out_shape=[
            jax.ShapeDtypeStruct((epochs, pixels, channels), BF16),
            jax.ShapeDtypeStruct((epochs, channels), BF16),
        ],
        in_specs=[vmem] * (len(arrived) + 14) + [hbm],
        out_specs=[hbm, vmem],
        input_output_aliases={len(arrived) + 14: 0},
        scratch_shapes=[
            pltpu.VMEM((epochs, pixels, channels - early * LANES), BF16),
            pltpu.SemaphoreType.DMA,
        ],
        compiler_params=pltpu.CompilerParams(vmem_limit_bytes=24 * 2**20),
    )(
        *arrived_far,
        *state_far,
        short_rows,
        months,
        slope,
        qkv_near,
        out_near,
        pooled,
        head_of,
        channel_of,
        pltpu.with_memory_space_constraint(memory, pltpu.HBM),
    )
    return (
        memory.reshape(epochs, height, width, channels),
        change.reshape(epochs, 1, 1, channels),
    )


def solution(mesh):
    placed = (
        P("epoch", ("groups", "tile"), None, None),
        P("epoch", ("groups", "tile"), None),
        P("groups"),
    ) + (P(),) * 17
    return jax.shard_map(
        body,
        mesh=mesh,
        in_specs=placed,
        out_specs=(
            P("epoch", ("groups", "tile"), None, None),
            P("epoch", ("groups", "tile"), None, None),
        ),
        check_vma=False,
    )
```
